32 devices in a mesh: img: 4 (over x, core), blk: 8 (over z, y).
Axes of the slice: x: 2, y: 2, z: 4, core: 2. Of those that a mesh axis runs over, the one named last changes fastest.
Arguments:
- pixels: bfloat16 [16, 10240, 261], P('img', 'blk'), may hold values from -6 to 6
- counts: int32 [16], P('img'), may hold values from 3160 to 10240, as said below
- latents: bfloat16 [16, 512, 1024], P('img', 'blk'), may hold values from -6 to 6
- cotangent: float32 [16, 512, 1024], P('img', 'blk'), may hold values from -6 to 6
- w_query: bfloat16 [1024, 1024], replicated, may hold values from -0.375 to 0.375
- w_key: bfloat16 [261, 1024], replicated, may hold values from -0.375 to 0.375
- w_value: bfloat16 [261, 1024], replicated, may hold values from -0.375 to 0.375
- w_out: bfloat16 [1024, 1024], replicated, may hold values from -4.5 to 4.5
- w_hidden: bfloat16 [1024, 1024], replicated, may hold values from -0.1875 to 0.1875
- w_back: bfloat16 [1024, 1024], replicated, may hold values from -0.1875 to 0.1875
- gain_query: float32 [1024], replicated, may hold values from 0.1 to 1.9
- gain_pixel: float32 [261], replicated, may hold values from 0.1 to 1.9
- gain_mlp: float32 [1024], replicated, may hold values from 0.1 to 1.9
Outputs:
- updated: float32 [16, 512, 1024], P('img', 'blk')
- grad_latents: float32 [16, 512, 1024], P('img', 'blk')
- grad_pixels: float32 [16, 10240, 261], P('img', 'blk')
- grad_w_query: float32 [1024, 1024], replicated
- grad_w_key: float32 [261, 1024], replicated
- grad_w_value: float32 [261, 1024], replicated
- grad_w_out: float32 [1024, 1024], replicated
- grad_w_hidden: float32 [1024, 1024], replicated
- grad_w_back: float32 [1024, 1024], replicated
- grad_gain_query: float32 [1024], replicated
- grad_gain_pixel: float32 [261], replicated
- grad_gain_mlp: float32 [1024], replicated
The draws below stay inside these ranges and needn't reach their ends.
Inputs may be any that keep to these rules, and one draw needn't show every extreme that they name: `counts`: each image's count is 10240 * s * s // 81 with s one of 5, 7 and 9; of the 4 images that share an index of img (consecutive images), one has s = 9.
All inputs are finite; a program needn't handle non-finite values.
Results may differ from the reference program's by a relative error of at most 0.013.
The reference program's roundings to bfloat16 on the way count: a program that leaves them out, or rounds other values in their place, can miss the bound.
Values may be sent and summed in bfloat16 or wider, within the bound.
A program may use at most 192 MiB of HBM per device.

```python
import math
import jax
import jax.numpy as jnp
from jax import lax

D = 1024
FEAT = 261
LAT = 512
MICRO = 4
PIX = 10240
IMAGES = 16


def draw_counts(key, part):
    key = jax.random.fold_in(key, 11)
    side_key, full_key = jax.random.split(key)
    sides = 5 + 2 * jax.random.randint(side_key, (IMAGES,), 0, 3, dtype=jnp.int32)
    full_slot = jax.random.randint(full_key, (IMAGES // MICRO,), 0, MICRO, dtype=jnp.int32)
    image_index = jnp.arange(IMAGES, dtype=jnp.int32)
    is_full = image_index % MICRO == full_slot[image_index // MICRO]
    sides = jnp.where(is_full, 9, sides)
    return (PIX * sides * sides // 81).astype(jnp.int32)


def levels(key, dims, cuts, smallest, top_value):
    level = 1.0
    for position, shards_of in cuts:
        heights = jax.random.uniform(jax.random.fold_in(jax.random.fold_in(key, 6), position), (shards_of,), jnp.float32, smallest / len(cuts), top_value / len(cuts))
        level = level * jnp.repeat(jnp.exp(heights), dims[position] // shards_of).reshape((-1,) + (1,) * (len(dims) - 1 - position))
    return level


def noise(rng, extent, width, reach, cuts=(), held_as=jnp.bfloat16):
    drawn = jax.random.normal(rng, extent, jnp.float32) * width
    if len(cuts) > 0:
        drawn = levels(rng, extent, cuts, -0.22, 0.18) * drawn
    return jnp.clip(drawn, min=-reach, max=reach).astype(held_as)


def setup_inputs(seed: int = 0) -> dict:
    keys = jax.random.split(jax.random.key(seed), 14)
    pixels = noise(keys[0], (IMAGES, PIX, FEAT), 1.0, 6.0, ((0, 4), (1, 8)))
    counts = draw_counts(jax.random.fold_in(keys[13], 71), 0)
    latents = noise(keys[2], (IMAGES, LAT, D), 1.0, 6.0, ((0, 4), (1, 8)))
    cotangent = noise(keys[3], (IMAGES, LAT, D), 1.0, 6.0, ((0, 4), (1, 8)), jnp.float32)
    w_query = noise(keys[4], (D, D), (D // 4) ** -0.5, 0.375)
    w_key = noise(keys[5], (FEAT, D), FEAT ** -0.5, 0.375)
    w_value = noise(keys[6], (FEAT, D), FEAT ** -0.5, 0.375)
    w_out = noise(keys[7], (D, D), 0.75, 4.5)
    w_hidden = noise(keys[8], (D, D), D ** -0.5, 0.1875)
    w_back = noise(keys[9], (D, D), D ** -0.5, 0.1875)
    gain_query = jnp.clip(1.0 + 0.18 * jax.random.normal(keys[10], (D,), jnp.float32), 0.1, 1.9)
    gain_pixel = jnp.clip(1.0 + 0.18 * jax.random.normal(keys[11], (FEAT,), jnp.float32), 0.1, 1.9)
    gain_mlp = jnp.clip(1.0 + 0.18 * jax.random.normal(keys[12], (D,), jnp.float32), 0.1, 1.9)
    return {"pixels": pixels, "counts": counts, "latents": latents, "cotangent": cotangent, "w_query": w_query, "w_key": w_key, "w_value": w_value, "w_out": w_out, "w_hidden": w_hidden, "w_back": w_back, "gain_query": gain_query, "gain_pixel": gain_pixel, "gain_mlp": gain_mlp}


EPSILON = 1e-05
MASKED = -1e+30

@jax.custom_vjp
def low(v):
    return lax.optimization_barrier(v.astype(jnp.bfloat16)).astype(jnp.float32)

@jax.custom_vjp
def low_back(v):
    return v

def low_keep(v):
    return (low(v), None)

def low_pass(kept, grad):
    return (grad,)

def back_keep(v):
    return (v, None)

def back_low(kept, grad):
    return (low(grad),)
low.defvjp(low_keep, low_pass)
low_back.defvjp(back_keep, back_low)

def layer_norm(values, gain_vec):
    centered = values - lax.optimization_barrier(jnp.mean(values, axis=-1, keepdims=True))
    variance = lax.optimization_barrier(jnp.mean(centered * centered, axis=-1, keepdims=True))
    return centered * lax.rsqrt(variance + EPSILON) * gain_vec

def matmul(left_mat, right_mat):
    return jnp.dot(left_mat, right_mat, precision=lax.Precision.HIGHEST)

def one_image(params, latent_rows, pixel_rows, pixel_count):
    w_query, w_key, w_value, w_out, w_hidden, w_back, gain_query, gain_pixel, gain_mlp = params
    scaling = 1.0 / math.sqrt(latent_rows.shape[-1])
    normed_q = low(layer_norm(latent_rows, gain_query))
    queries = low(low_back(matmul(normed_q, w_query)))
    normed_p = low(layer_norm(pixel_rows, gain_pixel))
    key_rows = low(low_back(matmul(normed_p, w_key)))
    value_rows = low(low_back(matmul(normed_p, w_value)))
    scores = low_back(matmul(queries, key_rows.T) * scaling)
    positions = jnp.arange(pixel_rows.shape[0], dtype=jnp.int32)
    scores = jnp.where((positions < pixel_count)[None, :], scores, MASKED)
    soft_probs = jax.nn.softmax(scores, axis=-1)
    attended = low(low_back(matmul(low(soft_probs), value_rows)))
    branch_out = low_back(matmul(attended, w_out))
    hidden_in = latent_rows + branch_out
    normed_m = low(layer_norm(hidden_in, gain_mlp))
    pre_act = low_back(matmul(normed_m, w_hidden))
    activated = low(jax.nn.gelu(pre_act, approximate=False))
    return hidden_in + low_back(matmul(activated, w_back))

def reference(pixels, counts, latents, cotangent, w_query, w_key, w_value, w_out, w_hidden, w_back, gain_query, gain_pixel, gain_mlp):
    params = (w_query.astype(jnp.float32), w_key.astype(jnp.float32), w_value.astype(jnp.float32), w_out.astype(jnp.float32), w_hidden.astype(jnp.float32), w_back.astype(jnp.float32), gain_query.astype(jnp.float32), gain_pixel.astype(jnp.float32), gain_mlp.astype(jnp.float32))
    stepper = jax.checkpoint(one_image)

    def forward(weight_set, latent_set, pixel_set):

        def per_image(entry):
            return stepper(weight_set, entry[0], entry[1], entry[2])
        return lax.map(per_image, (latent_set, pixel_set, counts))
    updated, pullback = jax.vjp(forward, params, latents.astype(jnp.float32), pixels.astype(jnp.float32))
    grad_params, grad_latents, grad_pixels = pullback(cotangent.astype(jnp.float32))
    return (updated, grad_latents, grad_pixels, grad_params[0], grad_params[1], grad_params[2], grad_params[3], grad_params[4], grad_params[5], grad_params[6], grad_params[7], grad_params[8])
```

```python
import math

import jax
import jax.numpy as jnp
from jax import lax
from jax.sharding import PartitionSpec as P

EPSILON = 1e-05
MASKED = -1e30


def layer_norm(values, gain_vec):
    centered = values - jnp.mean(values, axis=-1, keepdims=True)
    variance = jnp.mean(centered * centered, axis=-1, keepdims=True)
    return centered * lax.rsqrt(variance + EPSILON) * gain_vec


def gelu_exact(values):
    return jax.nn.gelu(values, approximate=False)


def low(values):
    return values.astype(jnp.bfloat16)


def product(left_mat, right_mat):
    return jnp.dot(left_mat, right_mat, preferred_element_type=jnp.float32)


def product_tn(left_mat, right_mat):
    return lax.dot_general(
        left_mat, right_mat, (((0,), (0,)), ((), ())), preferred_element_type=jnp.float32
    )


def product_nt(left_mat, right_mat):
    return lax.dot_general(
        left_mat, right_mat, (((1,), (1,)), ((), ())), preferred_element_type=jnp.float32
    )


def each(spec, left, right):
    return jnp.einsum(spec, left, right, preferred_element_type=jnp.float32)


def to_owner(x, peers):
    micro, rows = x.shape[:2]
    blocks = jnp.moveaxis(x.reshape(micro, peers, rows // peers, *x.shape[2:]), 1, 0)
    return lax.all_to_all(blocks, "blk", 0, 0, tiled=True)


def body(pixels, counts, latents, cotangent, w_query, w_key, w_value, w_out, w_hidden, w_back, gain_query, gain_pixel, gain_mlp):
    micro, pixel_rows, features = pixels.shape
    lat_rows, width = latents.shape[1:]
    peers = lax.axis_size("blk")
    scaling = 1.0 / math.sqrt(width)
    rows = micro * lat_rows
    positions = lax.axis_index("blk") * pixel_rows + jnp.arange(pixel_rows, dtype=jnp.int32)
    valid = positions[None, :] < counts[:, None]

    latent_in = latents.reshape(rows, width).astype(jnp.float32)
    normed_qf, query_pull = jax.vjp(layer_norm, latent_in, gain_query)
    normed_q = low(normed_qf)
    queries = low(product(normed_q, w_query))
    query_feats = low(product_nt(queries, w_key) * scaling).reshape(micro, lat_rows, features)
    all_query = lax.all_gather(query_feats, "blk", axis=1, tiled=True)
    normed_pf, pixel_pull = jax.vjp(layer_norm, pixels.astype(jnp.float32), gain_pixel)
    normed_p = low(normed_pf)
    scores = each("mqf,mpf->mqp", all_query, normed_p)
    scores = jnp.where(valid[:, None, :], scores, MASKED)
    highest = jnp.max(scores, axis=2)
    unscaled = jnp.exp(scores - highest[..., None])
    total = jnp.sum(unscaled, axis=2)
    sums = low(each("mqp,mpf->mqf", low(unscaled), normed_p))
    parts = to_owner(sums, peers).astype(jnp.float32)
    stats = to_owner(jnp.stack([highest, total], axis=2), peers)
    top = jnp.max(stats[..., 0], axis=0)
    scale = jnp.exp(stats[..., 0] - top)
    denom = jnp.sum(stats[..., 1] * scale, axis=0)
    lse = top + jnp.log(denom)
    seen = (jnp.sum(parts * scale[..., None], axis=0) / denom[..., None]).reshape(rows, features)
    seen_b = low(seen)
    attended_b = low(product(seen_b, w_value))
    hidden_in = latent_in + product(attended_b, w_out)
    normed_mf, mlp_pull = jax.vjp(layer_norm, hidden_in, gain_mlp)
    normed_m = low(normed_mf)
    pre_act = product(normed_m, w_hidden)
    activated_f, gelu_pull = jax.vjp(gelu_exact, pre_act)
    activated = low(activated_f)
    updated = hidden_in + product(activated, w_back)
    cot = cotangent.reshape(rows, width)
    cot_b = low(cot)
    grad_back = product_tn(activated, cot_b)
    (grad_pre,) = gelu_pull(product_nt(cot_b, w_back))
    grad_pre_b = low(grad_pre)
    grad_hidden = product_tn(normed_m, grad_pre_b)
    grad_h_ln, grad_gm = mlp_pull(product_nt(grad_pre_b, w_hidden))
    grad_h = cot + grad_h_ln
    grad_h_b = low(grad_h)
    grad_att = low(product_nt(grad_h_b, w_out))
    grad_seen = product_nt(grad_att, w_value)
    dots = jnp.sum(grad_seen * seen, axis=1).reshape(micro, lat_rows)
    value_side = product_tn(seen_b, grad_h_b)
    all_grad = lax.all_gather(low(grad_seen).reshape(micro, lat_rows, features), "blk", axis=1, tiled=True)
    all_stat = lax.all_gather(jnp.stack([lse, dots], axis=2), "blk", axis=1, tiled=True)
    probs = unscaled * jnp.exp(highest - all_stat[..., 0])[..., None]
    grad_probs = each("mqf,mpf->mqp", all_grad, normed_p)
    grad_scores = low(probs * (grad_probs - all_stat[..., 1][..., None]))
    back_sums = low(each("mqp,mpf->mqf", grad_scores, normed_p))
    grad_np = each("mqp,mqf->mpf", low(probs), all_grad) + each("mqp,mqf->mpf", grad_scores, all_query)
    grad_pixels, grad_gp = pixel_pull(grad_np)
    back_feats = jnp.sum(to_owner(back_sums, peers).astype(jnp.float32), axis=0).reshape(rows, features)
    back_b = low(back_feats)
    grad_q = low(product(back_b, w_key) * scaling)
    grad_lat_q, grad_gq = query_pull(product_nt(grad_q, w_query))
    grad_latents = grad_h + grad_lat_q
    query_side = product_tn(normed_q, back_b)
    query_side, value_side, grad_hidden, grad_back, grad_gq, grad_gp, grad_gm = lax.psum(
        (query_side, value_side, grad_hidden, grad_back, grad_gq, grad_gp, grad_gm), ("img", "blk")
    )
    query_b, value_b = low(query_side * scaling), low(value_side)
    return (
        updated.reshape(micro, lat_rows, width),
        grad_latents.reshape(micro, lat_rows, width),
        grad_pixels,
        product(query_b, w_key),
        product_tn(query_b, w_query),
        product_nt(value_b, w_out),
        product_tn(w_value, value_b),
        grad_hidden,
        grad_back,
        grad_gq,
        grad_gp,
        grad_gm,
    )


def solution(mesh):
    spread, same = P("img", "blk", None), P()
    return jax.shard_map(
        body,
        mesh=mesh,
        in_specs=(spread, P("img"), spread, spread) + (same,) * 9,
        out_specs=(spread,) * 3 + (same,) * 9,
        check_vma=False,
    )
```

```python
import functools
import math

import jax
import jax.numpy as jnp
from jax import lax
from jax.experimental import pallas as pl
from jax.experimental.pallas import tpu as pltpu
from jax.sharding import PartitionSpec as P

EPSILON = 1e-05
MASKED = -1e30
LANES = 128
MESH = pl.DeviceIdType.MESH
bf16, f32 = jnp.bfloat16, jnp.float32


def dot(left, right, left_dim, right_dim):
    return lax.dot_general(left, right, (((left_dim,), (right_dim,)), ((), ())), preferred_element_type=f32)


def lanes_of(shape):
    return lax.broadcasted_iota(jnp.int32, shape, 1)


def rows_of(shape):
    return lax.broadcasted_iota(jnp.int32, shape, 0)


def normed(values):
    part = 1.0 / values.shape[1]
    centered = values - jnp.sum(values, axis=1, keepdims=True) * part
    spread = lax.rsqrt(jnp.sum(centered * centered, axis=1, keepdims=True) * part + EPSILON)
    return centered * spread, spread


def normed_back(grad, unit, spread):
    part = 1.0 / grad.shape[1]
    first = jnp.sum(grad, axis=1, keepdims=True) * part
    second = jnp.sum(grad * unit, axis=1, keepdims=True) * part
    return spread * (grad - first - unit * second)


def split_low(values):
    high = values.astype(bf16).astype(f32)
    return high, (values - high).astype(bf16).astype(f32)


class Links:
    def __init__(self, send_sem, recv_sem):
        self.send_sem, self.recv_sem, self.used, self.sent = send_sem, recv_sem, 0, []

    def remote(self, src, dst, device):
        k = self.used
        self.used += 1
        return pltpu.make_async_remote_copy(
            src_ref=src, dst_ref=dst, send_sem=self.send_sem.at[k], recv_sem=self.recv_sem.at[k],
            device_id=device, device_id_type=MESH,
        )

    def start(self, copy):
        copy.start()
        self.sent.append(copy)

    def drain(self):
        for copy in self.sent:
            copy.wait_send()
        self.sent = []


class Place:
    def __init__(self, depth):
        img, blk = lax.axis_index("img"), lax.axis_index("blk")
        self.x, self.c = lax.div(img, 2), lax.rem(img, 2)
        self.z, self.y = lax.div(blk, 2), lax.rem(blk, 2)
        self.core_peer = (self.x * 2 + 1 - self.c, blk)
        self.x_peer = ((1 - self.x) * 2 + self.c, blk)
        self.y_peer = (img, self.z * 2 + 1 - self.y)
        self.z_index = [lax.rem(self.z + k, depth) for k in range(1, depth)]
        self.z_peers = [(img, other * 2 + self.y) for other in self.z_index]

    def all(self):
        return [self.core_peer, self.x_peer, self.y_peer] + self.z_peers


class Gather:
    def __init__(self, links, place, at):
        own = at(place.y, place.z)
        self.links = links
        self.along = [links.remote(own, at(place.y, place.z), peer) for peer in place.z_peers]
        self.across = links.remote(at(place.y, None), at(place.y, None), place.y_peer)

    def begin(self):
        for copy in self.along:
            self.links.start(copy)

    def forward(self):
        for copy in self.along:
            copy.wait_recv()
        self.links.start(self.across)

    def end(self):
        self.across.wait_recv()


class Total:
    def __init__(self, links, place, src, recv, out, local_sem, lanes):
        height = src.shape[0]
        self.links, self.src, self.recv, self.out = links, src, recv, out
        peers = (place.core_peer, place.x_peer, place.y_peer)
        coords = (place.c, place.x, place.y)
        self.halves, self.backs, offset = [], [], 0
        self.spans = []
        for peer, coord, held in zip(peers, coords, recv[:3]):
            height //= 2
            there = pl.multiple_of(offset + (1 - coord) * height, height)
            offset = pl.multiple_of(offset + coord * height, height)
            self.spans.append((offset, height))
            self.halves.append(links.remote(src.at[pl.ds(there, height)], held, peer))
        depth = len(place.z_peers) + 1
        height //= depth
        self.piece = pl.multiple_of(offset + place.z * height, height)
        self.height = height
        self.quarters = []
        for k, (peer, index) in enumerate(zip(place.z_peers, place.z_index)):
            there = pl.multiple_of(offset + index * height, height)
            self.quarters.append(links.remote(src.at[pl.ds(there, height)], recv[3].at[k], peer))
        mine = src.at[pl.ds(self.piece, height)]
        self.shown = [links.remote(mine, out.at[pl.ds(self.piece, height), lanes], peer) for peer in place.z_peers]
        self.kept = pltpu.make_async_copy(mine, out.at[pl.ds(self.piece, height), lanes], local_sem)
        for (start, size), peer in zip(reversed(self.spans), reversed(peers)):
            region = out.at[pl.ds(start, size), lanes]
            self.backs.append(links.remote(region, region, peer))

    def send(self, stage):
        if stage < 3:
            self.links.start(self.halves[stage])
        else:
            for copy in self.quarters:
                self.links.start(copy)

    def add(self, stage):
        if stage < 3:
            self.halves[stage].wait_recv()
            start, size = self.spans[stage]
            step = min(size, 64)

            def some(k):
                here = pl.ds(pl.multiple_of(start + k * step, step), step)
                there = pl.ds(pl.multiple_of(k * step, step), step)
                held = self.recv[stage][there, :].astype(f32)
                self.src[here, :] = (self.src[here, :].astype(f32) + held).astype(bf16)

            pl.loop(0, size // step)(some)
        else:
            for copy in self.quarters:
                copy.wait_recv()
            here = pl.ds(self.piece, self.height)
            total = self.src[here, :].astype(f32)
            for k in range(len(self.quarters)):
                total = total + self.recv[3][k].astype(f32)
            self.src[here, :] = total.astype(bf16)

    def turn(self):
        self.kept.start()
        for copy in self.shown:
            self.links.start(copy)

    def back(self, stage):
        if stage == 0:
            for copy in self.shown:
                copy.wait_recv()
            self.kept.wait()
        else:
            self.backs[stage - 1].wait_recv()
        if stage < 3:
            self.links.start(self.backs[stage])

    def rs(self, stage):
        self.add(stage)
        if stage < 3:
            self.send(stage + 1)
        else:
            self.turn()


def kernel(
    dims,
    counts, pixels, latents, cotangent, w_query, w_out, w_hidden, w_back, w_key, w_value, gain_query, gain_pixel, gain_mlp,
    updated, grad_latents, grad_pixels, sum_back, sum_hidden, sum_value, sum_late,
    px, np_all, npt_all, scores, probs, grad_s, x_in, cot_in, wq, wo, wh, wb, wk, wv,
    q_all, qx_all, g_all, gx_all,
    ob, oe, orecv, oerecv, zb, zx, zrecv, zxrecv,
    bb, be, brecv, berecv, yb, yx, yrecv, yxrecv,
    tops, seen, lse, nq, nm, act, gpre, grad_h, gh_low, up_out, px_out, gains, gp_acc,
    back_src, hidden_src, value_src, late_src, recvs, send_sem, recv_sem, load_sem, store_sem, kept_sem,
):
    micro, rows, depth, px_rows, feat, main, wide, width = dims
    ext = wide - LANES
    line = depth * rows
    everyone = 2 * line
    scaling = 1.0 / math.sqrt(width)
    links, place = Links(send_sem, recv_sem), Place(depth)
    loads = {}

    def load(name, src, dst):
        loads[name] = pltpu.make_async_copy(src, dst, load_sem.at[len(loads)])
        return loads[name]

    load("x", latents, x_in).start()
    load("wq", w_query, wq).start()
    load("wk", w_key, wk).start()
    load("px0", pixels.at[0], px.at[0]).start()
    load("px1", pixels.at[1], px.at[1]).start()
    for name, src, dst in (("wv", w_value, wv), ("wo", w_out, wo), ("wh", w_hidden, wh), ("wb", w_back, wb), ("cot", cotangent, cot_in)):
        load(name, src, dst).start()
    barrier = pltpu.get_barrier_semaphore()
    for peer in place.all():
        pl.semaphore_signal(barrier, inc=1, device_id=peer, device_id_type=MESH)
    gains[...] = jnp.zeros_like(gains)
    gp_acc[...] = jnp.zeros_like(gp_acc)

    loads["x"].wait()
    loads["wq"].wait()
    loads["wk"].wait()
    unit_q, _ = normed(x_in[...].reshape(micro * rows, width).astype(f32))
    nq[...] = (unit_q * gain_query[...]).astype(bf16)
    queries = dot(nq[...], wq[...], 1, 0).astype(bf16)
    feats = dot(queries, wk[...], 1, 1) * scaling
    small = jnp.where(lanes_of((rows, LANES)) % 16 == 6, 1.0, 0.0)
    for i in range(micro):
        here = slice(i * rows, (i + 1) * rows)
        q_all[i, place.y, place.z] = feats[here, :main].astype(bf16)
        tail = feats[here, main:]
        small = small + (tail if i == 0 else pltpu.roll(tail, 16 * i, 1))
    qx_all[place.y, place.z] = small.astype(bf16)
    pl.semaphore_wait(barrier, len(place.all()))

    def part(ref):
        return lambda y, z: ref.at[y] if z is None else ref.at[y, z]

    q_ext = Gather(links, place, part(qx_all))
    q_main = [Gather(links, place, part(q_all.at[i])) for i in range(micro)]
    q_ext.begin()
    for gather in q_main:
        gather.begin()

    first_pixel = lax.axis_index("blk") * px_rows

    def pixel_norm(i):
        loads[f"px{i}"].wait()
        unit, _ = normed(px[i % 2].astype(f32))
        value = unit * gain_pixel[:, :feat]
        value = jnp.concatenate([value, jnp.zeros((px_rows, wide - feat), f32)], axis=1)
        lane = lanes_of((px_rows, LANES)) + main
        tail = jnp.where((lane == main + 5) | (lane == main + 7), 1.0, value[:, main:])
        full = jnp.concatenate([value[:, :main], tail], axis=1)
        npt_all[i] = full.T[: main + 16].astype(bf16)
        np_all[i, :, :main] = value[:, :main].astype(bf16)
        masked = first_pixel + rows_of((px_rows, LANES)) >= counts[i]
        np_all[i, :, main:] = jnp.where((lane == main + 6) & masked, MASKED, tail).astype(bf16)
        if i + 2 < micro:
            load(f"px{i + 2}", pixels.at[i + 2], px.at[i % 2]).start()

    def with_ext(block, small_all, i):
        small = small_all[...].reshape(everyone, LANES).astype(f32)
        if i:
            small = pltpu.roll(small, LANES - 16 * i, 1)
        return block, small

    def query_block(i):
        small = qx_all[...].reshape(everyone, LANES).astype(f32)
        if i:
            small = pltpu.roll(small, LANES - 16 * i, 1)
        small = jnp.where(lanes_of((everyone, LANES)) < 16, small, 0.0)
        return jnp.concatenate([q_all[i].reshape(everyone, main), small.astype(bf16)], axis=1)

    def attend(i):
        q_main[i].end()
        scores[...] = dot(np_all[i], query_block(i), 1, 1)
        top = jnp.max(scores[...], axis=0, keepdims=True)
        tops[i] = jnp.broadcast_to(top, (8, everyone))
        probs[i] = jnp.exp(scores[...] - top).astype(bf16)
        sums = dot(npt_all[i], probs[i], 1, 0)
        small = jnp.where(rows_of((8, everyone)) == 6, top, sums[main : main + 8])
        for y in range(2):
            here = slice(y * line, (y + 1) * line)
            ob[i, y] = sums[:main, here].astype(bf16)
            oe[i, y] = small[:, here]

    def exchange(i, sums, ext_sums, held, ext_held):
        copies = [
            links.remote(sums.at[i, 1 - place.y], held.at[i], place.y_peer),
            links.remote(ext_sums.at[i, 1 - place.y], ext_held.at[i], place.y_peer),
        ]
        for copy in copies:
            links.start(copy)
        return copies

    def to_owners(src, dst):
        copies = [
            links.remote(src.at[other], dst.at[k], peer)
            for k, (peer, other) in enumerate(zip(place.z_peers, place.z_index))
        ]
        for copy in copies:
            links.start(copy)
        return copies

    def spread_small(parts, block):
        tall = jnp.concatenate(parts + [jnp.zeros((LANES - 8 * micro, line), f32)], axis=0)
        block[...] = tall.T.reshape(depth, rows, LANES)

    small_parts = []

    def merge(i, copies):
        for copy in copies:
            copy.wait_recv()
        mine, theirs = oe[i, place.y], oerecv[i]
        top_m, top_t = mine[6:7], theirs[6:7]
        top = jnp.maximum(top_m, top_t)
        scale_m, scale_t = jnp.exp(top_m - top), jnp.exp(top_t - top)
        total = ob[i, place.y].astype(f32) * scale_m + orecv[i].astype(f32) * scale_t
        zb[i] = total.T.astype(bf16).reshape(depth, rows, main)
        small = mine * scale_m + theirs * scale_t
        small_parts.append(jnp.where(rows_of((8, line)) == 6, top, small))
        return to_owners(zb.at[i], zrecv.at[i])

    q_swaps, q_merged = {}, {}
    pixel_norm(0)
    pixel_norm(1)
    q_ext.forward()
    q_main[0].forward()
    pixel_norm(2)
    q_main[1].forward()
    pixel_norm(3)
    q_main[2].forward()
    q_ext.end()
    for i in range(micro):
        attend(i)
        q_swaps[i] = exchange(i, ob, oe, orecv, oerecv)
        if i + 3 < micro:
            q_main[i + 3].forward()
        if i >= 1:
            q_merged[i - 1] = merge(i - 1, q_swaps[i - 1])
    q_merged[micro - 1] = merge(micro - 1, q_swaps[micro - 1])
    spread_small(small_parts, zx)
    arrivals = to_owners(zx, zxrecv)
    for i in range(micro):
        arrivals = arrivals + q_merged[i]
    for copy in arrivals:
        copy.wait_recv()

    lane = lanes_of((rows, LANES))
    for i in range(micro):
        mains = [zb[i, place.z]] + [zrecv[i, k] for k in range(depth - 1)]
        smalls = [zx[place.z]] + [zxrecv[k] for k in range(depth - 1)]
        highs = [small[:, 8 * i + 6 : 8 * i + 7] for small in smalls]
        top = functools.reduce(jnp.maximum, highs)
        scales = [jnp.exp(high - top) for high in highs]
        total = sum(small * scale for small, scale in zip(smalls, scales))
        denom = total[:, 8 * i + 5 : 8 * i + 6]
        here = slice(i * rows, (i + 1) * rows)
        seen[here, :main] = sum(value.astype(f32) * scale for value, scale in zip(mains, scales)) / denom
        if i:
            total = pltpu.roll(total, LANES - 8 * i, 1)
        seen[here, main:] = jnp.where(lane < feat - main, total / denom, 0.0)
        lse[here, :] = jnp.broadcast_to(top + jnp.log(denom), (rows, LANES))

    for name in ("wv", "wo", "wh", "wb", "cot"):
        loads[name].wait()
    owned = micro * rows
    attended = dot(seen[...].astype(bf16), wv[...], 1, 0).astype(bf16)
    hidden_in = x_in[...].reshape(owned, width).astype(f32) + dot(attended, wo[...], 1, 0)
    up_out[...] = hidden_in.reshape(micro, rows, width)
    unit_m, spread_m = normed(hidden_in)
    nm[...] = (unit_m * gain_mlp[...]).astype(bf16)
    pre = dot(nm[...], wh[...], 1, 0)
    cumulative = 0.5 * (1.0 + lax.erf(pre * math.sqrt(0.5)))
    act[...] = (pre * cumulative).astype(bf16)
    slope = cumulative + pre * jnp.exp(-0.5 * pre * pre) * (1.0 / math.sqrt(2.0 * math.pi))
    cot_low = cot_in[...].reshape(owned, width).astype(bf16)
    gpre[...] = (slope * dot(cot_low, wb[...], 1, 1)).astype(bf16)
    grad_nm = dot(gpre[...], wh[...], 1, 1)
    grad_gm = jnp.sum(grad_nm * unit_m, axis=0, keepdims=True)
    grad_h[...] = cot_in[...].reshape(owned, width) + normed_back(grad_nm * gain_mlp[...], unit_m, spread_m)
    gh_low[...] = grad_h[...].astype(bf16)
    grad_att = dot(gh_low[...], wo[...], 1, 1).astype(bf16)
    grad_seen = dot(grad_att, wv[...], 1, 1)
    dots = jnp.sum(grad_seen * seen[...], axis=1, keepdims=True)
    dots_high, dots_low = split_low(-dots)
    lse_value = lse[:, 0:1]
    lse_high = lse_value.astype(bf16).astype(f32)
    lse_mid, lse_low = split_low(lse_value - lse_high)
    lane = lanes_of((owned, LANES))
    tail = grad_seen[:, main:]
    for k, column in ((5, dots_high), (6, lse_high), (7, lse_mid), (8, lse_low), (9, dots_low)):
        tail = jnp.where(lane == k, column, tail)
    small = jnp.zeros((rows, LANES), f32)
    for i in range(micro):
        here = slice(i * rows, (i + 1) * rows)
        g_all[i, place.y, place.z] = grad_seen[here, :main].astype(bf16)
        small = small + (tail[here] if i == 0 else pltpu.roll(tail[here], 16 * i, 1))
    gx_all[place.y, place.z] = small.astype(bf16)
    g_ext = Gather(links, place, part(gx_all))
    g_main = [Gather(links, place, part(g_all.at[i])) for i in range(micro)]
    g_ext.begin()
    for gather in g_main:
        gather.begin()

    half = width // 2
    totals = []

    def grown(left, right, src, recv, out, lanes):
        src[...] = dot(left, right, 0, 0).astype(bf16)
        total = Total(links, place, src, recv, out, kept_sem.at[len(totals)], lanes)
        totals.append(total)
        total.send(0)

    for k in range(2):
        here = slice(k * half, (k + 1) * half)
        cot_half = cot_in[:, :, here].reshape(owned, half).astype(bf16)
        grown(act[...], cot_half, back_src.at[k], recvs[k], sum_back, here)
    g_ext.forward()
    g_main[0].forward()
    totals[0].rs(0)
    for k in range(2):
        here = slice(k * half, (k + 1) * half)
        grown(nm[...], gpre[:, here], hidden_src.at[k], recvs[2 + k], sum_hidden, here)
    g_main[1].forward()
    seen_low = seen[...].astype(bf16)
    grown(gh_low[...], seen_low[:, :main], value_src, recvs[4], sum_value, slice(0, main))
    up_out[...] = up_out[...] + dot(act[...], wb[...], 1, 0).reshape(micro, rows, width)
    g_main[2].forward()
    stores = [pltpu.make_async_copy(up_out, updated, store_sem.at[0])]
    stores[0].start()
    for k in range(1, 5):
        totals[k].rs(0)
    g_main[3].forward()
    load("px_again0", pixels.at[0], px.at[0]).start()
    load("px_again1", pixels.at[1], px.at[1]).start()

    def grad_block(i):
        small = gx_all[...].reshape(everyone, LANES).astype(f32)
        if i:
            small = pltpu.roll(small, LANES - 16 * i, 1)
        lane = lanes_of((everyone, LANES))
        whole = small[:, 6:7] + small[:, 7:8] + small[:, 8:9]
        own_top = jnp.broadcast_to(tops[i][0:1], (LANES, everyone)).T
        scale = jnp.exp(own_top[:, 0:1] - whole)
        dots_high, dots_low = split_low((small[:, 5:6] + small[:, 9:10]) * scale)
        tail = jnp.where(lane < 5, small * scale, 0.0)
        tail = jnp.where(lane == 5, dots_high, tail)
        tail = jnp.where(lane == 7, dots_low, tail)
        value = g_all[i].reshape(everyone, main).astype(f32) * scale
        return jnp.concatenate([value.astype(bf16), tail.astype(bf16)], axis=1)

    def attend_back(i):
        g_main[i].end()
        block = grad_block(i)
        grad_s[...] = (probs[i].astype(f32) * dot(np_all[i], block, 1, 1)).astype(bf16)
        sums = dot(npt_all[i], grad_s[...], 1, 0)
        for y in range(2):
            here = slice(y * line, (y + 1) * line)
            bb[i, y] = sums[:main, here].astype(bf16)
            be[i, y] = sums[main : main + 8, here]
        copies = exchange(i, bb, be, brecv, berecv)
        scores[:, :wide] = dot(probs[i], block, 1, 0) + dot(grad_s[...], query_block(i), 1, 0)
        loads[f"px_again{i}"].wait()
        unit, spread = normed(px[i % 2].astype(f32))
        grad_np = scores[:, :feat]
        gp_acc[:, :feat] += jnp.sum(grad_np * unit, axis=0, keepdims=True)
        if i >= 2:
            stores[i - 1].wait()
        px_out[i % 2] = normed_back(grad_np * gain_pixel[:, :feat], unit, spread)
        stores.append(pltpu.make_async_copy(px_out.at[i % 2], grad_pixels.at[i], store_sem.at[1 + i]))
        stores[-1].start()
        if i + 2 < micro:
            load(f"px_again{i + 2}", pixels.at[i + 2], px.at[i % 2]).start()
        return copies

    small_back = []

    def merge_back(i, copies):
        for copy in copies:
            copy.wait_recv()
        total = bb[i, place.y].astype(f32) + brecv[i].astype(f32)
        yb[i] = total.T.astype(bf16).reshape(depth, rows, main)
        small_back.append(be[i, place.y] + berecv[i])
        return to_owners(yb.at[i], yrecv.at[i])

    b_swaps, b_merged = {}, {}
    g_ext.end()
    b_swaps[0] = attend_back(0)
    totals[0].rs(1)
    b_swaps[1] = attend_back(1)
    b_merged[0] = merge_back(0, b_swaps[0])
    totals[1].rs(1)
    b_swaps[2] = attend_back(2)
    b_merged[1] = merge_back(1, b_swaps[1])
    totals[2].rs(1)
    b_swaps[3] = attend_back(3)
    b_merged[2] = merge_back(2, b_swaps[2])
    totals[3].rs(1)
    b_merged[3] = merge_back(3, b_swaps[3])
    spread_small(small_back, yx)
    arrivals = to_owners(yx, yxrecv)
    for i in range(micro):
        arrivals = arrivals + b_merged[i]
    for copy in arrivals:
        copy.wait_recv()

    lane = lanes_of((rows, LANES))
    parts = []
    for i in range(micro):
        value = yb[i, place.z].astype(f32) + sum(yrecv[i, k].astype(f32) for k in range(depth - 1))
        small = yx[place.z] + sum(yxrecv[k] for k in range(depth - 1))
        if i:
            small = pltpu.roll(small, LANES - 8 * i, 1)
        small = jnp.where(lane < feat - main, small, 0.0)
        parts.append(jnp.concatenate([value.astype(bf16), small.astype(bf16)], axis=1))
    back_feats = jnp.concatenate(parts, axis=0)
    late = dot(nq[...], back_feats, 0, 0)
    late_src[:, :main] = late[:, :main].astype(bf16)
    value_tail = pltpu.roll(seen[:, main:], 16, 1).astype(bf16)
    late_tail = late[:, main:] + dot(gh_low[...], value_tail, 0, 0)
    grad_q = (dot(back_feats, wk[...], 1, 0) * scaling).astype(bf16)
    grad_nq = dot(grad_q, wq[...], 1, 1)
    unit_q, spread_q = normed(x_in[...].reshape(owned, width).astype(f32))
    grad_gq = jnp.sum(grad_nq * unit_q, axis=0, keepdims=True)
    row = rows_of((8, width))
    gp_row = jnp.concatenate([gp_acc[...], jnp.zeros((1, width - wide), f32)], axis=1)
    gains[32:40, :] = jnp.where(row == 0, grad_gm, jnp.where(row == 1, grad_gq, jnp.where(row == 2, gp_row, 0.0)))
    late_src[:, main:] = (late_tail + gains[...].T).astype(bf16)
    total = Total(links, place, late_src, recvs[5], sum_late, kept_sem.at[len(totals)], slice(0, wide))
    totals.append(total)
    total.send(0)
    stores[0].wait()
    up_out[...] = (grad_h[...] + normed_back(grad_nq * gain_query[...], unit_q, spread_q)).reshape(micro, rows, width)
    last = pltpu.make_async_copy(up_out, grad_latents, store_sem.at[1 + micro])
    last.start()
    stores.append(last)

    total.rs(0)
    totals[4].rs(1)
    for stage in (2, 3):
        for k in range(5):
            totals[k].rs(stage)
        total.rs(stage - 1)
    total.rs(3)
    for stage in range(4):
        for k in range(6):
            totals[k].back(stage)
    for store in stores[max(1, len(stores) - 3) :]:
        store.wait()
    links.drain()


def fused(mesh, pixels, counts, latents, cotangent, w_query, w_key, w_value, w_out, w_hidden, w_back, gain_query, gain_pixel, gain_mlp):
    micro, px_rows, feat = pixels.shape
    rows, width = latents.shape[1:]
    depth = mesh.shape["blk"] // 2
    main = feat // LANES * LANES
    wide = main + LANES
    line = depth * rows
    dims = (micro, rows, depth, px_rows, feat, main, wide, width)
    tall = lambda w: jnp.pad(w, ((0, wide - feat), (0, 0)))
    any_spec = pl.BlockSpec(memory_space=pl.ANY)
    vmem = pl.BlockSpec(memory_space=pltpu.VMEM)
    V = pltpu.VMEM
    half = width // 2

    def total_recvs(lanes):
        return (
            V((width // 2, lanes), bf16), V((width // 4, lanes), bf16), V((width // 8, lanes), bf16),
            V((depth - 1, width // 8 // depth, lanes), bf16),
        )

    def reduce_buffers(stat_rows):
        return [
            V((micro, 2, main, line), bf16), V((micro, 2, stat_rows, line), f32),
            V((micro, main, line), bf16), V((micro, stat_rows, line), f32),
            V((micro, depth, rows, main), bf16), V((depth, rows, LANES), f32),
            V((micro, depth - 1, rows, main), bf16), V((depth - 1, rows, LANES), f32),
        ]

    per_gather, per_owner, per_total = depth, 2 + depth - 1, 3 + 2 * (depth - 1) + 3
    copies = 2 * (micro + 1) * per_gather + 2 * (micro * per_owner + depth - 1) + 6 * per_total
    scratch = (
        [
            V((2, px_rows, feat), bf16), V((micro, px_rows, wide), bf16), V((micro, main + 16, px_rows), bf16),
            V((px_rows, 2 * line), f32), V((micro, px_rows, 2 * line), bf16), V((px_rows, 2 * line), bf16),
            V(latents.shape, bf16), V(cotangent.shape, f32),
        ]
        + [V((width, width), bf16)] * 4
        + [V((wide, width), bf16)] * 2
        + [V((micro, 2, depth, rows, main), bf16), V((2, depth, rows, LANES), bf16)] * 2
        + reduce_buffers(8)
        + reduce_buffers(8)
        + [
            V((micro, 8, 2 * line), f32), V((micro * rows, wide), f32), V((micro * rows, LANES), f32),
        ]
        + [V((micro * rows, width), bf16)] * 4
        + [V((micro * rows, width), f32), V((micro * rows, width), bf16), V(latents.shape, f32)]
        + [V((2, px_rows, feat), f32), V((LANES, width), f32), V((1, wide), f32)]
        + [
            V((2, width, half), bf16), V((2, width, half), bf16), V((width, main), bf16), V((width, wide), bf16),
            [total_recvs(lanes) for lanes in (half, half, half, half, main, wide)],
            pltpu.SemaphoreType.DMA((copies,)), pltpu.SemaphoreType.DMA((copies,)),
            pltpu.SemaphoreType.DMA((8 + 2 * micro,)), pltpu.SemaphoreType.DMA((2 + micro,)), pltpu.SemaphoreType.DMA((6,)),
        ]
    )
    S = jax.ShapeDtypeStruct
    return pl.pallas_call(
        functools.partial(kernel, dims),
        out_shape=[
            S(latents.shape, f32), S(latents.shape, f32), S(pixels.shape, f32),
            S((width, width), bf16), S((width, width), bf16), S((width, main), bf16), S((width, wide), bf16),
        ],
        in_specs=[pl.BlockSpec(memory_space=pltpu.SMEM)] + [any_spec] * 9 + [vmem] * 3,
        out_specs=[any_spec] * 7,
        scratch_shapes=scratch,
        compiler_params=pltpu.CompilerParams(collective_id=0, has_side_effects=True, vmem_limit_bytes=63 * 2**20),
        name="layer",
    )(
        counts, pixels, latents, cotangent, w_query, w_out, w_hidden, w_back, tall(w_key), tall(w_value),
        gain_query.reshape(1, -1), jnp.pad(gain_pixel.reshape(1, -1), ((0, 0), (0, wide - feat))), gain_mlp.reshape(1, -1),
    )


def fused_body(mesh, *args):
    w_query, w_key, w_value, w_out = args[4:8]
    feat, width = w_key.shape
    main = feat // LANES * LANES
    updated, grad_latents, grad_pixels, back, hidden, value, late = fused(mesh, *args)
    scaling = 1.0 / math.sqrt(width)
    query_b = late[:, :feat]
    value_b = jnp.concatenate([value, late[:, main + 16 : main + 16 + feat - main]], axis=1)
    gains = late[:, main + 32 : main + 35].astype(f32)
    return (
        updated,
        grad_latents,
        grad_pixels,
        dot(query_b, w_key, 1, 0) * scaling,
        dot(query_b, w_query, 0, 0) * scaling,
        dot(value_b, w_out, 0, 1),
        dot(w_value, value_b, 0, 1),
        hidden.astype(f32),
        back.astype(f32),
        gains[:, 1],
        gains[:feat, 2],
        gains[:, 0],
    )


def layer_norm(values, gain_vec):
    centered = values - jnp.mean(values, axis=-1, keepdims=True)
    variance = jnp.mean(centered * centered, axis=-1, keepdims=True)
    return centered * lax.rsqrt(variance + EPSILON) * gain_vec


def gelu_exact(values):
    return jax.nn.gelu(values, approximate=False)


def low(values):
    return values.astype(jnp.bfloat16)


def product(left_mat, right_mat):
    return jnp.dot(left_mat, right_mat, preferred_element_type=jnp.float32)


def product_tn(left_mat, right_mat):
    return lax.dot_general(
        left_mat, right_mat, (((0,), (0,)), ((), ())), preferred_element_type=jnp.float32
    )


def product_nt(left_mat, right_mat):
    return lax.dot_general(
        left_mat, right_mat, (((1,), (1,)), ((), ())), preferred_element_type=jnp.float32
    )


def each(spec, left, right):
    return jnp.einsum(spec, left, right, preferred_element_type=jnp.float32)


def to_owner(x, peers):
    micro, rows = x.shape[:2]
    blocks = jnp.moveaxis(x.reshape(micro, peers, rows // peers, *x.shape[2:]), 1, 0)
    return lax.all_to_all(blocks, "blk", 0, 0, tiled=True)


def plain_body(pixels, counts, latents, cotangent, w_query, w_key, w_value, w_out, w_hidden, w_back, gain_query, gain_pixel, gain_mlp):
    micro, pixel_rows, features = pixels.shape
    lat_rows, width = latents.shape[1:]
    peers = lax.axis_size("blk")
    scaling = 1.0 / math.sqrt(width)
    rows = micro * lat_rows
    positions = lax.axis_index("blk") * pixel_rows + jnp.arange(pixel_rows, dtype=jnp.int32)
    valid = positions[None, :] < counts[:, None]

    latent_in = latents.reshape(rows, width).astype(jnp.float32)
    normed_qf, query_pull = jax.vjp(layer_norm, latent_in, gain_query)
    normed_q = low(normed_qf)
    queries = low(product(normed_q, w_query))
    query_feats = low(product_nt(queries, w_key) * scaling).reshape(micro, lat_rows, features)
    all_query = lax.all_gather(query_feats, "blk", axis=1, tiled=True)
    normed_pf, pixel_pull = jax.vjp(layer_norm, pixels.astype(jnp.float32), gain_pixel)
    normed_p = low(normed_pf)
    scores = each("mqf,mpf->mqp", all_query, normed_p)
    scores = jnp.where(valid[:, None, :], scores, MASKED)
    highest = jnp.max(scores, axis=2)
    unscaled = jnp.exp(scores - highest[..., None])
    total = jnp.sum(unscaled, axis=2)
    sums = low(each("mqp,mpf->mqf", low(unscaled), normed_p))
    parts = to_owner(sums, peers).astype(jnp.float32)
    stats = to_owner(jnp.stack([highest, total], axis=2), peers)
    top = jnp.max(stats[..., 0], axis=0)
    scale = jnp.exp(stats[..., 0] - top)
    denom = jnp.sum(stats[..., 1] * scale, axis=0)
    lse = top + jnp.log(denom)
    seen = (jnp.sum(parts * scale[..., None], axis=0) / denom[..., None]).reshape(rows, features)
    seen_b = low(seen)
    attended_b = low(product(seen_b, w_value))
    hidden_in = latent_in + product(attended_b, w_out)
    normed_mf, mlp_pull = jax.vjp(layer_norm, hidden_in, gain_mlp)
    normed_m = low(normed_mf)
    pre_act = product(normed_m, w_hidden)
    activated_f, gelu_pull = jax.vjp(gelu_exact, pre_act)
    activated = low(activated_f)
    updated = hidden_in + product(activated, w_back)
    cot = cotangent.reshape(rows, width)
    cot_b = low(cot)
    grad_back = product_tn(activated, cot_b)
    (grad_pre,) = gelu_pull(product_nt(cot_b, w_back))
    grad_pre_b = low(grad_pre)
    grad_hidden = product_tn(normed_m, grad_pre_b)
    grad_h_ln, grad_gm = mlp_pull(product_nt(grad_pre_b, w_hidden))
    grad_h = cot + grad_h_ln
    grad_h_b = low(grad_h)
    grad_att = low(product_nt(grad_h_b, w_out))
    grad_seen = product_nt(grad_att, w_value)
    dots = jnp.sum(grad_seen * seen, axis=1).reshape(micro, lat_rows)
    value_side = product_tn(seen_b, grad_h_b)
    all_grad = lax.all_gather(low(grad_seen).reshape(micro, lat_rows, features), "blk", axis=1, tiled=True)
    all_stat = lax.all_gather(jnp.stack([lse, dots], axis=2), "blk", axis=1, tiled=True)
    probs = unscaled * jnp.exp(highest - all_stat[..., 0])[..., None]
    grad_probs = each("mqf,mpf->mqp", all_grad, normed_p)
    grad_scores = low(probs * (grad_probs - all_stat[..., 1][..., None]))
    back_sums = low(each("mqp,mpf->mqf", grad_scores, normed_p))
    grad_np = each("mqp,mqf->mpf", low(probs), all_grad) + each("mqp,mqf->mpf", grad_scores, all_query)
    grad_pixels, grad_gp = pixel_pull(grad_np)
    back_feats = jnp.sum(to_owner(back_sums, peers).astype(jnp.float32), axis=0).reshape(rows, features)
    back_b = low(back_feats)
    grad_q = low(product(back_b, w_key) * scaling)
    grad_lat_q, grad_gq = query_pull(product_nt(grad_q, w_query))
    grad_latents = grad_h + grad_lat_q
    query_side = product_tn(normed_q, back_b)
    query_side, value_side, grad_hidden, grad_back, grad_gq, grad_gp, grad_gm = lax.psum(
        (query_side, value_side, grad_hidden, grad_back, grad_gq, grad_gp, grad_gm), ("img", "blk")
    )
    query_b, value_b = low(query_side * scaling), low(value_side)
    return (
        updated.reshape(micro, lat_rows, width),
        grad_latents.reshape(micro, lat_rows, width),
        grad_pixels,
        product(query_b, w_key),
        product_tn(query_b, w_query),
        product_nt(value_b, w_out),
        product_tn(w_value, value_b),
        grad_hidden,
        grad_back,
        grad_gq,
        grad_gp,
        grad_gm,
    )


def body(mesh, *args):
    pixels, latents = args[0], args[2]
    rows, width = latents.shape[1:]
    fits = rows % 16 == 0 and width % (16 * mesh.size) == 0 and mesh.shape["img"] == 4 and mesh.shape["blk"] % 2 == 0
    return fused_body(mesh, *args) if fits else plain_body(*args)


def solution(mesh):
    spread, same = P("img", "blk", None), P()
    return jax.shard_map(
        functools.partial(body, mesh),
        mesh=mesh,
        in_specs=(spread, P("img"), spread, spread) + (same,) * 9,
        out_specs=(spread,) * 3 + (same,) * 9,
        check_vma=False,
    )
```

```python
import functools
import math

import jax
import jax.numpy as jnp
from jax import lax
from jax.experimental import pallas as pl
from jax.experimental.pallas import tpu as pltpu
from jax.sharding import PartitionSpec as P

EPSILON = 1e-05
MASKED = -1e30
LANES = 128
MESH = pl.DeviceIdType.MESH
bf16, f32 = jnp.bfloat16, jnp.float32


def dot(left, right, left_dim, right_dim):
    return lax.dot_general(left, right, (((left_dim,), (right_dim,)), ((), ())), preferred_element_type=f32)


def lanes_of(shape):
    return lax.broadcasted_iota(jnp.int32, shape, 1)


def rows_of(shape):
    return lax.broadcasted_iota(jnp.int32, shape, 0)


def normed(values):
    part = 1.0 / values.shape[1]
    centered = values - jnp.sum(values, axis=1, keepdims=True) * part
    spread = lax.rsqrt(jnp.sum(centered * centered, axis=1, keepdims=True) * part + EPSILON)
    return centered * spread, spread


def normed_back(grad, unit, spread):
    part = 1.0 / grad.shape[1]
    first = jnp.sum(grad, axis=1, keepdims=True) * part
    second = jnp.sum(grad * unit, axis=1, keepdims=True) * part
    return spread * (grad - first - unit * second)


def split_low(values):
    high = values.astype(bf16).astype(f32)
    return high, (values - high).astype(bf16).astype(f32)


ORDER = (
    "B0", "B1", "x0", "g0", "H0", "H1", "V0", "r00", "r01", "g1", "r02", "r03", "r04", "e0", "a0", "g2", "r10", "a1", "g3", "m0",
    "U0", "a2", "m1", "r20", "a3", "r30", "m2", "b00", "m3", "r11", "r12", "r13", "r14", "Q0", "r21", "r22", "b10", "r05", "r31",
    "s0", "r23", "b01", "r32", "r24", "r15", "s1", "b11", "b02", "r33", "s2", "b12", "r25", "b03", "r34", "r35", "b13", "S0",
    "b04", "b20", "b05", "b14", "b21", "b15", "b22", "b23", "b24", "b25", "b30", "b31", "b32", "b33", "b34", "b35",
)


class Links:
    def __init__(self, send_sem, recv_sem):
        self.send_sem, self.recv_sem, self.used, self.sent = send_sem, recv_sem, 0, []

    def remote(self, src, dst, device):
        k = self.used
        self.used += 1
        return pltpu.make_async_remote_copy(
            src_ref=src, dst_ref=dst, send_sem=self.send_sem.at[k], recv_sem=self.recv_sem.at[k],
            device_id=device, device_id_type=MESH,
        )

    def start(self, copy):
        copy.start()
        self.sent.append(copy)

    def drain(self):
        for copy in self.sent:
            copy.wait_send()
        self.sent = []


class Place:
    def __init__(self, depth):
        img, blk = lax.axis_index("img"), lax.axis_index("blk")
        self.x, self.c = lax.div(img, 2), lax.rem(img, 2)
        self.z, self.y = lax.div(blk, 2), lax.rem(blk, 2)
        self.core_peer = (self.x * 2 + 1 - self.c, blk)
        self.x_peer = ((1 - self.x) * 2 + self.c, blk)
        self.y_peer = (img, self.z * 2 + 1 - self.y)
        self.z_index = [lax.rem(self.z + k, depth) for k in range(1, depth)]
        self.z_peers = [(img, other * 2 + self.y) for other in self.z_index]
        self.z_sources = [lax.rem(self.z + depth - k, depth) for k in range(1, depth)]

    def all(self):
        return [self.core_peer, self.x_peer, self.y_peer] + self.z_peers


class Gather:
    def __init__(self, links, place, block):
        own = block(place.y, place.z)
        self.links = links
        self.along = [links.remote(own, own, peer) for peer in place.z_peers]
        self.across = [links.remote(own, own, place.y_peer)]
        for source in place.z_sources:
            self.across.append(links.remote(block(place.y, source), block(place.y, source), place.y_peer))

    def begin(self):
        for copy in self.along + self.across[:1]:
            self.links.start(copy)

    def forward(self):
        for came, copy in zip(self.along, self.across[1:]):
            came.wait_recv()
            self.links.start(copy)

    def end(self):
        for copy in self.across:
            copy.wait_recv()


class Everywhere:
    def __init__(self, links, place, src, recv, slots):
        self.links, self.src, self.recv, self.slots, self.z = links, src, recv, slots, place.z
        peers = (place.core_peer, place.x_peer, place.y_peer)
        self.swaps = [links.remote(src.at[k], recv.at[k], peer) for k, peer in enumerate(peers)]
        self.along = [links.remote(slots.at[place.z], slots.at[place.z], peer) for peer in place.z_peers]

    def begin(self, value):
        self.src[0] = value.astype(bf16)
        self.links.start(self.swaps[0])

    def stage(self, k):
        self.swaps[k].wait_recv()
        total = (self.src[k].astype(f32) + self.recv[k].astype(f32)).astype(bf16)
        if k < 2:
            self.src[k + 1] = total
            self.links.start(self.swaps[k + 1])
        else:
            self.slots[self.z] = total
            for copy in self.along:
                self.links.start(copy)

    def end(self):
        for copy in self.along:
            copy.wait_recv()
        return sum(self.slots[k].astype(f32) for k in range(len(self.along) + 1))


class Total:
    def __init__(self, links, place, src, recv, out, local_sem, lanes):
        height = src.shape[0]
        self.links, self.src, self.recv, self.out = links, src, recv, out
        peers = (place.core_peer, place.x_peer, place.y_peer)
        coords = (place.c, place.x, place.y)
        self.halves, self.backs, offset = [], [], 0
        self.spans = []
        for peer, coord, held in zip(peers, coords, recv[:3]):
            height //= 2
            there = pl.multiple_of(offset + (1 - coord) * height, height)
            offset = pl.multiple_of(offset + coord * height, height)
            self.spans.append((offset, height))
            self.halves.append(links.remote(src.at[pl.ds(there, height)], held, peer))
        depth = len(place.z_peers) + 1
        height //= depth
        self.piece = pl.multiple_of(offset + place.z * height, height)
        self.height = height
        self.quarters = []
        for k, (peer, index) in enumerate(zip(place.z_peers, place.z_index)):
            there = pl.multiple_of(offset + index * height, height)
            self.quarters.append(links.remote(src.at[pl.ds(there, height)], recv[3].at[k], peer))
        mine = src.at[pl.ds(self.piece, height)]
        self.shown = [links.remote(mine, out.at[pl.ds(self.piece, height), lanes], peer) for peer in place.z_peers]
        self.kept = pltpu.make_async_copy(mine, out.at[pl.ds(self.piece, height), lanes], local_sem)
        for (start, size), peer in zip(reversed(self.spans), reversed(peers)):
            region = out.at[pl.ds(start, size), lanes]
            self.backs.append(links.remote(region, region, peer))

    def send(self, stage):
        if stage < 3:
            self.links.start(self.halves[stage])
        else:
            for copy in self.quarters:
                self.links.start(copy)

    def add(self, stage):
        if stage < 3:
            self.halves[stage].wait_recv()
            start, size = self.spans[stage]
            step = min(size, 64)

            def some(k):
                here = pl.ds(pl.multiple_of(start + k * step, step), step)
                there = pl.ds(pl.multiple_of(k * step, step), step)
                held = self.recv[stage][there, :].astype(f32)
                self.src[here, :] = (self.src[here, :].astype(f32) + held).astype(bf16)

            pl.loop(0, size // step)(some)
        else:
            for copy in self.quarters:
                copy.wait_recv()
            here = pl.ds(self.piece, self.height)
            total = self.src[here, :].astype(f32)
            for k in range(len(self.quarters)):
                total = total + self.recv[3][k].astype(f32)
            self.src[here, :] = total.astype(bf16)

    def turn(self):
        self.kept.start()
        for copy in self.shown:
            self.links.start(copy)

    def back(self, stage):
        if stage == 0:
            for copy in self.shown:
                copy.wait_recv()
            self.kept.wait()
        else:
            self.backs[stage - 1].wait_recv()
        if stage < 3:
            self.links.start(self.backs[stage])

    def rs(self, stage):
        self.add(stage)
        if stage < 3:
            self.send(stage + 1)
        else:
            self.turn()


def kernel(
    dims,
    counts, pixels, latents, cotangent, w_query, w_out, w_hidden, w_back, w_key, w_value, gain_query, gain_pixel, gain_mlp,
    updated, grad_latents, grad_pixels, sum_back, sum_hidden, sum_value, sum_late, sum_small,
    px, px_t, px_stats, np_all, npt_all, scores, probs, grad_s, x_in, cot_in, wq, wo, wh, wb, wk_in, wv_in, wk, wv,
    q_all, qx_all, g_all, gx_all,
    ob, oe, orecv, oerecv, zb, zx, zrecv, zxrecv,
    bb, be, brecv, berecv, yb, yx, yrecv, yxrecv,
    tops, seen, lse, nq, nm, act, gpre, grad_h, gh_low, up_out, px_out, small_src, small_recv, small_slots, small_out, gp_acc,
    back_src, hidden_src, value_src, late_src, recvs, send_sem, recv_sem, load_sem, store_sem, kept_sem,
):
    micro, rows, depth, px_rows, feat, main, wide, width = dims
    ext = wide - LANES
    line = depth * rows
    everyone = 2 * line
    scaling = 1.0 / math.sqrt(width)
    links, place = Links(send_sem, recv_sem), Place(depth)
    loads = {}

    def load(name, src, dst):
        loads[name] = pltpu.make_async_copy(src, dst, load_sem.at[len(loads)])
        return loads[name]

    load("x", latents, x_in).start()
    load("wq", w_query, wq).start()
    load("wk", w_key, wk_in).start()
    barrier = pltpu.get_barrier_semaphore()
    for peer in place.all():
        pl.semaphore_signal(barrier, inc=1, device_id=peer, device_id_type=MESH)
    gp_acc[...] = jnp.zeros_like(gp_acc)

    def pad_rows(raw, dst):
        dst[:main] = raw[:main]
        last = raw[main:].astype(f32)
        dst[main:] = jnp.concatenate([last, jnp.zeros((wide - feat, width), f32)], axis=0).astype(bf16)

    loads["x"].wait()
    loads["wq"].wait()
    loads["wk"].wait()
    load("px", pixels, px).start()
    for name, src, dst in (("wv", w_value, wv_in), ("wo", w_out, wo), ("wh", w_hidden, wh), ("wb", w_back, wb), ("cot", cotangent, cot_in)):
        load(name, src, dst).start()
    pad_rows(wk_in, wk)
    unit_q, _ = normed(x_in[...].reshape(micro * rows, width).astype(f32))
    nq[...] = (unit_q * gain_query[...]).astype(bf16)
    queries = dot(nq[...], wq[...], 1, 0).astype(bf16)
    feats = dot(queries, wk[...], 1, 1) * scaling
    small = jnp.where(lanes_of((rows, LANES)) % 16 == 6, 1.0, 0.0)
    for i in range(micro):
        here = slice(i * rows, (i + 1) * rows)
        q_all[i, place.y, place.z] = feats[here, :main].astype(bf16)
        tail = feats[here, main:]
        small = small + (tail if i == 0 else pltpu.roll(tail, 16 * i, 1))
    qx_all[place.y, place.z] = small.astype(bf16)
    pl.semaphore_wait(barrier, len(place.all()))

    def part(ref):
        return lambda y, z: ref.at[y, z]

    q_ext = Gather(links, place, part(qx_all))
    q_main = [Gather(links, place, part(q_all.at[i])) for i in range(micro)]
    q_ext.begin()
    for gather in q_main:
        gather.begin()

    first_pixel = lax.axis_index("blk") * px_rows
    tall = main + 16
    gain_column = jnp.broadcast_to(gain_pixel[...], (LANES, feat))
    gain_column = jnp.concatenate([gain_column, jnp.zeros((LANES, wide - feat), f32)], axis=1).T[:tall, 0:1]

    def pixel_rows():
        loads["px"].wait()
        for first in range(0, feat, 16):
            last = min(first + 16, feat)
            block = px[first:last].astype(f32)
            if last - first < 16:
                block = jnp.concatenate([block, jnp.zeros((16 - last + first,) + block.shape[1:], f32)], axis=0)
            block = jnp.swapaxes(block, 0, 1)
            for i in range(micro):
                px_t[i, first : first + 16] = block[i].astype(bf16)

    def pixel_unit(i, mean):
        centered = px_t[i].astype(f32) - mean
        return jnp.where(rows_of((tall, px_rows)) < feat, centered, 0.0)

    def pixel_norm(i):
        mean = jnp.sum(px_t[i].astype(f32), axis=0, keepdims=True) * (1.0 / feat)
        centered = pixel_unit(i, mean)
        spread = lax.rsqrt(jnp.sum(centered * centered, axis=0, keepdims=True) * (1.0 / feat) + EPSILON)
        px_stats[i, 0:1], px_stats[i, 1:2] = mean, spread
        row = rows_of((tall, px_rows))
        value = centered * spread * gain_column
        value = jnp.where((row == main + 5) | (row == main + 7), 1.0, value)
        npt_all[i] = value.astype(bf16)
        masked = first_pixel + lanes_of((tall, px_rows)) >= counts[i]
        value = jnp.where((row == main + 6) & masked, MASKED, value)
        np_all[i] = jnp.concatenate([value, jnp.zeros((wide - tall, px_rows), f32)], axis=0).T.astype(bf16)

    def query_block(i):
        small = qx_all[...].reshape(everyone, LANES).astype(f32)
        if i:
            small = pltpu.roll(small, LANES - 16 * i, 1)
        small = jnp.where(lanes_of((everyone, LANES)) < 16, small, 0.0)
        return jnp.concatenate([q_all[i].reshape(everyone, main), small.astype(bf16)], axis=1)

    def attend(i):
        q_main[i].end()
        scores[...] = dot(np_all[i], query_block(i), 1, 1)
        top = jnp.max(scores[...], axis=0, keepdims=True)
        tops[i] = jnp.broadcast_to(top, (8, everyone))
        probs[i] = jnp.exp(scores[...] - top).astype(bf16)
        sums = dot(npt_all[i], probs[i], 1, 0)
        small = jnp.where(rows_of((8, everyone)) == 6, top, sums[main : main + 8])
        for y in range(2):
            here = slice(y * line, (y + 1) * line)
            ob[i, y] = sums[:main, here].astype(bf16)
            oe[i, y] = small[:, here]

    def exchange(i, sums, ext_sums, held, ext_held):
        copies = [
            links.remote(sums.at[i, 1 - place.y], held.at[i], place.y_peer),
            links.remote(ext_sums.at[i, 1 - place.y], ext_held.at[i], place.y_peer),
        ]
        for copy in copies:
            links.start(copy)
        return copies

    def to_owners(src, dst):
        copies = [
            links.remote(src.at[other], dst.at[k], peer)
            for k, (peer, other) in enumerate(zip(place.z_peers, place.z_index))
        ]
        for copy in copies:
            links.start(copy)
        return copies

    def spread_small(parts, block):
        tall = jnp.concatenate(parts + [jnp.zeros((LANES - 8 * micro, line), f32)], axis=0)
        block[...] = tall.T.reshape(depth, rows, LANES)

    small_parts = []

    def merge(i, copies):
        for copy in copies:
            copy.wait_recv()
        mine, theirs = oe[i, place.y], oerecv[i]
        top_m, top_t = mine[6:7], theirs[6:7]
        top = jnp.maximum(top_m, top_t)
        scale_m, scale_t = jnp.exp(top_m - top), jnp.exp(top_t - top)
        total = ob[i, place.y].astype(f32) * scale_m + orecv[i].astype(f32) * scale_t
        zb[i] = total.T.astype(bf16).reshape(depth, rows, main)
        small = mine * scale_m + theirs * scale_t
        small_parts.append(jnp.where(rows_of((8, line)) == 6, top, small))
        return to_owners(zb.at[i], zrecv.at[i])

    q_swaps, q_merged = {}, {}
    pixel_rows()
    pixel_norm(0)
    q_ext.forward()
    q_main[0].forward()
    pixel_norm(1)
    q_main[1].forward()
    q_ext.end()
    for i in range(micro):
        if i + 2 < micro:
            pixel_norm(i + 2)
        attend(i)
        q_swaps[i] = exchange(i, ob, oe, orecv, oerecv)
        if i + 2 < micro:
            q_main[i + 2].forward()
        if i >= 1:
            q_merged[i - 1] = merge(i - 1, q_swaps[i - 1])
    q_merged[micro - 1] = merge(micro - 1, q_swaps[micro - 1])
    spread_small(small_parts, zx)
    arrivals = to_owners(zx, zxrecv)
    for i in range(micro):
        arrivals = arrivals + q_merged[i]
    for copy in arrivals:
        copy.wait_recv()

    lane = lanes_of((rows, LANES))
    for i in range(micro):
        mains = [zb[i, place.z]] + [zrecv[i, k] for k in range(depth - 1)]
        smalls = [zx[place.z]] + [zxrecv[k] for k in range(depth - 1)]
        highs = [small[:, 8 * i + 6 : 8 * i + 7] for small in smalls]
        top = functools.reduce(jnp.maximum, highs)
        scales = [jnp.exp(high - top) for high in highs]
        total = sum(small * scale for small, scale in zip(smalls, scales))
        denom = total[:, 8 * i + 5 : 8 * i + 6]
        here = slice(i * rows, (i + 1) * rows)
        seen[here, :main] = sum(value.astype(f32) * scale for value, scale in zip(mains, scales)) / denom
        if i:
            total = pltpu.roll(total, LANES - 8 * i, 1)
        seen[here, main:] = jnp.where(lane < feat - main, total / denom, 0.0)
        lse[here, :] = jnp.broadcast_to(top + jnp.log(denom), (rows, LANES))

    for name in ("wv", "wo", "wh", "wb", "cot"):
        loads[name].wait()
    pad_rows(wv_in, wv)
    owned = micro * rows
    attended = dot(seen[...].astype(bf16), wv[...], 1, 0).astype(bf16)
    hidden_in = x_in[...].reshape(owned, width).astype(f32) + dot(attended, wo[...], 1, 0)
    up_out[...] = hidden_in.reshape(micro, rows, width)
    unit_m, spread_m = normed(hidden_in)
    nm[...] = (unit_m * gain_mlp[...]).astype(bf16)
    pre = dot(nm[...], wh[...], 1, 0)
    cumulative = 0.5 * (1.0 + lax.erf(pre * math.sqrt(0.5)))
    act[...] = (pre * cumulative).astype(bf16)
    slope = cumulative + pre * jnp.exp(-0.5 * pre * pre) * (1.0 / math.sqrt(2.0 * math.pi))
    cot_low = cot_in[...].reshape(owned, width).astype(bf16)
    gpre[...] = (slope * dot(cot_low, wb[...], 1, 1)).astype(bf16)
    grad_nm = dot(gpre[...], wh[...], 1, 1)
    grad_gm = jnp.sum(grad_nm * unit_m, axis=0, keepdims=True)
    grad_h[...] = cot_in[...].reshape(owned, width) + normed_back(grad_nm * gain_mlp[...], unit_m, spread_m)
    gh_low[...] = grad_h[...].astype(bf16)
    grad_att = dot(gh_low[...], wo[...], 1, 1).astype(bf16)
    grad_seen = dot(grad_att, wv[...], 1, 1)
    dots = jnp.sum(grad_seen * seen[...], axis=1, keepdims=True)
    dots_high, dots_low = split_low(-dots)
    lse_value = lse[:, 0:1]
    lse_high = lse_value.astype(bf16).astype(f32)
    lse_mid, lse_low = split_low(lse_value - lse_high)
    lane = lanes_of((owned, LANES))
    tail = grad_seen[:, main:]
    for k, column in ((5, dots_high), (6, lse_high), (7, lse_mid), (8, lse_low), (9, dots_low)):
        tail = jnp.where(lane == k, column, tail)
    small = jnp.zeros((rows, LANES), f32)
    for i in range(micro):
        here = slice(i * rows, (i + 1) * rows)
        g_all[i, place.y, place.z] = grad_seen[here, :main].astype(bf16)
        small = small + (tail[here] if i == 0 else pltpu.roll(tail[here], 16 * i, 1))
    gx_all[place.y, place.z] = small.astype(bf16)
    g_ext = Gather(links, place, part(gx_all))
    g_main = [Gather(links, place, part(g_all.at[i])) for i in range(micro)]
    g_ext.begin()
    for gather in g_main:
        gather.begin()

    half = width // 2
    totals = []

    stores = []
    up_store = pltpu.make_async_copy(up_out, updated, store_sem.at[0])

    def summed(src, recv, out, lanes):
        total = Total(links, place, src, recv, out, kept_sem.at[len(totals)], lanes)
        totals.append(total)
        total.send(0)

    def grown(left, right, src, recv, out, lanes):
        src[...] = dot(left, right, 0, 0).astype(bf16)
        summed(src, recv, out, lanes)

    def grad_block(i):
        small = gx_all[...].reshape(everyone, LANES).astype(f32)
        if i:
            small = pltpu.roll(small, LANES - 16 * i, 1)
        lane = lanes_of((everyone, LANES))
        whole = small[:, 6:7] + small[:, 7:8] + small[:, 8:9]
        own_top = jnp.broadcast_to(tops[i][0:1], (LANES, everyone)).T
        scale = jnp.exp(own_top[:, 0:1] - whole)
        dots_high, dots_low = split_low((small[:, 5:6] + small[:, 9:10]) * scale)
        tail = jnp.where(lane < 5, small * scale, 0.0)
        tail = jnp.where(lane == 5, dots_high, tail)
        tail = jnp.where(lane == 7, dots_low, tail)
        value = g_all[i].reshape(everyone, main).astype(f32) * scale
        return jnp.concatenate([value.astype(bf16), tail.astype(bf16)], axis=1)

    def attend_back(i):
        g_main[i].end()
        block = grad_block(i)
        grad_s[...] = (probs[i].astype(f32) * dot(np_all[i], block, 1, 1)).astype(bf16)
        sums = dot(npt_all[i], grad_s[...], 1, 0)
        for y in range(2):
            here = slice(y * line, (y + 1) * line)
            bb[i, y] = sums[:main, here].astype(bf16)
            be[i, y] = sums[main : main + 8, here]
        copies = exchange(i, bb, be, brecv, berecv)
        block_t = block.astype(f32).T[:tall].astype(bf16)
        query_t = query_block(i).astype(f32).T[:tall].astype(bf16)
        grad_np = dot(block_t, probs[i], 1, 1) + dot(query_t, grad_s[...], 1, 1)
        grad_np = jnp.where(rows_of((tall, px_rows)) < feat, grad_np, 0.0)
        spread = px_stats[i, 1:2]
        unit = pixel_unit(i, px_stats[i, 0:1]) * spread
        terms = grad_np * unit
        gp_acc[...] += sum(terms[:, k : k + LANES] for k in range(0, px_rows, LANES))
        grad_np = grad_np * gain_column
        first = jnp.sum(grad_np, axis=0, keepdims=True) * (1.0 / feat)
        second = jnp.sum(grad_np * unit, axis=0, keepdims=True) * (1.0 / feat)
        px_out[i] = (spread * (grad_np - first - unit * second)).astype(bf16)
        stores.append(pltpu.make_async_copy(px_out.at[i], grad_pixels.at[i], store_sem.at[1 + i]))
        stores[-1].start()
        return copies

    small_back = []

    def merge_back(i, copies):
        for copy in copies:
            copy.wait_recv()
        total = bb[i, place.y].astype(f32) + brecv[i].astype(f32)
        yb[i] = total.T.astype(bf16).reshape(depth, rows, main)
        small_back.append(be[i, place.y] + berecv[i])
        return to_owners(yb.at[i], yrecv.at[i])

    b_swaps, b_merged = {}, {}

    def swap_back(i):
        b_swaps[i] = attend_back(i)

    def join_back(i):
        b_merged[i] = merge_back(i, b_swaps[i])

    def back_term(k):
        here = slice(k * half, (k + 1) * half)
        grown(act[...], cot_in[:, :, here].reshape(owned, half).astype(bf16), back_src.at[k], recvs[k], sum_back, here)

    def hidden_term(k):
        here = slice(k * half, (k + 1) * half)
        grown(nm[...], gpre[:, here], hidden_src.at[k], recvs[2 + k], sum_hidden, here)

    def value_term(k):
        grown(gh_low[...], seen[:, :main].astype(bf16), value_src, recvs[4], sum_value, slice(0, main))

    def layer_out(k):
        up_out[...] = up_out[...] + dot(act[...], wb[...], 1, 0).reshape(micro, rows, width)
        up_store.start()

    def queries_back(k):
        spread_small(small_back, yx)
        arrivals = to_owners(yx, yxrecv)
        for i in range(micro):
            arrivals = arrivals + b_merged[i]
        for copy in arrivals:
            copy.wait_recv()
        lane = lanes_of((rows, LANES))
        parts = []
        for i in range(micro):
            value = yb[i, place.z].astype(f32) + sum(yrecv[i, k].astype(f32) for k in range(depth - 1))
            small = yx[place.z] + sum(yxrecv[k] for k in range(depth - 1))
            if i:
                small = pltpu.roll(small, LANES - 8 * i, 1)
            small = jnp.where(lane < feat - main, small, 0.0)
            parts.append(jnp.concatenate([value.astype(bf16), small.astype(bf16)], axis=1))
        back_feats = jnp.concatenate(parts, axis=0)
        late_src[...] = dot(nq[...], back_feats[:, :main], 0, 0).astype(bf16)
        summed(late_src, recvs[5], sum_late, slice(0, main))
        grad_q = (dot(back_feats, wk[...], 1, 0) * scaling).astype(bf16)
        grad_nq = dot(grad_q, wq[...], 1, 1)
        unit_q, spread_q = normed(x_in[...].reshape(owned, width).astype(f32))
        value_tail = pltpu.roll(seen[:, main:], 5, 1).astype(bf16)
        row = rows_of((16, width))
        terms = dot(back_feats[:, main:], nq[...], 0, 0)[:16] + dot(value_tail, gh_low[...], 0, 0)[:16]
        terms = jnp.where(row == 10, grad_gm, terms)
        terms = jnp.where(row == 11, jnp.sum(grad_nq * unit_q, axis=0, keepdims=True), terms)
        grad_gp = jnp.concatenate([gp_acc[...], jnp.zeros((wide - tall, LANES), f32)], axis=0).T
        grad_gp = jnp.sum(grad_gp, axis=0, keepdims=True)
        grad_gp = jnp.concatenate([grad_gp, jnp.zeros((1, width - wide), f32)], axis=1)
        small_sum.begin(jnp.where(row == 12, grad_gp, terms))
        up_store.wait()
        up_out[...] = (grad_h[...] + normed_back(grad_nq * gain_query[...], unit_q, spread_q)).reshape(micro, rows, width)
        last = pltpu.make_async_copy(up_out, grad_latents, store_sem.at[1 + micro])
        last.start()
        stores.append(last)


    small_sum = Everywhere(links, place, small_src, small_recv, small_slots)

    def small_end(k):
        small_out[...] = small_sum.end()
        stores.append(pltpu.make_async_copy(small_out, sum_small, store_sem.at[2 + micro]))
        stores[-1].start()

    steps = {
        "B": back_term, "H": hidden_term, "V": value_term, "U": layer_out, "Q": queries_back,
        "x": lambda k: g_ext.forward(), "g": lambda k: g_main[k].forward(), "e": lambda k: g_ext.end(), "s": lambda k: small_sum.stage(k), "S": small_end,
        "a": swap_back, "m": join_back,
    }
    for step in ORDER:
        if step[0] == "r":
            totals[int(step[2])].rs(int(step[1]))
        elif step[0] == "b":
            totals[int(step[2])].back(int(step[1]))
        else:
            steps[step[0]](int(step[1]))
    for store in stores:
        store.wait()
    links.drain()


def fused(mesh, pixels, counts, latents, cotangent, w_query, w_key, w_value, w_out, w_hidden, w_back, gain_query, gain_pixel, gain_mlp):
    micro, px_rows, feat = pixels.shape
    rows, width = latents.shape[1:]
    depth = mesh.shape["blk"] // 2
    main = feat // LANES * LANES
    wide = main + LANES
    line = depth * rows
    dims = (micro, rows, depth, px_rows, feat, main, wide, width)
    tall = main + 16
    any_spec = pl.BlockSpec(memory_space=pl.ANY)
    vmem = pl.BlockSpec(memory_space=pltpu.VMEM)
    V = pltpu.VMEM
    half = width // 2

    def total_recvs(lanes):
        return (
            V((width // 2, lanes), bf16), V((width // 4, lanes), bf16), V((width // 8, lanes), bf16),
            V((depth - 1, width // 8 // depth, lanes), bf16),
        )

    def reduce_buffers(stat_rows):
        return [
            V((micro, 2, main, line), bf16), V((micro, 2, stat_rows, line), f32),
            V((micro, main, line), bf16), V((micro, stat_rows, line), f32),
            V((micro, depth, rows, main), bf16), V((depth, rows, LANES), f32),
            V((micro, depth - 1, rows, main), bf16), V((depth - 1, rows, LANES), f32),
        ]

    per_gather, per_owner, per_total = 2 * depth - 1, 2 + depth - 1, 3 + 2 * (depth - 1) + 3
    copies = 2 * (micro + 1) * per_gather + 2 * (micro * per_owner + depth - 1) + 6 * per_total + 3 + depth - 1
    scratch = (
        [
            V((feat, micro, px_rows), bf16), V((micro, tall, px_rows), bf16), V((micro, 8, px_rows), f32),
            V((micro, px_rows, wide), bf16), V((micro, tall, px_rows), bf16),
            V((px_rows, 2 * line), f32), V((micro, px_rows, 2 * line), bf16), V((px_rows, 2 * line), bf16),
            V(latents.shape, bf16), V(cotangent.shape, f32),
        ]
        + [V((width, width), bf16)] * 4
        + [V((feat, width), bf16)] * 2
        + [V((wide, width), bf16)] * 2
        + [V((micro, 2, depth, rows, main), bf16), V((2, depth, rows, LANES), bf16)] * 2
        + reduce_buffers(8)
        + reduce_buffers(8)
        + [
            V((micro, 8, 2 * line), f32), V((micro * rows, wide), f32), V((micro * rows, LANES), f32),
        ]
        + [V((micro * rows, width), bf16)] * 4
        + [V((micro * rows, width), f32), V((micro * rows, width), bf16), V(latents.shape, f32)]
        + [V((micro, tall, px_rows), bf16),
            V((3, 16, width), bf16), V((3, 16, width), bf16), V((depth, 16, width), bf16), V((16, width), f32), V((tall, LANES), f32),
        ]
        + [
            V((2, width, half), bf16), V((2, width, half), bf16), V((width, main), bf16), V((width, main), bf16),
            [total_recvs(lanes) for lanes in (half, half, half, half, main, main)],
            pltpu.SemaphoreType.DMA((copies,)), pltpu.SemaphoreType.DMA((copies,)),
            pltpu.SemaphoreType.DMA((16,)), pltpu.SemaphoreType.DMA((3 + micro,)), pltpu.SemaphoreType.DMA((6,)),
        ]
    )
    S = jax.ShapeDtypeStruct
    return pl.pallas_call(
        functools.partial(kernel, dims),
        out_shape=[
            S(latents.shape, f32), S(latents.shape, f32), S((micro, tall, px_rows), bf16),
            S((width, width), bf16), S((width, width), bf16), S((width, main), bf16), S((width, main), bf16), S((16, width), f32),
        ],
        in_specs=[pl.BlockSpec(memory_space=pltpu.SMEM)] + [any_spec] * 9 + [vmem] * 3,
        out_specs=[any_spec] * 8,
        scratch_shapes=scratch,
        compiler_params=pltpu.CompilerParams(collective_id=0, has_side_effects=True, vmem_limit_bytes=63 * 2**20),
        name="layer",
    )(
        counts, jnp.transpose(pixels, (2, 0, 1)), latents, cotangent, w_query, w_out, w_hidden, w_back, w_key, w_value,
        gain_query.reshape(1, -1), gain_pixel.reshape(1, -1), gain_mlp.reshape(1, -1),
    )


def finish(
    dims,
    late, value, small, w_key, w_value, w_query, w_out, hidden, back, px, up, lat,
    out_query, out_key, out_value, out_out, out_hidden, out_back, out_px, out_up, out_lat, out_gq, out_gp, out_gm,
    key_rows, value_rows, late_t, value_t, late_rows,
):
    feat, main, wide, width = dims
    scaling = 1.0 / math.sqrt(width)
    step = out_query.shape[0]
    here = pl.ds(pl.multiple_of(pl.program_id(0) * step, step), step)

    @pl.when(pl.program_id(0) == 0)
    def prepare():
        for raw, dst in ((w_key, key_rows), (w_value, value_rows)):
            dst[:main] = raw[:main]
            last = raw[main:].astype(f32)
            dst[main:] = jnp.concatenate([last, jnp.zeros((wide - feat, width), f32)], axis=0).astype(bf16)
        row = rows_of((16, width))
        rest = jnp.zeros((LANES - 16, width), f32)
        tail = jnp.concatenate([jnp.where(row < 5, small[...], 0.0), rest], axis=0)
        late_rows[:, :main] = late[...]
        late_rows[:, main:] = tail.T.astype(bf16)
        late_t[:main] = late[...].astype(f32).T.astype(bf16)
        late_t[main:] = tail.astype(bf16)
        tail = jnp.concatenate([jnp.where(row < 5, pltpu.roll(small[...], 11, 0), 0.0), rest], axis=0)
        value_t[:main] = value[...].astype(f32).T.astype(bf16)
        value_t[main:] = tail.astype(bf16)
        out_gm[...] = small[10]
        out_gq[...] = small[11]
        out_gp[...] = small[12, :feat]

    out_query[...] = dot(late_rows[here, :], key_rows[...], 1, 0) * scaling
    out_out[...] = dot(value_rows[:, here], value_t[...], 0, 0)
    out_key[...] = (dot(late_t[...], w_query[...], 1, 0) * scaling)[:feat]
    out_value[...] = dot(value_t[...], w_out[...], 1, 1)[:feat]
    out_hidden[...] = hidden[...].astype(f32)
    out_back[...] = back[...].astype(f32)
    out_px[...] = jnp.swapaxes(px[...].astype(f32), 0, 1)
    out_up[...] = up[...]
    out_lat[...] = lat[...]


def fused_body(mesh, *args):
    pixels, latents = args[0], args[2]
    w_query, w_key, w_value, w_out = args[4:8]
    micro, px_rows, feat = pixels.shape
    rows, width = latents.shape[1:]
    main = feat // LANES * LANES
    wide = main + LANES
    up, lat, px, back, hidden, value, late, small = fused(mesh, *args)
    steps = 4
    step, px_step = width // steps, -(-feat // (16 * steps)) * 16
    whole = lambda *shape: pl.BlockSpec(shape, lambda k: (0,) * len(shape))
    by_row = pl.BlockSpec((step, width), lambda k: (k, 0))
    by_column = lambda height: pl.BlockSpec((height, step), lambda k: (0, k))
    lat_block = pl.BlockSpec((micro, rows // steps, width), lambda k: (0, k, 0))
    S = jax.ShapeDtypeStruct
    out = pl.pallas_call(
        functools.partial(finish, (feat, main, wide, width)),
        grid=(steps,),
        in_specs=[
            whole(width, main), whole(width, main), whole(16, width), whole(feat, width), whole(feat, width), by_column(width), by_row,
            by_row, by_row, pl.BlockSpec((micro, px_step, px_rows), lambda k: (0, k, 0)), lat_block, lat_block,
        ],
        out_specs=[
            by_row, by_column(feat), by_column(feat), by_row, by_row, by_row,
            pl.BlockSpec((px_step, micro, px_rows), lambda k: (k, 0, 0)), lat_block, lat_block,
            whole(width), whole(feat), whole(width),
        ],
        out_shape=[
            S((width, width), f32), S((feat, width), f32), S((feat, width), f32), S((width, width), f32),
            S((width, width), f32), S((width, width), f32), S((feat, micro, px_rows), f32),
            S(latents.shape, f32), S(latents.shape, f32), S((width,), f32), S((feat,), f32), S((width,), f32),
        ],
        scratch_shapes=[pltpu.VMEM((wide, width), bf16)] * 4 + [pltpu.VMEM((width, wide), bf16)],
        compiler_params=pltpu.CompilerParams(vmem_limit_bytes=60 * 2**20),
        name="finish",
    )(late, value, small, w_key, w_value, w_query, w_out, hidden, back, px, up, lat)
    g_query, g_key, g_value, g_out, g_hidden, g_back, g_px, g_up, g_lat, g_gq, g_gp, g_gm = out
    g_px = jnp.transpose(g_px, (1, 2, 0))
    return g_up, g_lat, g_px, g_query, g_key, g_value, g_out, g_hidden, g_back, g_gq, g_gp, g_gm


def layer_norm(values, gain_vec):
    centered = values - jnp.mean(values, axis=-1, keepdims=True)
    variance = jnp.mean(centered * centered, axis=-1, keepdims=True)
    return centered * lax.rsqrt(variance + EPSILON) * gain_vec


def gelu_exact(values):
    return jax.nn.gelu(values, approximate=False)


def low(values):
    return values.astype(jnp.bfloat16)


def product(left_mat, right_mat):
    return jnp.dot(left_mat, right_mat, preferred_element_type=jnp.float32)


def product_tn(left_mat, right_mat):
    return lax.dot_general(
        left_mat, right_mat, (((0,), (0,)), ((), ())), preferred_element_type=jnp.float32
    )


def product_nt(left_mat, right_mat):
    return lax.dot_general(
        left_mat, right_mat, (((1,), (1,)), ((), ())), preferred_element_type=jnp.float32
    )


def each(spec, left, right):
    return jnp.einsum(spec, left, right, preferred_element_type=jnp.float32)


def to_owner(x, peers):
    micro, rows = x.shape[:2]
    blocks = jnp.moveaxis(x.reshape(micro, peers, rows // peers, *x.shape[2:]), 1, 0)
    return lax.all_to_all(blocks, "blk", 0, 0, tiled=True)


def plain_body(pixels, counts, latents, cotangent, w_query, w_key, w_value, w_out, w_hidden, w_back, gain_query, gain_pixel, gain_mlp):
    micro, pixel_rows, features = pixels.shape
    lat_rows, width = latents.shape[1:]
    peers = lax.axis_size("blk")
    scaling = 1.0 / math.sqrt(width)
    rows = micro * lat_rows
    positions = lax.axis_index("blk") * pixel_rows + jnp.arange(pixel_rows, dtype=jnp.int32)
    valid = positions[None, :] < counts[:, None]

    latent_in = latents.reshape(rows, width).astype(jnp.float32)
    normed_qf, query_pull = jax.vjp(layer_norm, latent_in, gain_query)
    normed_q = low(normed_qf)
    queries = low(product(normed_q, w_query))
    query_feats = low(product_nt(queries, w_key) * scaling).reshape(micro, lat_rows, features)
    all_query = lax.all_gather(query_feats, "blk", axis=1, tiled=True)
    normed_pf, pixel_pull = jax.vjp(layer_norm, pixels.astype(jnp.float32), gain_pixel)
    normed_p = low(normed_pf)
    scores = each("mqf,mpf->mqp", all_query, normed_p)
    scores = jnp.where(valid[:, None, :], scores, MASKED)
    highest = jnp.max(scores, axis=2)
    unscaled = jnp.exp(scores - highest[..., None])
    total = jnp.sum(unscaled, axis=2)
    sums = low(each("mqp,mpf->mqf", low(unscaled), normed_p))
    parts = to_owner(sums, peers).astype(jnp.float32)
    stats = to_owner(jnp.stack([highest, total], axis=2), peers)
    top = jnp.max(stats[..., 0], axis=0)
    scale = jnp.exp(stats[..., 0] - top)
    denom = jnp.sum(stats[..., 1] * scale, axis=0)
    lse = top + jnp.log(denom)
    seen = (jnp.sum(parts * scale[..., None], axis=0) / denom[..., None]).reshape(rows, features)
    seen_b = low(seen)
    attended_b = low(product(seen_b, w_value))
    hidden_in = latent_in + product(attended_b, w_out)
    normed_mf, mlp_pull = jax.vjp(layer_norm, hidden_in, gain_mlp)
    normed_m = low(normed_mf)
    pre_act = product(normed_m, w_hidden)
    activated_f, gelu_pull = jax.vjp(gelu_exact, pre_act)
    activated = low(activated_f)
    updated = hidden_in + product(activated, w_back)
    cot = cotangent.reshape(rows, width)
    cot_b = low(cot)
    grad_back = product_tn(activated, cot_b)
    (grad_pre,) = gelu_pull(product_nt(cot_b, w_back))
    grad_pre_b = low(grad_pre)
    grad_hidden = product_tn(normed_m, grad_pre_b)
    grad_h_ln, grad_gm = mlp_pull(product_nt(grad_pre_b, w_hidden))
    grad_h = cot + grad_h_ln
    grad_h_b = low(grad_h)
    grad_att = low(product_nt(grad_h_b, w_out))
    grad_seen = product_nt(grad_att, w_value)
    dots = jnp.sum(grad_seen * seen, axis=1).reshape(micro, lat_rows)
    value_side = product_tn(seen_b, grad_h_b)
    all_grad = lax.all_gather(low(grad_seen).reshape(micro, lat_rows, features), "blk", axis=1, tiled=True)
    all_stat = lax.all_gather(jnp.stack([lse, dots], axis=2), "blk", axis=1, tiled=True)
    probs = unscaled * jnp.exp(highest - all_stat[..., 0])[..., None]
    grad_probs = each("mqf,mpf->mqp", all_grad, normed_p)
    grad_scores = low(probs * (grad_probs - all_stat[..., 1][..., None]))
    back_sums = low(each("mqp,mpf->mqf", grad_scores, normed_p))
    grad_np = each("mqp,mqf->mpf", low(probs), all_grad) + each("mqp,mqf->mpf", grad_scores, all_query)
    grad_pixels, grad_gp = pixel_pull(grad_np)
    back_feats = jnp.sum(to_owner(back_sums, peers).astype(jnp.float32), axis=0).reshape(rows, features)
    back_b = low(back_feats)
    grad_q = low(product(back_b, w_key) * scaling)
    grad_lat_q, grad_gq = query_pull(product_nt(grad_q, w_query))
    grad_latents = grad_h + grad_lat_q
    query_side = product_tn(normed_q, back_b)
    query_side, value_side, grad_hidden, grad_back, grad_gq, grad_gp, grad_gm = lax.psum(
        (query_side, value_side, grad_hidden, grad_back, grad_gq, grad_gp, grad_gm), ("img", "blk")
    )
    query_b, value_b = low(query_side * scaling), low(value_side)
    return (
        updated.reshape(micro, lat_rows, width),
        grad_latents.reshape(micro, lat_rows, width),
        grad_pixels,
        product(query_b, w_key),
        product_tn(query_b, w_query),
        product_nt(value_b, w_out),
        product_tn(w_value, value_b),
        grad_hidden,
        grad_back,
        grad_gq,
        grad_gp,
        grad_gm,
    )


def body(mesh, *args):
    pixels, latents = args[0], args[2]
    rows, width = latents.shape[1:]
    fits = rows % 16 == 0 and width % (16 * mesh.size) == 0 and mesh.shape["img"] == 4 and mesh.shape["blk"] % 2 == 0
    return fused_body(mesh, *args) if fits else plain_body(*args)


def solution(mesh):
    spread, same = P("img", "blk", None), P()
    return jax.shard_map(
        functools.partial(body, mesh),
        mesh=mesh,
        in_specs=(spread, P("img"), spread, spread) + (same,) * 9,
        out_specs=(spread,) * 3 + (same,) * 9,
        check_vma=False,
    )
```

```python
import functools
import math

import jax
import jax.numpy as jnp
from jax import lax
from jax.experimental import pallas as pl
from jax.experimental.pallas import tpu as pltpu
from jax.sharding import PartitionSpec as P

EPSILON = 1e-05
MASKED = -1e30
LANES = 128
MESH = pl.DeviceIdType.MESH
bf16, f32 = jnp.bfloat16, jnp.float32


def dot(left, right, left_dim, right_dim):
    return lax.dot_general(left, right, (((left_dim,), (right_dim,)), ((), ())), preferred_element_type=f32)


def lanes_of(shape):
    return lax.broadcasted_iota(jnp.int32, shape, 1)


def rows_of(shape):
    return lax.broadcasted_iota(jnp.int32, shape, 0)


def normed(values):
    part = 1.0 / values.shape[1]
    centered = values - jnp.sum(values, axis=1, keepdims=True) * part
    spread = lax.rsqrt(jnp.sum(centered * centered, axis=1, keepdims=True) * part + EPSILON)
    return centered * spread, spread


def normed_back(grad, unit, spread):
    part = 1.0 / grad.shape[1]
    first = jnp.sum(grad, axis=1, keepdims=True) * part
    second = jnp.sum(grad * unit, axis=1, keepdims=True) * part
    return spread * (grad - first - unit * second)


def split_low(values):
    high = values.astype(bf16).astype(f32)
    return high, (values - high).astype(bf16).astype(f32)


ORDER = (
    "P0", "p0", "p1", "p3", "p2", "X0", "q0", "E0", "q1", "A0", "q2", "A1", "q3", "M0", "A2", "M1", "Z0", "A3", "M2", "O0", "M3",
    "Z1", "N0", "O1", "N1", "B4", "U0", "B2", "g0", "B3", "x0", "B1", "B0", "x1", "g1", "r04", "r02", "g2", "e0", "e1", "a0",
    "r03", "r14", "r01", "a1", "g3", "r00", "a2", "m0", "r12", "r24", "m1", "a3", "r34", "r13", "m2", "b04", "r11", "r22", "m3",
    "r10", "r23", "r32", "b14", "Q0", "L0", "r33", "r21", "b24", "r20", "r05", "b02", "s0", "b34", "b03", "r15", "s1", "b12",
    "r31", "b13", "r30", "r25", "s2", "b01", "b22", "b00", "r35", "b11", "b32", "S0", "b23", "b10", "b05", "b33", "b15", "b21",
    "b31", "b20", "b25", "b30", "b35",
)


def chunks_of(width, main):
    half = width // 2
    return (
        (0, slice(0, half), "xyz"), (0, slice(half, width), "xyz"), (1, slice(0, half), "xyz"), (1, slice(half, width), "xyz"),
        (2, slice(0, main), "xyz"), (3, slice(0, main), "xyz"),
    )


class Links:
    def __init__(self, send_sem, recv_sem):
        self.send_sem, self.recv_sem, self.arrivals, self.groups = send_sem, recv_sem, 0, []

    def group(self, size):
        self.groups.append(size)
        return len(self.groups) - 1

    def arrival(self):
        self.arrivals += 1
        return self.arrivals - 1

    def remote(self, src, dst, device, group, arrival):
        return pltpu.make_async_remote_copy(
            src_ref=src, dst_ref=dst, send_sem=self.send_sem.at[group], recv_sem=self.recv_sem.at[arrival],
            device_id=device, device_id_type=MESH,
        )

    def wait(self, size, arrival):
        pltpu.make_async_copy(size, size, self.recv_sem.at[arrival]).wait()

    def drain(self):
        for group, size in enumerate(self.groups):
            pltpu.make_async_copy(size, size, self.send_sem.at[group]).wait()


class Place:
    def __init__(self, depth):
        img, blk = lax.axis_index("img"), lax.axis_index("blk")
        self.x, self.c = lax.div(img, 2), lax.rem(img, 2)
        self.z, self.y = lax.div(blk, 2), lax.rem(blk, 2)
        self.core_peer = (self.x * 2 + 1 - self.c, blk)
        self.x_peer = ((1 - self.x) * 2 + self.c, blk)
        self.y_peer = (img, self.z * 2 + 1 - self.y)
        self.z_index = [lax.rem(self.z + k, depth) for k in range(1, depth)]
        self.z_peers = [(img, other * 2 + self.y) for other in self.z_index]
        self.z_sources = [lax.rem(self.z + depth - k, depth) for k in range(1, depth)]

    def all(self):
        return [self.core_peer, self.x_peer, self.y_peer] + self.z_peers


class Gather:
    def __init__(self, links, place, ref, group, size):
        own = ref.at[place.y, place.z]
        self.links, self.size, self.line = links, size, ref.at[0]
        self.came_z, self.came_y = links.arrival(), links.arrival()
        self.along = [links.remote(own, own, peer, group, self.came_z) for peer in place.z_peers]
        self.across = []
        for source in [place.z] + place.z_sources:
            block = ref.at[place.y, source]
            self.across.append(links.remote(block, block, place.y_peer, group, self.came_y))

    def begin(self):
        for copy in self.along + self.across[:1]:
            copy.start()

    def forward(self):
        self.links.wait(self.size, self.came_z)
        for copy in self.across[1:]:
            copy.start()

    def end(self):
        self.links.wait(self.line, self.came_y)


class Everywhere:
    def __init__(self, links, place, src, recv, slots, group):
        self.links, self.src, self.recv, self.slots, self.z = links, src, recv, slots, place.z
        peers = (place.core_peer, place.x_peer, place.y_peer)
        self.came = [links.arrival() for _ in range(4)]
        self.swaps = [links.remote(src.at[k], recv.at[k], peer, group, self.came[k]) for k, peer in enumerate(peers)]
        mine = slots.at[place.z]
        self.along = [links.remote(mine, mine, peer, group, self.came[3]) for peer in place.z_peers]

    def begin(self, value):
        self.src[0] = value.astype(bf16)
        self.swaps[0].start()

    def stage(self, k):
        self.links.wait(self.recv.at[k], self.came[k])
        total = (self.src[k].astype(f32) + self.recv[k].astype(f32)).astype(bf16)
        if k < 2:
            self.src[k + 1] = total
            self.swaps[k + 1].start()
        else:
            self.slots[self.z] = total
            for copy in self.along:
                copy.start()

    def end(self):
        count = len(self.along)
        self.links.wait(self.slots.at[pl.ds(0, count)], self.came[3])
        return sum(self.slots[k].astype(f32) for k in range(count + 1))


class Total:
    def __init__(self, links, place, along, src, recv, out, local_sem, lanes):
        self.links, self.src, self.recv = links, src, recv
        half_peers = {"c": (place.core_peer, place.c), "x": (place.x_peer, place.x), "y": (place.y_peer, place.y)}
        depth = len(place.z_peers) + 1
        region = lambda ref, start, size: ref.at[pl.ds(start, size)]
        shown = lambda start, size: out.at[pl.ds(start, size), lanes]
        axes = ("c",) + tuple(along)
        self.came = [links.arrival() for _ in axes]
        self.came_back = [links.arrival() for _ in axes]
        last = src.shape[0] // (8 * depth)
        sizes = [region(src, 0, src.shape[0] - last)] * 2
        there, back = links.group(sizes[0]), links.group(sizes[1])
        offset, height = 0, src.shape[0]
        self.there, self.spans, peers_of = [], [], []
        for k, axis in enumerate(axes):
            if axis == "z":
                height //= depth
                starts = [pl.multiple_of(offset + index * height, height) for index in place.z_index]
                peers, index = place.z_peers, place.z
            else:
                height //= 2
                peer, index = half_peers[axis]
                starts, peers = [pl.multiple_of(offset + (1 - index) * height, height)], [peer]
            self.there.append([
                links.remote(region(src, start, height), recv[k].at[n], peer, there, self.came[k])
                for n, (start, peer) in enumerate(zip(starts, peers))
            ])
            offset = pl.multiple_of(offset + index * height, height)
            self.spans.append((offset, height))
            peers_of.append(peers)
        mine = region(src, offset, height)
        self.kept = pltpu.make_async_copy(mine, shown(offset, height), local_sem)
        self.backs = []
        for k in range(3, -1, -1):
            start, size = self.spans[k]
            held = mine if k == 3 else shown(start, size)
            self.backs.append([links.remote(held, shown(start, size), peer, back, self.came_back[k]) for peer in peers_of[k]])

    def send(self, stage):
        for copy in self.there[stage]:
            copy.start()

    def rs(self, stage):
        held = self.recv[stage]
        self.links.wait(held, self.came[stage])
        start, size = self.spans[stage]
        step = min(size, 64)

        def some(k):
            here = pl.ds(pl.multiple_of(start + k * step, step), step)
            block = pl.ds(pl.multiple_of(k * step, step), step)
            total = self.src[here, :].astype(f32)
            for n in range(held.shape[0]):
                total = total + held[n, block, :].astype(f32)
            self.src[here, :] = total.astype(bf16)

        pl.loop(0, size // step)(some)
        if stage < 3:
            self.send(stage + 1)
        else:
            self.kept.start()
            for copy in self.backs[0]:
                copy.start()

    def back(self, stage):
        self.links.wait(self.recv[3 - stage], self.came_back[3 - stage])
        if stage == 0:
            self.kept.wait()
        if stage < 3:
            for copy in self.backs[stage + 1]:
                copy.start()


def kernel(
    dims,
    counts, pixels, latents, cotangent, w_query, w_out, w_hidden, w_back, w_key, w_value, gain_query, gain_pixel, gain_mlp,
    updated, grad_latents, grad_pixels, sum_back, sum_hidden, sum_value, sum_late, sum_small,
    px, px_t, px_stats, np_all, npt_all, scores, probs, grad_s, x_in, cot_in, wq, wo, wh, wb, wk_in, wv_in, wk, wv,
    q_all, qx_all, g_all, gx_all,
    ob, oe, orecv, oerecv, zb, zrecv, bb, be, brecv, berecv, yb, yrecv, zs, zsrecv, y_small, ys, ysrecv,
    tops, seen, lse, g_small, back_low, nq, nm, act, gpre, grad_h, gh_low, up_out, small_src, small_recv, small_slots, small_out, gp_acc,
    sources, recvs, send_sem, recv_sem, load_sem, store_sem, kept_sem,
):
    micro, rows, depth, px_rows, feat, main, wide, width = dims
    pair = micro // 2
    chunks = chunks_of(width, main)
    line = depth * rows
    everyone = 2 * line
    scaling = 1.0 / math.sqrt(width)
    links, place = Links(send_sem, recv_sem), Place(depth)
    loads = {}

    def load(name, src, dst):
        loads[name] = pltpu.make_async_copy(src, dst, load_sem.at[len(loads)])
        return loads[name]

    load("x", latents, x_in).start()
    load("wq", w_query, wq).start()
    load("wk", w_key, wk_in).start()
    barrier = pltpu.get_barrier_semaphore()
    for peer in place.all():
        pl.semaphore_signal(barrier, inc=1, device_id=peer, device_id_type=MESH)
    gp_acc[...] = jnp.zeros_like(gp_acc)

    def pad_rows(raw, dst):
        dst[:main] = raw[:main]
        last = raw[main:].astype(f32)
        dst[main:] = jnp.concatenate([last, jnp.zeros((wide - feat, width), f32)], axis=0).astype(bf16)

    loads["x"].wait()
    unit_q, _ = normed(x_in[...].reshape(micro * rows, width).astype(f32))
    nq[...] = (unit_q * gain_query[...]).astype(bf16)
    loads["wq"].wait()
    loads["wk"].wait()
    load("px", pixels, px).start()
    for name, src, dst in (("wv", w_value, wv_in), ("wo", w_out, wo), ("wh", w_hidden, wh), ("wb", w_back, wb), ("cot", cotangent, cot_in)):
        load(name, src, dst).start()
    pad_rows(wk_in, wk)
    queries = dot(nq[...], wq[...], 1, 0).astype(bf16)
    feats = dot(queries, wk[...], 1, 1) * scaling
    small = jnp.where(lanes_of((rows, LANES)) % 16 == 6, 1.0, 0.0)
    for i in range(micro):
        here = slice(i * rows, (i + 1) * rows)
        q_all[i, place.y, place.z] = feats[here, :main].astype(bf16)
        tail = feats[here, main:]
        small = small + (tail if i == 0 else pltpu.roll(tail, 16 * i, 1))
    qx_all[place.y, place.z] = small.astype(bf16)
    pl.semaphore_wait(barrier, len(place.all()))

    def gathers(main_ref, ext_refs, ext_size):
        blocks = micro * (2 * depth - 1)
        group = links.group(wq.at[pl.ds(0, blocks * rows * main // width)])
        mains = [Gather(links, place, main_ref.at[i], group, zrecv.at[i]) for i in range(micro)]
        group = links.group(lse.at[pl.ds(0, len(ext_refs) * (2 * depth - 1) * ext_size.shape[0] // (depth - 1))])
        return mains, [Gather(links, place, ref, group, ext_size) for ref in ext_refs]

    q_main, (q_ext,) = gathers(q_all, [qx_all], lse.at[pl.ds(0, (depth - 1) * rows // 2)])
    g_main, g_ext = gathers(g_all, [gx_all.at[g] for g in range(2)], lse.at[pl.ds(0, (depth - 1) * 8)])
    q_ext.begin()
    for gather in q_main:
        gather.begin()

    first_pixel = lax.axis_index("blk") * px_rows
    tall = main + 16
    gain_column = jnp.broadcast_to(gain_pixel[...].reshape(1, feat), (LANES, feat))
    gain_column = jnp.concatenate([gain_column, jnp.zeros((LANES, wide - feat), f32)], axis=1).T[:tall, 0:1]

    def pixel_rows():
        loads["px"].wait()
        for first in range(0, feat, 16):
            last = min(first + 16, feat)
            block = px[first:last].astype(f32)
            if last - first < 16:
                block = jnp.concatenate([block, jnp.zeros((16 - last + first,) + block.shape[1:], f32)], axis=0)
            block = jnp.swapaxes(block, 0, 1)
            for i in range(micro):
                px_t[i, first : first + 16] = block[i].astype(bf16)

    def pixel_unit(i, mean):
        centered = px_t[i].astype(f32) - mean
        return jnp.where(rows_of((tall, px_rows)) < feat, centered, 0.0)

    def pixel_norm(i):
        mean = jnp.sum(px_t[i].astype(f32), axis=0, keepdims=True) * (1.0 / feat)
        centered = pixel_unit(i, mean)
        spread = lax.rsqrt(jnp.sum(centered * centered, axis=0, keepdims=True) * (1.0 / feat) + EPSILON)
        px_stats[i, 0:1], px_stats[i, 1:2] = mean, spread
        row = rows_of((tall, px_rows))
        value = centered * spread * gain_column
        value = jnp.where((row == main + 5) | (row == main + 7), 1.0, value)
        npt_all[i] = value.astype(bf16)
        masked = first_pixel + lanes_of((tall, px_rows)) >= counts[i]
        value = jnp.where((row == main + 6) & masked, MASKED, value)
        np_all[i] = jnp.concatenate([value, jnp.zeros((wide - tall, px_rows), f32)], axis=0).T.astype(bf16)

    def query_block(i):
        small = qx_all[...].reshape(everyone, LANES).astype(f32)
        if i:
            small = pltpu.roll(small, LANES - 16 * i, 1)
        small = jnp.where(lanes_of((everyone, LANES)) < 16, small, 0.0)
        return jnp.concatenate([q_all[i].reshape(everyone, main), small.astype(bf16)], axis=1)

    def attend(i):
        q_main[i].end()
        scores[...] = dot(np_all[i], query_block(i), 1, 1)
        top = jnp.max(scores[...], axis=0, keepdims=True)
        tops[i] = jnp.broadcast_to(top, (8, everyone))
        probs[i] = jnp.exp(scores[...] - top).astype(bf16)
        sums = dot(npt_all[i], probs[i], 1, 0)
        small = jnp.where(rows_of((8, everyone)) == 6, top, sums[main : main + 8])
        for y in range(2):
            here = slice(y * line, (y + 1) * line)
            ob[i, y] = sums[:main, here].astype(bf16)
            oe[i, y] = small[:, here]

    def exchanges(sums, small, held, small_held, parts, parts_held):
        main_group = links.group(wq.at[pl.ds(0, micro * line * main // width)])
        small_group = links.group(wq.at[pl.ds(0, micro * 2 * 8 * line // width)])
        owner_group = links.group(wq.at[pl.ds(0, micro * (depth - 1) * rows * main // width)])
        out = []
        for i in range(micro):
            came, small_came, owner_came = links.arrival(), links.arrival(), links.arrival()
            swaps = [
                links.remote(sums.at[i, 1 - place.y], held.at[i], place.y_peer, main_group, came),
                links.remote(small.at[i, 1 - place.y], small_held.at[i], place.y_peer, small_group, small_came),
            ]
            owners = [
                links.remote(parts.at[i, other], parts_held.at[i, k], peer, owner_group, owner_came)
                for k, (peer, other) in enumerate(zip(place.z_peers, place.z_index))
            ]
            out.append((swaps, owners, ((held.at[i], came), (small_held.at[i], small_came), (parts_held.at[i], owner_came))))
        return out

    def begin(copies):
        for copy in copies:
            copy.start()

    q_parts = exchanges(ob, oe, orecv, oerecv, zb, zrecv)
    b_parts = exchanges(bb, be, brecv, berecv, yb, yrecv)

    def own_lanes(part):
        part = pltpu.roll(part, lax.rem((depth - place.z) * rows, line), 1)[:, :LANES]
        return jnp.concatenate([part, jnp.zeros((LANES - part.shape[0], LANES), f32)], axis=0).T[:rows]

    def join(i):
        _, owners, waits = q_parts[i]
        links.wait(*waits[0])
        links.wait(*waits[1])
        mine, theirs = oe[i, place.y], oerecv[i]
        top_m, top_t = mine[6:7], theirs[6:7]
        top = jnp.maximum(top_m, top_t)
        scale_m, scale_t = jnp.exp(top_m - top), jnp.exp(top_t - top)
        total = ob[i, place.y].astype(f32) * scale_m + orecv[i].astype(f32) * scale_t
        zb[i] = total.T.astype(bf16).reshape(depth, rows, main)
        small = mine * scale_m + theirs * scale_t
        zs[i // pair, 8 * (i % pair) : 8 * (i % pair) + 8] = jnp.where(rows_of((8, line)) == 6, top, small)
        begin(owners)

    def attend_out(i):
        attend(i)
        begin(q_parts[i][0])

    def to_peers(src, dst, group):
        came = links.arrival()
        return [links.remote(src, dst.at[k], peer, group, came) for k, peer in enumerate(place.z_peers)], (dst, came)

    z_group = links.group(wq.at[pl.ds(0, 2 * (depth - 1) * 2 * 8 * pair * line // width)])
    z_small = [to_peers(zs.at[g], zsrecv.at[g], z_group) for g in range(2)]
    y_copies, y_came = to_peers(ys, ysrecv, links.group(lse.at[pl.ds(0, (depth - 1) * 4 * micro * line // LANES)]))

    def small_out_of(g):
        begin(z_small[g][0])

    grad_gm, owners = [], {}

    def owner_starts(g):
        owners[g] = owner(g)
        next(owners[g])

    def owner(g):
        images = range(g * pair, (g + 1) * pair)
        links.wait(*z_small[g][1])
        for i in images:
            links.wait(*q_parts[i][2][2])
        smalls = [own_lanes(zs[g])] + [own_lanes(zsrecv[g, k]) for k in range(depth - 1)]
        lane = lanes_of((rows, LANES))
        for i in images:
            mains = [zb[i, place.z]] + [zrecv[i, k] for k in range(depth - 1)]
            base = 8 * (i % pair)
            highs = [small[:, base + 6 : base + 7] for small in smalls]
            top = functools.reduce(jnp.maximum, highs)
            scales = [jnp.exp(high - top) for high in highs]
            total = sum(small * scale for small, scale in zip(smalls, scales))
            denom = total[:, base + 5 : base + 6]
            here = slice(i * rows, (i + 1) * rows)
            seen[here, :main] = sum(value.astype(f32) * scale for value, scale in zip(mains, scales)) / denom
            if base:
                total = pltpu.roll(total, LANES - base, 1)
            seen[here, main:] = jnp.where(lane < feat - main, total / denom, 0.0)
            lse[here, :] = jnp.broadcast_to(top + jnp.log(denom), (rows, LANES))
        if g == 0:
            for name in ("wv", "wo", "wh", "wb", "cot"):
                loads[name].wait()
            pad_rows(wv_in, wv)
        own = pair * rows
        here, images = slice(g * own, (g + 1) * own), slice(g * pair, (g + 1) * pair)
        attended = dot(seen[here, :].astype(bf16), wv[...], 1, 0).astype(bf16)
        hidden_in = x_in[images].reshape(own, width).astype(f32) + dot(attended, wo[...], 1, 0)
        up_out[images] = hidden_in.reshape(pair, rows, width)
        unit_m, spread_m = normed(hidden_in)
        normed_m = (unit_m * gain_mlp[...]).astype(bf16)
        nm[here, :] = normed_m
        pre = dot(normed_m, wh[...], 1, 0)
        cumulative = 0.5 * (1.0 + lax.erf(pre * math.sqrt(0.5)))
        act[here, :] = (pre * cumulative).astype(bf16)
        yield
        slope = cumulative + pre * jnp.exp(-0.5 * pre * pre) * (1.0 / math.sqrt(2.0 * math.pi))
        cot_rows = cot_in[images].reshape(own, width)
        grad_pre = (slope * dot(cot_rows.astype(bf16), wb[...], 1, 1)).astype(bf16)
        gpre[here, :] = grad_pre
        grad_nm = dot(grad_pre, wh[...], 1, 1)
        grad_gm.append(jnp.sum(grad_nm * unit_m, axis=0, keepdims=True))
        grad_hidden = cot_rows + normed_back(grad_nm * gain_mlp[...], unit_m, spread_m)
        grad_h[here, :] = grad_hidden
        grad_low = grad_hidden.astype(bf16)
        gh_low[here, :] = grad_low
        grad_att = dot(grad_low, wo[...], 1, 1).astype(bf16)
        grad_seen = dot(grad_att, wv[...], 1, 1)
        dots_high, dots_low = split_low(-jnp.sum(grad_seen * seen[here, :], axis=1, keepdims=True))
        lse_value = lse[here, 0:1]
        lse_high = lse_value.astype(bf16).astype(f32)
        lse_mid, lse_low = split_low(lse_value - lse_high)
        lane = lanes_of((own, LANES))
        tail = grad_seen[:, main:]
        for k, column in ((5, dots_high), (6, lse_high), (7, lse_mid), (8, lse_low), (9, dots_low)):
            tail = jnp.where(lane == k, column, tail)
        gx_all[g, place.y, place.z] = tail.T[:16].astype(bf16)
        grad_seen = grad_seen[:, :main].astype(bf16)
        for n, i in enumerate(range(g * pair, (g + 1) * pair)):
            g_all[i, place.y, place.z] = grad_seen[n * rows : (n + 1) * rows]
        g_ext[g].begin()
        for i in range(g * pair, (g + 1) * pair):
            g_main[i].begin()

    def small_in(g):
        g_ext[g].end()
        for y in range(2):
            for z in range(depth):
                block = gx_all[g, y, z].astype(f32)
                block = jnp.concatenate([block, jnp.zeros((LANES - 16, LANES), f32)], axis=0).T
                for n in range(pair):
                    g_small[g * pair + n, y, z] = block[n * rows : (n + 1) * rows].astype(bf16)

    stores, totals = [], {}
    owned = micro * rows
    up_store = pltpu.make_async_copy(up_out, updated, store_sem.at[0])

    def summed(k, value):
        sources[k][...] = value.astype(bf16)
        kind, lanes, along = chunks[k]
        totals[k] = Total(
            links, place, along, sources[k], recvs[k], (sum_back, sum_hidden, sum_value, sum_late)[kind], kept_sem.at[k], lanes
        )
        totals[k].send(0)

    def term(k):
        kind, lanes, _ = chunks[k]
        if kind == 0:
            right = cot_in[:, :, lanes].reshape(owned, lanes.stop - lanes.start).astype(bf16)
            summed(k, dot(act[...], right, 0, 0))
        elif kind == 1:
            summed(k, dot(nm[...], gpre[:, lanes], 0, 0))
        else:
            summed(k, dot(gh_low[...], seen[:, lanes].astype(bf16), 0, 0))

    def grad_block(i):
        small = g_small[i].reshape(everyone, LANES).astype(f32)
        lane = lanes_of((everyone, LANES))
        whole = small[:, 6:7] + small[:, 7:8] + small[:, 8:9]
        own_top = jnp.broadcast_to(tops[i][0:1], (LANES, everyone)).T
        scale = jnp.exp(own_top[:, 0:1] - whole)
        dots_high, dots_low = split_low((small[:, 5:6] + small[:, 9:10]) * scale)
        tail = jnp.where(lane < 5, small * scale, 0.0)
        tail = jnp.where(lane == 5, dots_high, tail)
        tail = jnp.where(lane == 7, dots_low, tail)
        value = g_all[i].reshape(everyone, main).astype(f32) * scale
        return jnp.concatenate([value.astype(bf16), tail.astype(bf16)], axis=1)

    def attend_back(i):
        g_main[i].end()
        block = grad_block(i)
        scores[...] = dot(np_all[i], block, 1, 1)
        grad_s[...] = (probs[i].astype(f32) * scores[...]).astype(bf16)
        sums = dot(npt_all[i], grad_s[...], 1, 0)
        for y in range(2):
            here = slice(y * line, (y + 1) * line)
            bb[i, y] = sums[:main, here].astype(bf16)
            be[i, y] = sums[main : main + 8, here]
        begin(b_parts[i][0])
        block_t = block.astype(f32).T[:tall].astype(bf16)
        query_t = query_block(i).astype(f32).T[:tall].astype(bf16)
        grad_np = dot(block_t, probs[i], 1, 1) + dot(query_t, grad_s[...], 1, 1)
        grad_np = jnp.where(rows_of((tall, px_rows)) < feat, grad_np, 0.0)
        spread = px_stats[i, 1:2]
        unit = pixel_unit(i, px_stats[i, 0:1]) * spread
        terms = grad_np * unit
        gp_acc[...] += sum(terms[:, k : k + LANES] for k in range(0, px_rows, LANES))
        grad_np = grad_np * gain_column
        first = jnp.sum(grad_np, axis=0, keepdims=True) * (1.0 / feat)
        second = jnp.sum(grad_np * unit, axis=0, keepdims=True) * (1.0 / feat)
        px_t[i] = (spread * (grad_np - first - unit * second)).astype(bf16)
        stores.append(pltpu.make_async_copy(px_t.at[i], grad_pixels.at[i], store_sem.at[1 + i]))
        stores[-1].start()

    def join_back(i):
        _, owners, waits = b_parts[i]
        links.wait(*waits[0])
        links.wait(*waits[1])
        total = bb[i, place.y].astype(f32) + brecv[i].astype(f32)
        yb[i] = total.T.astype(bf16).reshape(depth, rows, main)
        y_small[8 * i : 8 * i + 8] = be[i, place.y] + berecv[i]
        begin(owners)

    def layer_out(k):
        up_out[...] = up_out[...] + dot(act[...], wb[...], 1, 0).reshape(micro, rows, width)
        up_store.start()

    def queries_back(k):
        ys[...] = y_small[...].astype(bf16)
        begin(y_copies)
        for i in range(micro):
            links.wait(*b_parts[i][2][2])
        links.wait(*y_came)
        lane = lanes_of((rows, LANES))
        smalls = own_lanes(y_small[...] + sum(ysrecv[k].astype(f32) for k in range(depth - 1)))
        parts = []
        for i in range(micro):
            value = yb[i, place.z].astype(f32) + sum(yrecv[i, k].astype(f32) for k in range(depth - 1))
            small = smalls if i == 0 else pltpu.roll(smalls, LANES - 8 * i, 1)
            small = jnp.where(lane < feat - main, small, 0.0)
            parts.append(jnp.concatenate([value.astype(bf16), small.astype(bf16)], axis=1))
        back_low[...] = jnp.concatenate(parts, axis=0)
        for j, (kind, lanes, _) in enumerate(chunks):
            if kind == 3:
                summed(j, dot(nq[...], back_low[:, lanes], 0, 0))

    def queries_in(k):
        back_feats = back_low[...]
        grad_q = (dot(back_feats, wk[...], 1, 0) * scaling).astype(bf16)
        grad_nq = dot(grad_q, wq[...], 1, 1)
        unit_q, spread_q = normed(x_in[...].reshape(owned, width).astype(f32))
        value_tail = pltpu.roll(seen[:, main:], 5, 1).astype(bf16)
        row = rows_of((16, width))
        terms = dot(back_feats[:, main:], nq[...], 0, 0)[:16] + dot(value_tail, gh_low[...], 0, 0)[:16]
        terms = jnp.where(row == 10, sum(grad_gm), terms)
        terms = jnp.where(row == 11, jnp.sum(grad_nq * unit_q, axis=0, keepdims=True), terms)
        grad_gp = jnp.concatenate([gp_acc[...], jnp.zeros((wide - tall, LANES), f32)], axis=0).T
        grad_gp = jnp.sum(grad_gp, axis=0, keepdims=True)
        grad_gp = jnp.concatenate([grad_gp, jnp.zeros((1, width - wide), f32)], axis=1)
        small_sum.begin(jnp.where(row == 12, grad_gp, terms))
        up_store.wait()
        up_out[...] = (grad_h[...] + normed_back(grad_nq * gain_query[...], unit_q, spread_q)).reshape(micro, rows, width)
        last = pltpu.make_async_copy(up_out, grad_latents, store_sem.at[1 + micro])
        last.start()
        stores.append(last)


    small_sum = Everywhere(
        links, place, small_src, small_recv, small_slots, links.group(wq.at[pl.ds(0, (3 + depth - 1) * 16)])
    )

    def small_end(k):
        small_out[...] = small_sum.end()
        stores.append(pltpu.make_async_copy(small_out, sum_small, store_sem.at[2 + micro]))
        stores[-1].start()

    steps = {
        "P": lambda k: pixel_rows(), "p": pixel_norm, "X": lambda k: q_ext.forward(), "q": lambda k: q_main[k].forward(),
        "E": lambda k: q_ext.end(), "A": attend_out, "M": join, "Z": small_out_of, "O": owner_starts, "N": lambda k: next(owners[k], None), "B": term, "U": layer_out,
        "x": lambda k: g_ext[k].forward(), "g": lambda k: g_main[k].forward(), "e": small_in, "a": attend_back, "m": join_back,
        "Q": queries_back, "L": queries_in, "s": lambda k: small_sum.stage(k), "S": small_end,
    }
    for step in ORDER:
        if step[0] == "r":
            totals[int(step[2:])].rs(int(step[1]))
        elif step[0] == "b":
            totals[int(step[2:])].back(int(step[1]))
        else:
            steps[step[0]](int(step[1:]))
    for store in stores:
        store.wait()
    links.drain()


def fused(mesh, pixels, counts, latents, cotangent, w_query, w_key, w_value, w_out, w_hidden, w_back, gain_query, gain_pixel, gain_mlp):
    micro, px_rows, feat = pixels.shape
    rows, width = latents.shape[1:]
    depth = mesh.shape["blk"] // 2
    main = feat // LANES * LANES
    wide = main + LANES
    line = depth * rows
    dims = (micro, rows, depth, px_rows, feat, main, wide, width)
    tall = main + 16
    any_spec = pl.BlockSpec(memory_space=pl.ANY)
    vmem = pl.BlockSpec(memory_space=pltpu.VMEM)
    V = pltpu.VMEM
    chunks = chunks_of(width, main)

    def total_recvs(lanes, along):
        held, height = [], width
        for axis in ("c",) + tuple(along):
            height //= depth if axis == "z" else 2
            held.append(V((depth - 1 if axis == "z" else 1, height, lanes.stop - lanes.start), bf16))
        return held

    reduce_buffers = [
        V((micro, 2, main, line), bf16), V((micro, 2, 8, line), f32), V((micro, main, line), bf16), V((micro, 8, line), f32),
        V((micro, depth, rows, main), bf16), V((micro, depth - 1, rows, main), bf16),
    ]
    arrivals = 2 * (2 * micro + 3) + 3 * 2 * micro + 3 + 8 * len(chunks) + 4
    groups = 4 + 6 + 2 + 2 * len(chunks) + 1
    scratch = (
        [
            V((feat, micro, px_rows), bf16), V((micro, tall, px_rows), bf16), V((micro, 8, px_rows), f32),
            V((micro, px_rows, wide), bf16), V((micro, tall, px_rows), bf16),
            V((px_rows, 2 * line), f32), V((micro, px_rows, 2 * line), bf16), V((px_rows, 2 * line), bf16),
            V(latents.shape, bf16), V(cotangent.shape, f32),
        ]
        + [V((width, width), bf16)] * 4
        + [V((feat, width), bf16)] * 2
        + [V((wide, width), bf16)] * 2
        + [V((micro, 2, depth, rows, main), bf16), V((2, depth, rows, LANES), bf16)]
        + [V((micro, 2, depth, rows, main), bf16), V((2, 2, depth, 16, LANES), bf16)]
        + reduce_buffers * 2
        + [
            V((2, 4 * micro, line), f32), V((2, depth - 1, 4 * micro, line), f32),
            V((8 * micro, line), f32), V((8 * micro, line), bf16), V((depth - 1, 8 * micro, line), bf16),
            V((micro, 8, 2 * line), f32), V((micro * rows, wide), f32), V((micro * rows, LANES), f32),
            V((micro, 2, depth, rows, LANES), bf16), V((micro * rows, wide), bf16),
        ]
        + [V((micro * rows, width), bf16)] * 4
        + [V((micro * rows, width), f32), V((micro * rows, width), bf16), V(latents.shape, f32)]
        + [
            V((3, 16, width), bf16), V((3, 16, width), bf16), V((depth, 16, width), bf16), V((16, width), f32), V((tall, LANES), f32),
        ]
        + [
            [V((width, lanes.stop - lanes.start), bf16) for _, lanes, _ in chunks],
            [total_recvs(lanes, along) for _, lanes, along in chunks],
            pltpu.SemaphoreType.DMA((groups,)), pltpu.SemaphoreType.DMA((arrivals,)),
            pltpu.SemaphoreType.DMA((9,)), pltpu.SemaphoreType.DMA((3 + micro,)), pltpu.SemaphoreType.DMA((len(chunks),)),
        ]
    )
    S = jax.ShapeDtypeStruct
    return pl.pallas_call(
        functools.partial(kernel, dims),
        out_shape=[
            S(latents.shape, f32), S(latents.shape, f32), S((micro, tall, px_rows), bf16),
            S((width, width), bf16), S((width, width), bf16), S((width, main), bf16), S((width, main), bf16), S((16, width), f32),
        ],
        in_specs=[pl.BlockSpec(memory_space=pltpu.SMEM)] + [any_spec] * 9 + [vmem] * 3,
        out_specs=[any_spec] * 8,
        scratch_shapes=scratch,
        compiler_params=pltpu.CompilerParams(collective_id=0, has_side_effects=True, vmem_limit_bytes=63 * 2**20),
        name="layer",
    )(
        counts, jnp.transpose(pixels, (2, 0, 1)), latents, cotangent, w_query, w_out, w_hidden, w_back, w_key, w_value,
        gain_query.reshape(1, -1), gain_pixel, gain_mlp.reshape(1, -1),
    )


def finish(
    dims,
    late, value, small, w_key, w_value, w_query, w_out, hidden, back, px, up, lat,
    out_query, out_key, out_value, out_out, out_hidden, out_back, out_px, out_up, out_lat, out_gq, out_gp, out_gm,
    key_rows, value_rows, late_t, value_t, late_rows,
):
    feat, main, wide, width = dims
    scaling = 1.0 / math.sqrt(width)
    step = out_query.shape[0]
    here = pl.ds(pl.multiple_of(pl.program_id(0) * step, step), step)

    @pl.when(pl.program_id(0) == 0)
    def prepare():
        for raw, dst in ((w_key, key_rows), (w_value, value_rows)):
            dst[:main] = raw[:main]
            last = raw[main:].astype(f32)
            dst[main:] = jnp.concatenate([last, jnp.zeros((wide - feat, width), f32)], axis=0).astype(bf16)
        row = rows_of((16, width))
        rest = jnp.zeros((LANES - 16, width), f32)
        tail = jnp.concatenate([jnp.where(row < 5, small[...], 0.0), rest], axis=0)
        late_rows[:, :main] = late[...]
        late_rows[:, main:] = tail.T.astype(bf16)
        late_t[:main] = late[...].astype(f32).T.astype(bf16)
        late_t[main:] = tail.astype(bf16)
        tail = jnp.concatenate([jnp.where(row < 5, pltpu.roll(small[...], 11, 0), 0.0), rest], axis=0)
        value_t[:main] = value[...].astype(f32).T.astype(bf16)
        value_t[main:] = tail.astype(bf16)
        out_gm[...] = small[10]
        out_gq[...] = small[11]
        out_gp[...] = small[12, :feat]

    out_query[...] = dot(late_rows[here, :], key_rows[...], 1, 0) * scaling
    out_out[...] = dot(value_rows[:, here], value_t[...], 0, 0)
    out_key[...] = (dot(late_t[...], w_query[...], 1, 0) * scaling)[:feat]
    out_value[...] = dot(value_t[...], w_out[...], 1, 1)[:feat]
    out_hidden[...] = hidden[...].astype(f32)
    out_back[...] = back[...].astype(f32)
    out_px[...] = jnp.swapaxes(px[...].astype(f32), 0, 1)
    out_up[...] = up[...]
    out_lat[...] = lat[...]


def fused_body(mesh, *args):
    pixels, latents = args[0], args[2]
    w_query, w_key, w_value, w_out = args[4:8]
    micro, px_rows, feat = pixels.shape
    rows, width = latents.shape[1:]
    main = feat // LANES * LANES
    wide = main + LANES
    up, lat, px, back, hidden, value, late, small = fused(mesh, *args)
    steps = 4
    step, px_step = width // steps, -(-feat // (16 * steps)) * 16
    whole = lambda *shape: pl.BlockSpec(shape, lambda k: (0,) * len(shape))
    by_row = pl.BlockSpec((step, width), lambda k: (k, 0))
    by_column = lambda height: pl.BlockSpec((height, step), lambda k: (0, k))
    lat_block = pl.BlockSpec((micro, rows // steps, width), lambda k: (0, k, 0))
    S = jax.ShapeDtypeStruct
    out = pl.pallas_call(
        functools.partial(finish, (feat, main, wide, width)),
        grid=(steps,),
        in_specs=[
            whole(width, main), whole(width, main), whole(16, width), whole(feat, width), whole(feat, width), by_column(width), by_row,
            by_row, by_row, pl.BlockSpec((micro, px_step, px_rows), lambda k: (0, k, 0)), lat_block, lat_block,
        ],
        out_specs=[
            by_row, by_column(feat), by_column(feat), by_row, by_row, by_row,
            pl.BlockSpec((px_step, micro, px_rows), lambda k: (k, 0, 0)), lat_block, lat_block,
            whole(width), whole(feat), whole(width),
        ],
        out_shape=[
            S((width, width), f32), S((feat, width), f32), S((feat, width), f32), S((width, width), f32),
            S((width, width), f32), S((width, width), f32), S((feat, micro, px_rows), f32),
            S(latents.shape, f32), S(latents.shape, f32), S((width,), f32), S((feat,), f32), S((width,), f32),
        ],
        scratch_shapes=[pltpu.VMEM((wide, width), bf16)] * 4 + [pltpu.VMEM((width, wide), bf16)],
        compiler_params=pltpu.CompilerParams(vmem_limit_bytes=60 * 2**20),
        name="finish",
    )(late, value, small, w_key, w_value, w_query, w_out, hidden, back, px, up, lat)
    g_query, g_key, g_value, g_out, g_hidden, g_back, g_px, g_up, g_lat, g_gq, g_gp, g_gm = out
    g_px = jnp.transpose(g_px, (1, 2, 0))
    return g_up, g_lat, g_px, g_query, g_key, g_value, g_out, g_hidden, g_back, g_gq, g_gp, g_gm


def layer_norm(values, gain_vec):
    centered = values - jnp.mean(values, axis=-1, keepdims=True)
    variance = jnp.mean(centered * centered, axis=-1, keepdims=True)
    return centered * lax.rsqrt(variance + EPSILON) * gain_vec


def gelu_exact(values):
    return jax.nn.gelu(values, approximate=False)


def low(values):
    return values.astype(jnp.bfloat16)


def product(left_mat, right_mat):
    return jnp.dot(left_mat, right_mat, preferred_element_type=jnp.float32)


def product_tn(left_mat, right_mat):
    return lax.dot_general(
        left_mat, right_mat, (((0,), (0,)), ((), ())), preferred_element_type=jnp.float32
    )


def product_nt(left_mat, right_mat):
    return lax.dot_general(
        left_mat, right_mat, (((1,), (1,)), ((), ())), preferred_element_type=jnp.float32
    )


def each(spec, left, right):
    return jnp.einsum(spec, left, right, preferred_element_type=jnp.float32)


def to_owner(x, peers):
    micro, rows = x.shape[:2]
    blocks = jnp.moveaxis(x.reshape(micro, peers, rows // peers, *x.shape[2:]), 1, 0)
    return lax.all_to_all(blocks, "blk", 0, 0, tiled=True)


def plain_body(pixels, counts, latents, cotangent, w_query, w_key, w_value, w_out, w_hidden, w_back, gain_query, gain_pixel, gain_mlp):
    micro, pixel_rows, features = pixels.shape
    lat_rows, width = latents.shape[1:]
    peers = lax.axis_size("blk")
    scaling = 1.0 / math.sqrt(width)
    rows = micro * lat_rows
    positions = lax.axis_index("blk") * pixel_rows + jnp.arange(pixel_rows, dtype=jnp.int32)
    valid = positions[None, :] < counts[:, None]

    latent_in = latents.reshape(rows, width).astype(jnp.float32)
    normed_qf, query_pull = jax.vjp(layer_norm, latent_in, gain_query)
    normed_q = low(normed_qf)
    queries = low(product(normed_q, w_query))
    query_feats = low(product_nt(queries, w_key) * scaling).reshape(micro, lat_rows, features)
    all_query = lax.all_gather(query_feats, "blk", axis=1, tiled=True)
    normed_pf, pixel_pull = jax.vjp(layer_norm, pixels.astype(jnp.float32), gain_pixel)
    normed_p = low(normed_pf)
    scores = each("mqf,mpf->mqp", all_query, normed_p)
    scores = jnp.where(valid[:, None, :], scores, MASKED)
    highest = jnp.max(scores, axis=2)
    unscaled = jnp.exp(scores - highest[..., None])
    total = jnp.sum(unscaled, axis=2)
    sums = low(each("mqp,mpf->mqf", low(unscaled), normed_p))
    parts = to_owner(sums, peers).astype(jnp.float32)
    stats = to_owner(jnp.stack([highest, total], axis=2), peers)
    top = jnp.max(stats[..., 0], axis=0)
    scale = jnp.exp(stats[..., 0] - top)
    denom = jnp.sum(stats[..., 1] * scale, axis=0)
    lse = top + jnp.log(denom)
    seen = (jnp.sum(parts * scale[..., None], axis=0) / denom[..., None]).reshape(rows, features)
    seen_b = low(seen)
    attended_b = low(product(seen_b, w_value))
    hidden_in = latent_in + product(attended_b, w_out)
    normed_mf, mlp_pull = jax.vjp(layer_norm, hidden_in, gain_mlp)
    normed_m = low(normed_mf)
    pre_act = product(normed_m, w_hidden)
    activated_f, gelu_pull = jax.vjp(gelu_exact, pre_act)
    activated = low(activated_f)
    updated = hidden_in + product(activated, w_back)
    cot = cotangent.reshape(rows, width)
    cot_b = low(cot)
    grad_back = product_tn(activated, cot_b)
    (grad_pre,) = gelu_pull(product_nt(cot_b, w_back))
    grad_pre_b = low(grad_pre)
    grad_hidden = product_tn(normed_m, grad_pre_b)
    grad_h_ln, grad_gm = mlp_pull(product_nt(grad_pre_b, w_hidden))
    grad_h = cot + grad_h_ln
    grad_h_b = low(grad_h)
    grad_att = low(product_nt(grad_h_b, w_out))
    grad_seen = product_nt(grad_att, w_value)
    dots = jnp.sum(grad_seen * seen, axis=1).reshape(micro, lat_rows)
    value_side = product_tn(seen_b, grad_h_b)
    all_grad = lax.all_gather(low(grad_seen).reshape(micro, lat_rows, features), "blk", axis=1, tiled=True)
    all_stat = lax.all_gather(jnp.stack([lse, dots], axis=2), "blk", axis=1, tiled=True)
    probs = unscaled * jnp.exp(highest - all_stat[..., 0])[..., None]
    grad_probs = each("mqf,mpf->mqp", all_grad, normed_p)
    grad_scores = low(probs * (grad_probs - all_stat[..., 1][..., None]))
    back_sums = low(each("mqp,mpf->mqf", grad_scores, normed_p))
    grad_np = each("mqp,mqf->mpf", low(probs), all_grad) + each("mqp,mqf->mpf", grad_scores, all_query)
    grad_pixels, grad_gp = pixel_pull(grad_np)
    back_feats = jnp.sum(to_owner(back_sums, peers).astype(jnp.float32), axis=0).reshape(rows, features)
    back_b = low(back_feats)
    grad_q = low(product(back_b, w_key) * scaling)
    grad_lat_q, grad_gq = query_pull(product_nt(grad_q, w_query))
    grad_latents = grad_h + grad_lat_q
    query_side = product_tn(normed_q, back_b)
    query_side, value_side, grad_hidden, grad_back, grad_gq, grad_gp, grad_gm = lax.psum(
        (query_side, value_side, grad_hidden, grad_back, grad_gq, grad_gp, grad_gm), ("img", "blk")
    )
    query_b, value_b = low(query_side * scaling), low(value_side)
    return (
        updated.reshape(micro, lat_rows, width),
        grad_latents.reshape(micro, lat_rows, width),
        grad_pixels,
        product(query_b, w_key),
        product_tn(query_b, w_query),
        product_nt(value_b, w_out),
        product_tn(w_value, value_b),
        grad_hidden,
        grad_back,
        grad_gq,
        grad_gp,
        grad_gm,
    )


def body(mesh, *args):
    pixels, latents = args[0], args[2]
    rows, width = latents.shape[1:]
    fits = pixels.shape[0] // 2 * rows == LANES and rows % 16 == 0 and width % (16 * mesh.size) == 0
    fits = fits and mesh.shape["img"] == 4 and mesh.shape["blk"] % 2 == 0
    return fused_body(mesh, *args) if fits else plain_body(*args)


def solution(mesh):
    spread, same = P("img", "blk", None), P()
    return jax.shard_map(
        functools.partial(body, mesh),
        mesh=mesh,
        in_specs=(spread, P("img"), spread, spread) + (same,) * 9,
        out_specs=(spread,) * 3 + (same,) * 9,
        check_vma=False,
    )
```

```python
import functools
import math

import jax
import jax.numpy as jnp
from jax import lax
from jax.experimental import pallas as pl
from jax.experimental.pallas import tpu as pltpu
from jax.sharding import PartitionSpec as P

EPSILON = 1e-05
MASKED = -1e30
LANES = 128
MESH = pl.DeviceIdType.MESH
bf16, f32 = jnp.bfloat16, jnp.float32


def dot(left, right, left_dim, right_dim):
    return lax.dot_general(left, right, (((left_dim,), (right_dim,)), ((), ())), preferred_element_type=f32)


def lanes_of(shape):
    return lax.broadcasted_iota(jnp.int32, shape, 1)


def rows_of(shape):
    return lax.broadcasted_iota(jnp.int32, shape, 0)


def normed(values):
    part = 1.0 / values.shape[1]
    centered = values - jnp.sum(values, axis=1, keepdims=True) * part
    spread = lax.rsqrt(jnp.sum(centered * centered, axis=1, keepdims=True) * part + EPSILON)
    return centered * spread, spread


def normed_back(grad, unit, spread):
    part = 1.0 / grad.shape[1]
    first = jnp.sum(grad, axis=1, keepdims=True) * part
    second = jnp.sum(grad * unit, axis=1, keepdims=True) * part
    return spread * (grad - first - unit * second)


def split_low(values):
    high = values.astype(bf16).astype(f32)
    return high, (values - high).astype(bf16).astype(f32)


ORDER = (
    "P0", "p1", "p2", "p3", "p0", "X0", "q0", "E0", "q1", "A0", "q2", "A1", "q3", "M0", "A2", "M1", "Z0", "A3", "M2", "O0", "M3",
    "Z1", "N0", "O1", "B1", "x0", "N1", "U0", "B3", "B0", "e0", "g0", "B2", "g1", "B4", "r01", "x1", "r03", "g2", "a0", "r00",
    "g3", "r02", "a1", "e1", "r04", "r11", "a2", "m0", "a3", "r13", "m1", "r21", "m2", "r10", "m3", "r23", "r12", "r31", "r14",
    "Q0", "r20", "L0", "r22", "r33", "r24", "r05", "b01", "s0", "r30", "r15", "r32", "b03", "b11", "s1", "r25", "r34", "b02",
    "b00", "b13", "r35", "b12", "b04", "b05", "b10", "b21", "s2", "b14", "b23", "b31", "b15", "b20", "b24", "b33", "b22", "b25",
    "b30", "S0", "b34", "b32", "b35",
)


def chunks_of(width, main):
    half = width // 2
    return (
        (0, slice(0, half), ("xyz", "zxy")),
        (0, slice(half, width), ("xzy", "zxy")),
        (1, slice(0, half), ("xyz", "yxz")),
        (1, slice(half, width), ("xyz", "zyx")),
        (2, slice(0, main), ("xyz", "zyx")),
        (3, slice(0, main), ("xyz", "zxy")),
    )


class Links:
    def __init__(self, send_sem, recv_sem):
        self.send_sem, self.recv_sem, self.arrivals, self.groups = send_sem, recv_sem, 0, []

    def group(self, size):
        self.groups.append(size)
        return len(self.groups) - 1

    def arrival(self):
        self.arrivals += 1
        return self.arrivals - 1

    def remote(self, src, dst, device, group, arrival):
        return pltpu.make_async_remote_copy(
            src_ref=src, dst_ref=dst, send_sem=self.send_sem.at[group], recv_sem=self.recv_sem.at[arrival],
            device_id=device, device_id_type=MESH,
        )

    def wait(self, size, arrival):
        pltpu.make_async_copy(size, size, self.recv_sem.at[arrival]).wait()

    def drain(self):
        for group, size in enumerate(self.groups):
            pltpu.make_async_copy(size, size, self.send_sem.at[group]).wait()


class Place:
    def __init__(self, depth):
        img, blk = lax.axis_index("img"), lax.axis_index("blk")
        self.x, self.c = lax.div(img, 2), lax.rem(img, 2)
        self.z, self.y = lax.div(blk, 2), lax.rem(blk, 2)
        self.core_peer = (self.x * 2 + 1 - self.c, blk)
        self.x_peer = ((1 - self.x) * 2 + self.c, blk)
        self.y_peer = (img, self.z * 2 + 1 - self.y)
        self.z_index = [lax.rem(self.z + k, depth) for k in range(1, depth)]
        self.z_peers = [(img, other * 2 + self.y) for other in self.z_index]
        self.z_sources = [lax.rem(self.z + depth - k, depth) for k in range(1, depth)]

    def all(self):
        return [self.core_peer, self.x_peer, self.y_peer] + self.z_peers


class Gather:
    def __init__(self, links, place, ref, group, size):
        own = ref.at[place.y, place.z]
        self.links, self.size, self.line = links, size, ref.at[0]
        self.came_z, self.came_y = links.arrival(), links.arrival()
        self.along = [links.remote(own, own, peer, group, self.came_z) for peer in place.z_peers]
        self.across = []
        for source in [place.z] + place.z_sources:
            block = ref.at[place.y, source]
            self.across.append(links.remote(block, block, place.y_peer, group, self.came_y))

    def begin(self):
        for copy in self.along + self.across[:1]:
            copy.start()

    def forward(self):
        self.links.wait(self.size, self.came_z)
        for copy in self.across[1:]:
            copy.start()

    def end(self):
        self.links.wait(self.line, self.came_y)


class Everywhere:
    def __init__(self, links, place, src, recv, slots, group):
        self.links, self.src, self.recv, self.slots, self.z = links, src, recv, slots, place.z
        peers = (place.core_peer, place.x_peer, place.y_peer)
        self.came = [links.arrival() for _ in range(4)]
        self.swaps = [links.remote(src.at[k], recv.at[k], peer, group, self.came[k]) for k, peer in enumerate(peers)]
        mine = slots.at[place.z]
        self.along = [links.remote(mine, mine, peer, group, self.came[3]) for peer in place.z_peers]

    def begin(self, value):
        self.src[0] = value.astype(bf16)
        self.swaps[0].start()

    def stage(self, k):
        self.links.wait(self.recv.at[k], self.came[k])
        total = (self.src[k].astype(f32) + self.recv[k].astype(f32)).astype(bf16)
        if k < 2:
            self.src[k + 1] = total
            self.swaps[k + 1].start()
        else:
            self.slots[self.z] = total
            for copy in self.along:
                copy.start()

    def end(self):
        count = len(self.along)
        self.links.wait(self.slots.at[pl.ds(0, count)], self.came[3])
        return sum(self.slots[k].astype(f32) for k in range(count + 1))


class Total:
    def __init__(self, links, place, orders, src, recv, out, local_sem, lanes):
        self.links, self.src, self.recv = links, src, recv
        there_order, back_order = orders
        depth = len(place.z_peers) + 1
        axes = {
            "c": ([place.core_peer], [1 - place.c], place.c, 2), "x": ([place.x_peer], [1 - place.x], place.x, 2),
            "y": ([place.y_peer], [1 - place.y], place.y, 2), "z": (place.z_peers, place.z_index, place.z, depth),
        }
        last = src.shape[0] // (8 * depth)
        everything = src.at[pl.ds(0, src.shape[0] - last)]
        there, back = links.group(everything), links.group(everything)
        offset, height = 0, src.shape[0]
        self.there, self.spans, heights = [], [], {}
        for k, axis in enumerate("c" + there_order):
            peers, indices, own, count = axes[axis]
            height //= count
            heights[axis] = height
            came = links.arrival()
            copies = []
            for n, (peer, index) in enumerate(zip(peers, indices)):
                start = pl.multiple_of(offset + index * height, height)
                copies.append(links.remote(src.at[pl.ds(start, height)], recv[k].at[n], peer, there, came))
            offset = pl.multiple_of(offset + own * height, height)
            self.there.append((copies, came))
            self.spans.append((offset, height))
        self.kept = pltpu.make_async_copy(src.at[pl.ds(offset, height)], out.at[pl.ds(offset, height), lanes], local_sem)
        self.backs, held, source = [], [(offset, height)], src
        for axis in back_order + "c":
            peers, _, own, count = axes[axis]
            came, step = links.arrival(), heights[axis]
            copies = []
            for peer in peers:
                for start, size in held:
                    region = out.at[pl.ds(start, size), lanes]
                    first = src.at[pl.ds(start, size)] if source is src else region
                    copies.append(links.remote(first, region, peer, back, came))
            size = src.at[pl.ds(0, len(peers) * sum(size for _, size in held))]
            self.backs.append((copies, size, came))
            source = out
            if held[0][1] == step:
                held = [(pl.multiple_of(start - own * step, step), size * count) for start, size in held]
            else:
                align = min(step, held[0][1])
                held = [(pl.multiple_of(start + (v - own) * step, align), size) for start, size in held for v in range(count)]

    def send(self, stage):
        for copy in self.there[stage][0]:
            copy.start()

    def rs(self, stage):
        held = self.recv[stage]
        self.links.wait(held, self.there[stage][1])
        start, size = self.spans[stage]
        step = min(size, 64)

        def some(k):
            here = pl.ds(pl.multiple_of(start + k * step, step), step)
            block = pl.ds(pl.multiple_of(k * step, step), step)
            total = self.src[here, :].astype(f32)
            for n in range(held.shape[0]):
                total = total + held[n, block, :].astype(f32)
            self.src[here, :] = total.astype(bf16)

        pl.loop(0, size // step)(some)
        if stage < 3:
            self.send(stage + 1)
        else:
            self.kept.start()
            for copy in self.backs[0][0]:
                copy.start()

    def back(self, stage):
        _, size, came = self.backs[stage]
        self.links.wait(size, came)
        if stage == 0:
            self.kept.wait()
        if stage < 3:
            for copy in self.backs[stage + 1][0]:
                copy.start()


def kernel(
    dims,
    counts, pixels, latents, cotangent, w_query, w_out, w_hidden, w_back, w_key, w_value, gain_query, gain_pixel, gain_mlp,
    updated, grad_latents, grad_pixels, sum_back, sum_hidden, sum_value, sum_late, sum_small,
    px, px_t, px_stats, np_all, npt_all, scores, probs, grad_s, x_in, cot_in, wq, wo, wh, wb, wk_in, wv_in, wk, wv,
    q_all, qx_all, g_all, gx_all,
    ob, oe, orecv, oerecv, zb, zrecv, bb, be, brecv, berecv, yb, yrecv, zs, zsrecv, y_small, ys, ysrecv,
    tops, seen, lse, g_small, back_low, nq, nm, act, gpre, grad_h, gh_low, up_out, small_src, small_recv, small_slots, small_out, gp_acc,
    sources, recvs, send_sem, recv_sem, load_sem, store_sem, kept_sem,
):
    micro, rows, depth, px_rows, feat, main, wide, width = dims
    pair = micro // 2
    chunks = chunks_of(width, main)
    line = depth * rows
    everyone = 2 * line
    scaling = 1.0 / math.sqrt(width)
    links, place = Links(send_sem, recv_sem), Place(depth)
    loads = {}

    def load(name, src, dst):
        loads[name] = pltpu.make_async_copy(src, dst, load_sem.at[len(loads)])
        return loads[name]

    load("x", latents, x_in).start()
    load("wq", w_query, wq).start()
    load("wk", w_key, wk_in).start()
    barrier = pltpu.get_barrier_semaphore()
    for peer in place.all():
        pl.semaphore_signal(barrier, inc=1, device_id=peer, device_id_type=MESH)
    gp_acc[...] = jnp.zeros_like(gp_acc)

    def pad_rows(raw, dst):
        dst[:main] = raw[:main]
        last = raw[main:].astype(f32)
        dst[main:] = jnp.concatenate([last, jnp.zeros((wide - feat, width), f32)], axis=0).astype(bf16)

    loads["x"].wait()
    unit_q, _ = normed(x_in[...].reshape(micro * rows, width).astype(f32))
    nq[...] = (unit_q * gain_query[...]).astype(bf16)
    loads["wq"].wait()
    loads["wk"].wait()
    load("px", pixels, px).start()
    for name, src, dst in (("wv", w_value, wv_in), ("wo", w_out, wo), ("wh", w_hidden, wh), ("wb", w_back, wb), ("cot", cotangent, cot_in)):
        load(name, src, dst).start()
    pad_rows(wk_in, wk)
    queries = dot(nq[...], wq[...], 1, 0).astype(bf16)
    feats = dot(queries, wk[...], 1, 1) * scaling
    small = jnp.where(lanes_of((rows, LANES)) % 16 == 6, 1.0, 0.0)
    for i in range(micro):
        here = slice(i * rows, (i + 1) * rows)
        q_all[i, place.y, place.z] = feats[here, :main].astype(bf16)
        tail = feats[here, main:]
        small = small + (tail if i == 0 else pltpu.roll(tail, 16 * i, 1))
    qx_all[place.y, place.z] = small.astype(bf16)
    pl.semaphore_wait(barrier, len(place.all()))

    def gathers(main_ref, ext_refs, ext_size):
        blocks = micro * (2 * depth - 1)
        group = links.group(wq.at[pl.ds(0, blocks * rows * main // width)])
        mains = [Gather(links, place, main_ref.at[i], group, zrecv.at[i]) for i in range(micro)]
        group = links.group(lse.at[pl.ds(0, len(ext_refs) * (2 * depth - 1) * ext_size.shape[0] // (depth - 1))])
        return mains, [Gather(links, place, ref, group, ext_size) for ref in ext_refs]

    q_main, (q_ext,) = gathers(q_all, [qx_all], lse.at[pl.ds(0, (depth - 1) * rows // 2)])
    g_main, g_ext = gathers(g_all, [gx_all.at[g] for g in range(2)], lse.at[pl.ds(0, (depth - 1) * 8)])
    q_ext.begin()
    for gather in q_main:
        gather.begin()

    first_pixel = lax.axis_index("blk") * px_rows
    tall = main + 16
    gain_column = jnp.broadcast_to(gain_pixel[...].reshape(1, feat), (LANES, feat))
    gain_column = jnp.concatenate([gain_column, jnp.zeros((LANES, wide - feat), f32)], axis=1).T[:tall, 0:1]

    def pixel_rows():
        loads["px"].wait()
        for first in range(0, feat, 16):
            last = min(first + 16, feat)
            block = px[first:last].astype(f32)
            if last - first < 16:
                block = jnp.concatenate([block, jnp.zeros((16 - last + first,) + block.shape[1:], f32)], axis=0)
            block = jnp.swapaxes(block, 0, 1)
            for i in range(micro):
                px_t[i, first : first + 16] = block[i].astype(bf16)

    def pixel_unit(i, mean):
        centered = px_t[i].astype(f32) - mean
        return jnp.where(rows_of((tall, px_rows)) < feat, centered, 0.0)

    def pixel_norm(i):
        mean = jnp.sum(px_t[i].astype(f32), axis=0, keepdims=True) * (1.0 / feat)
        centered = pixel_unit(i, mean)
        spread = lax.rsqrt(jnp.sum(centered * centered, axis=0, keepdims=True) * (1.0 / feat) + EPSILON)
        px_stats[i, 0:1], px_stats[i, 1:2] = mean, spread
        row = rows_of((tall, px_rows))
        value = centered * spread * gain_column
        value = jnp.where((row == main + 5) | (row == main + 7), 1.0, value)
        npt_all[i] = value.astype(bf16)
        masked = first_pixel + lanes_of((tall, px_rows)) >= counts[i]
        value = jnp.where((row == main + 6) & masked, MASKED, value)
        np_all[i] = jnp.concatenate([value, jnp.zeros((wide - tall, px_rows), f32)], axis=0).T.astype(bf16)

    def query_block(i):
        small = qx_all[...].reshape(everyone, LANES).astype(f32)
        if i:
            small = pltpu.roll(small, LANES - 16 * i, 1)
        small = jnp.where(lanes_of((everyone, LANES)) < 16, small, 0.0)
        return jnp.concatenate([q_all[i].reshape(everyone, main), small.astype(bf16)], axis=1)

    def attend(i):
        q_main[i].end()
        scores[...] = dot(np_all[i], query_block(i), 1, 1)
        top = jnp.max(scores[...], axis=0, keepdims=True)
        tops[i] = jnp.broadcast_to(top, (8, everyone))
        probs[i] = jnp.exp(scores[...] - top).astype(bf16)
        sums = dot(npt_all[i], probs[i], 1, 0)
        small = jnp.where(rows_of((8, everyone)) == 6, top, sums[main : main + 8])
        for y in range(2):
            here = slice(y * line, (y + 1) * line)
            ob[i, y] = sums[:main, here].astype(bf16)
            oe[i, y] = small[:, here]

    def exchanges(sums, small, held, small_held, parts, parts_held):
        main_group = links.group(wq.at[pl.ds(0, micro * line * main // width)])
        small_group = links.group(wq.at[pl.ds(0, micro * 2 * 8 * line // width)])
        owner_group = links.group(wq.at[pl.ds(0, micro * (depth - 1) * rows * main // width)])
        out = []
        for i in range(micro):
            came, small_came, owner_came = links.arrival(), links.arrival(), links.arrival()
            swaps = [
                links.remote(sums.at[i, 1 - place.y], held.at[i], place.y_peer, main_group, came),
                links.remote(small.at[i, 1 - place.y], small_held.at[i], place.y_peer, small_group, small_came),
            ]
            owners = [
                links.remote(parts.at[i, other], parts_held.at[i, k], peer, owner_group, owner_came)
                for k, (peer, other) in enumerate(zip(place.z_peers, place.z_index))
            ]
            out.append((swaps, owners, ((held.at[i], came), (small_held.at[i], small_came), (parts_held.at[i], owner_came))))
        return out

    def begin(copies):
        for copy in copies:
            copy.start()

    q_parts = exchanges(ob, oe, orecv, oerecv, zb, zrecv)
    b_parts = exchanges(bb, be, brecv, berecv, yb, yrecv)

    def own_lanes(part):
        part = pltpu.roll(part, lax.rem((depth - place.z) * rows, line), 1)[:, :LANES]
        return jnp.concatenate([part, jnp.zeros((LANES - part.shape[0], LANES), f32)], axis=0).T[:rows]

    def join(i):
        _, owners, waits = q_parts[i]
        links.wait(*waits[0])
        links.wait(*waits[1])
        mine, theirs = oe[i, place.y], oerecv[i]
        top_m, top_t = mine[6:7], theirs[6:7]
        top = jnp.maximum(top_m, top_t)
        scale_m, scale_t = jnp.exp(top_m - top), jnp.exp(top_t - top)
        total = ob[i, place.y].astype(f32) * scale_m + orecv[i].astype(f32) * scale_t
        zb[i] = total.T.astype(bf16).reshape(depth, rows, main)
        small = mine * scale_m + theirs * scale_t
        zs[i // pair, 8 * (i % pair) : 8 * (i % pair) + 8] = jnp.where(rows_of((8, line)) == 6, top, small)
        begin(owners)

    def attend_out(i):
        attend(i)
        begin(q_parts[i][0])

    def to_peers(src, dst, group):
        came = links.arrival()
        return [links.remote(src, dst.at[k], peer, group, came) for k, peer in enumerate(place.z_peers)], (dst, came)

    z_group = links.group(wq.at[pl.ds(0, 2 * (depth - 1) * 2 * 8 * pair * line // width)])
    z_small = [to_peers(zs.at[g], zsrecv.at[g], z_group) for g in range(2)]
    y_copies, y_came = to_peers(ys, ysrecv, links.group(lse.at[pl.ds(0, (depth - 1) * 4 * micro * line // LANES)]))

    def small_out_of(g):
        begin(z_small[g][0])

    grad_gm, owners = [], {}

    def owner_starts(g):
        owners[g] = owner(g)
        next(owners[g])

    def owner(g):
        images = range(g * pair, (g + 1) * pair)
        links.wait(*z_small[g][1])
        for i in images:
            links.wait(*q_parts[i][2][2])
        smalls = [own_lanes(zs[g])] + [own_lanes(zsrecv[g, k]) for k in range(depth - 1)]
        lane = lanes_of((rows, LANES))
        for i in images:
            mains = [zb[i, place.z]] + [zrecv[i, k] for k in range(depth - 1)]
            base = 8 * (i % pair)
            highs = [small[:, base + 6 : base + 7] for small in smalls]
            top = functools.reduce(jnp.maximum, highs)
            scales = [jnp.exp(high - top) for high in highs]
            total = sum(small * scale for small, scale in zip(smalls, scales))
            denom = total[:, base + 5 : base + 6]
            here = slice(i * rows, (i + 1) * rows)
            seen[here, :main] = sum(value.astype(f32) * scale for value, scale in zip(mains, scales)) / denom
            if base:
                total = pltpu.roll(total, LANES - base, 1)
            seen[here, main:] = jnp.where(lane < feat - main, total / denom, 0.0)
            lse[here, :] = jnp.broadcast_to(top + jnp.log(denom), (rows, LANES))
        if g == 0:
            for name in ("wv", "wo", "wh", "wb", "cot"):
                loads[name].wait()
            pad_rows(wv_in, wv)
        own = pair * rows
        here, images = slice(g * own, (g + 1) * own), slice(g * pair, (g + 1) * pair)
        attended = dot(seen[here, :].astype(bf16), wv[...], 1, 0).astype(bf16)
        hidden_in = x_in[images].reshape(own, width).astype(f32) + dot(attended, wo[...], 1, 0)
        up_out[images] = hidden_in.reshape(pair, rows, width)
        unit_m, spread_m = normed(hidden_in)
        normed_m = (unit_m * gain_mlp[...]).astype(bf16)
        nm[here, :] = normed_m
        pre = dot(normed_m, wh[...], 1, 0)
        cumulative = 0.5 * (1.0 + lax.erf(pre * math.sqrt(0.5)))
        act[here, :] = (pre * cumulative).astype(bf16)
        yield
        slope = cumulative + pre * jnp.exp(-0.5 * pre * pre) * (1.0 / math.sqrt(2.0 * math.pi))
        cot_rows = cot_in[images].reshape(own, width)
        grad_pre = (slope * dot(cot_rows.astype(bf16), wb[...], 1, 1)).astype(bf16)
        gpre[here, :] = grad_pre
        grad_nm = dot(grad_pre, wh[...], 1, 1)
        grad_gm.append(jnp.sum(grad_nm * unit_m, axis=0, keepdims=True))
        grad_hidden = cot_rows + normed_back(grad_nm * gain_mlp[...], unit_m, spread_m)
        grad_h[here, :] = grad_hidden
        grad_low = grad_hidden.astype(bf16)
        gh_low[here, :] = grad_low
        grad_att = dot(grad_low, wo[...], 1, 1).astype(bf16)
        grad_seen = dot(grad_att, wv[...], 1, 1)
        dots_high, dots_low = split_low(-jnp.sum(grad_seen * seen[here, :], axis=1, keepdims=True))
        lse_value = lse[here, 0:1]
        lse_high = lse_value.astype(bf16).astype(f32)
        lse_mid, lse_low = split_low(lse_value - lse_high)
        lane = lanes_of((own, LANES))
        tail = grad_seen[:, main:]
        for k, column in ((5, dots_high), (6, lse_high), (7, lse_mid), (8, lse_low), (9, dots_low)):
            tail = jnp.where(lane == k, column, tail)
        gx_all[g, place.y, place.z] = tail.T[:16].astype(bf16)
        grad_seen = grad_seen[:, :main].astype(bf16)
        for n, i in enumerate(range(g * pair, (g + 1) * pair)):
            g_all[i, place.y, place.z] = grad_seen[n * rows : (n + 1) * rows]
        g_ext[g].begin()
        for i in range(g * pair, (g + 1) * pair):
            g_main[i].begin()

    def small_in(g):
        g_ext[g].end()
        for y in range(2):
            for z in range(depth):
                block = gx_all[g, y, z].astype(f32)
                block = jnp.concatenate([block, jnp.zeros((LANES - 16, LANES), f32)], axis=0).T
                for n in range(pair):
                    g_small[g * pair + n, y, z] = block[n * rows : (n + 1) * rows].astype(bf16)

    stores, totals = [], {}
    owned = micro * rows
    up_store = pltpu.make_async_copy(up_out, updated, store_sem.at[0])

    def summed(k, value):
        sources[k][...] = value.astype(bf16)
        kind, lanes, orders = chunks[k]
        totals[k] = Total(
            links, place, orders, sources[k], recvs[k], (sum_back, sum_hidden, sum_value, sum_late)[kind], kept_sem.at[k], lanes
        )
        totals[k].send(0)

    def term(k):
        kind, lanes, _ = chunks[k]
        if kind == 0:
            right = cot_in[:, :, lanes].reshape(owned, lanes.stop - lanes.start).astype(bf16)
            summed(k, dot(act[...], right, 0, 0))
        elif kind == 1:
            summed(k, dot(nm[...], gpre[:, lanes], 0, 0))
        else:
            summed(k, dot(gh_low[...], seen[:, lanes].astype(bf16), 0, 0))

    def grad_block(i):
        small = g_small[i].reshape(everyone, LANES).astype(f32)
        lane = lanes_of((everyone, LANES))
        whole = small[:, 6:7] + small[:, 7:8] + small[:, 8:9]
        own_top = jnp.broadcast_to(tops[i][0:1], (LANES, everyone)).T
        scale = jnp.exp(own_top[:, 0:1] - whole)
        dots_high, dots_low = split_low((small[:, 5:6] + small[:, 9:10]) * scale)
        tail = jnp.where(lane < 5, small * scale, 0.0)
        tail = jnp.where(lane == 5, dots_high, tail)
        tail = jnp.where(lane == 7, dots_low, tail)
        value = g_all[i].reshape(everyone, main).astype(f32) * scale
        return jnp.concatenate([value.astype(bf16), tail.astype(bf16)], axis=1)

    def attend_back(i):
        g_main[i].end()
        block = grad_block(i)
        scores[...] = dot(np_all[i], block, 1, 1)
        grad_s[...] = (probs[i].astype(f32) * scores[...]).astype(bf16)
        sums = dot(npt_all[i], grad_s[...], 1, 0)
        for y in range(2):
            here = slice(y * line, (y + 1) * line)
            bb[i, y] = sums[:main, here].astype(bf16)
            be[i, y] = sums[main : main + 8, here]
        begin(b_parts[i][0])
        block_t = block.astype(f32).T[:tall].astype(bf16)
        query_t = query_block(i).astype(f32).T[:tall].astype(bf16)
        grad_np = dot(block_t, probs[i], 1, 1) + dot(query_t, grad_s[...], 1, 1)
        grad_np = jnp.where(rows_of((tall, px_rows)) < feat, grad_np, 0.0)
        spread = px_stats[i, 1:2]
        unit = pixel_unit(i, px_stats[i, 0:1]) * spread
        terms = grad_np * unit
        gp_acc[...] += sum(terms[:, k : k + LANES] for k in range(0, px_rows, LANES))
        grad_np = grad_np * gain_column
        first = jnp.sum(grad_np, axis=0, keepdims=True) * (1.0 / feat)
        second = jnp.sum(grad_np * unit, axis=0, keepdims=True) * (1.0 / feat)
        px_t[i] = (spread * (grad_np - first - unit * second)).astype(bf16)
        stores.append(pltpu.make_async_copy(px_t.at[i], grad_pixels.at[i], store_sem.at[1 + i]))
        stores[-1].start()

    def join_back(i):
        _, owners, waits = b_parts[i]
        links.wait(*waits[0])
        links.wait(*waits[1])
        total = bb[i, place.y].astype(f32) + brecv[i].astype(f32)
        yb[i] = total.T.astype(bf16).reshape(depth, rows, main)
        y_small[8 * i : 8 * i + 8] = be[i, place.y] + berecv[i]
        begin(owners)

    def layer_out(k):
        up_out[...] = up_out[...] + dot(act[...], wb[...], 1, 0).reshape(micro, rows, width)
        up_store.start()

    def queries_back(k):
        ys[...] = y_small[...].astype(bf16)
        begin(y_copies)
        for i in range(micro):
            links.wait(*b_parts[i][2][2])
        links.wait(*y_came)
        lane = lanes_of((rows, LANES))
        smalls = own_lanes(y_small[...] + sum(ysrecv[k].astype(f32) for k in range(depth - 1)))
        parts = []
        for i in range(micro):
            value = yb[i, place.z].astype(f32) + sum(yrecv[i, k].astype(f32) for k in range(depth - 1))
            small = smalls if i == 0 else pltpu.roll(smalls, LANES - 8 * i, 1)
            small = jnp.where(lane < feat - main, small, 0.0)
            parts.append(jnp.concatenate([value.astype(bf16), small.astype(bf16)], axis=1))
        back_low[...] = jnp.concatenate(parts, axis=0)
        for j, (kind, lanes, _) in enumerate(chunks):
            if kind == 3:
                summed(j, dot(nq[...], back_low[:, lanes], 0, 0))

    def queries_in(k):
        back_feats = back_low[...]
        grad_q = (dot(back_feats, wk[...], 1, 0) * scaling).astype(bf16)
        grad_nq = dot(grad_q, wq[...], 1, 1)
        unit_q, spread_q = normed(x_in[...].reshape(owned, width).astype(f32))
        value_tail = pltpu.roll(seen[:, main:], 5, 1).astype(bf16)
        row = rows_of((16, width))
        terms = dot(back_feats[:, main:], nq[...], 0, 0)[:16] + dot(value_tail, gh_low[...], 0, 0)[:16]
        terms = jnp.where(row == 10, sum(grad_gm), terms)
        terms = jnp.where(row == 11, jnp.sum(grad_nq * unit_q, axis=0, keepdims=True), terms)
        grad_gp = jnp.concatenate([gp_acc[...], jnp.zeros((wide - tall, LANES), f32)], axis=0).T
        grad_gp = jnp.sum(grad_gp, axis=0, keepdims=True)
        grad_gp = jnp.concatenate([grad_gp, jnp.zeros((1, width - wide), f32)], axis=1)
        small_sum.begin(jnp.where(row == 12, grad_gp, terms))
        up_store.wait()
        up_out[...] = (grad_h[...] + normed_back(grad_nq * gain_query[...], unit_q, spread_q)).reshape(micro, rows, width)
        last = pltpu.make_async_copy(up_out, grad_latents, store_sem.at[1 + micro])
        last.start()
        stores.append(last)


    small_sum = Everywhere(
        links, place, small_src, small_recv, small_slots, links.group(wq.at[pl.ds(0, (3 + depth - 1) * 16)])
    )

    def small_end(k):
        small_out[...] = small_sum.end()
        stores.append(pltpu.make_async_copy(small_out, sum_small, store_sem.at[2 + micro]))
        stores[-1].start()

    steps = {
        "P": lambda k: pixel_rows(), "p": pixel_norm, "X": lambda k: q_ext.forward(), "q": lambda k: q_main[k].forward(),
        "E": lambda k: q_ext.end(), "A": attend_out, "M": join, "Z": small_out_of, "O": owner_starts, "N": lambda k: next(owners[k], None), "B": term, "U": layer_out,
        "x": lambda k: g_ext[k].forward(), "g": lambda k: g_main[k].forward(), "e": small_in, "a": attend_back, "m": join_back,
        "Q": queries_back, "L": queries_in, "s": lambda k: small_sum.stage(k), "S": small_end,
    }
    for step in ORDER:
        if step[0] == "r":
            totals[int(step[2:])].rs(int(step[1]))
        elif step[0] == "b":
            totals[int(step[2:])].back(int(step[1]))
        else:
            steps[step[0]](int(step[1:]))
    for store in stores:
        store.wait()
    links.drain()


def fused(mesh, pixels, counts, latents, cotangent, w_query, w_key, w_value, w_out, w_hidden, w_back, gain_query, gain_pixel, gain_mlp):
    micro, px_rows, feat = pixels.shape
    rows, width = latents.shape[1:]
    depth = mesh.shape["blk"] // 2
    main = feat // LANES * LANES
    wide = main + LANES
    line = depth * rows
    dims = (micro, rows, depth, px_rows, feat, main, wide, width)
    tall = main + 16
    any_spec = pl.BlockSpec(memory_space=pl.ANY)
    vmem = pl.BlockSpec(memory_space=pltpu.VMEM)
    V = pltpu.VMEM
    chunks = chunks_of(width, main)

    def total_recvs(lanes, orders):
        held, height = [], width
        for axis in "c" + orders[0]:
            height //= depth if axis == "z" else 2
            held.append(V((depth - 1 if axis == "z" else 1, height, lanes.stop - lanes.start), bf16))
        return held

    reduce_buffers = [
        V((micro, 2, main, line), bf16), V((micro, 2, 8, line), f32), V((micro, main, line), bf16), V((micro, 8, line), f32),
        V((micro, depth, rows, main), bf16), V((micro, depth - 1, rows, main), bf16),
    ]
    arrivals = 2 * (2 * micro + 3) + 3 * 2 * micro + 3 + 8 * len(chunks) + 4
    groups = 4 + 6 + 2 + 2 * len(chunks) + 1
    scratch = (
        [
            V((feat, micro, px_rows), bf16), V((micro, tall, px_rows), bf16), V((micro, 8, px_rows), f32),
            V((micro, px_rows, wide), bf16), V((micro, tall, px_rows), bf16),
            V((px_rows, 2 * line), f32), V((micro, px_rows, 2 * line), bf16), V((px_rows, 2 * line), bf16),
            V(latents.shape, bf16), V(cotangent.shape, f32),
        ]
        + [V((width, width), bf16)] * 4
        + [V((feat, width), bf16)] * 2
        + [V((wide, width), bf16)] * 2
        + [V((micro, 2, depth, rows, main), bf16), V((2, depth, rows, LANES), bf16)]
        + [V((micro, 2, depth, rows, main), bf16), V((2, 2, depth, 16, LANES), bf16)]
        + reduce_buffers * 2
        + [
            V((2, 4 * micro, line), f32), V((2, depth - 1, 4 * micro, line), f32),
            V((8 * micro, line), f32), V((8 * micro, line), bf16), V((depth - 1, 8 * micro, line), bf16),
            V((micro, 8, 2 * line), f32), V((micro * rows, wide), f32), V((micro * rows, LANES), f32),
            V((micro, 2, depth, rows, LANES), bf16), V((micro * rows, wide), bf16),
        ]
        + [V((micro * rows, width), bf16)] * 4
        + [V((micro * rows, width), f32), V((micro * rows, width), bf16), V(latents.shape, f32)]
        + [
            V((3, 16, width), bf16), V((3, 16, width), bf16), V((depth, 16, width), bf16), V((16, width), f32), V((tall, LANES), f32),
        ]
        + [
            [V((width, lanes.stop - lanes.start), bf16) for _, lanes, _ in chunks],
            [total_recvs(lanes, orders) for _, lanes, orders in chunks],
            pltpu.SemaphoreType.DMA((groups,)), pltpu.SemaphoreType.DMA((arrivals,)),
            pltpu.SemaphoreType.DMA((9,)), pltpu.SemaphoreType.DMA((3 + micro,)), pltpu.SemaphoreType.DMA((len(chunks),)),
        ]
    )
    S = jax.ShapeDtypeStruct
    return pl.pallas_call(
        functools.partial(kernel, dims),
        out_shape=[
            S(latents.shape, f32), S(latents.shape, f32), S((micro, tall, px_rows), bf16),
            S((width, width), bf16), S((width, width), bf16), S((width, main), bf16), S((width, main), bf16), S((16, width), f32),
        ],
        in_specs=[pl.BlockSpec(memory_space=pltpu.SMEM)] + [any_spec] * 9 + [vmem] * 3,
        out_specs=[any_spec] * 8,
        scratch_shapes=scratch,
        compiler_params=pltpu.CompilerParams(collective_id=0, has_side_effects=True, vmem_limit_bytes=63 * 2**20),
        name="layer",
    )(
        counts, jnp.transpose(pixels, (2, 0, 1)), latents, cotangent, w_query, w_out, w_hidden, w_back, w_key, w_value,
        gain_query.reshape(1, -1), gain_pixel, gain_mlp.reshape(1, -1),
    )


def finish(
    dims,
    late, value, small, w_key, w_value, w_query, w_out, hidden, back, px, up, lat,
    out_query, out_key, out_value, out_out, out_hidden, out_back, out_px, out_up, out_lat, out_gq, out_gp, out_gm,
    key_rows, value_rows, late_t, value_t, late_rows,
):
    feat, main, wide, width = dims
    scaling = 1.0 / math.sqrt(width)
    step = out_query.shape[0]
    here = pl.ds(pl.multiple_of(pl.program_id(0) * step, step), step)

    @pl.when(pl.program_id(0) == 0)
    def prepare():
        for raw, dst in ((w_key, key_rows), (w_value, value_rows)):
            dst[:main] = raw[:main]
            last = raw[main:].astype(f32)
            dst[main:] = jnp.concatenate([last, jnp.zeros((wide - feat, width), f32)], axis=0).astype(bf16)
        row = rows_of((16, width))
        rest = jnp.zeros((LANES - 16, width), f32)
        tail = jnp.concatenate([jnp.where(row < 5, small[...], 0.0), rest], axis=0)
        late_rows[:, :main] = late[...]
        late_rows[:, main:] = tail.T.astype(bf16)
        late_t[:main] = late[...].astype(f32).T.astype(bf16)
        late_t[main:] = tail.astype(bf16)
        tail = jnp.concatenate([jnp.where(row < 5, pltpu.roll(small[...], 11, 0), 0.0), rest], axis=0)
        value_t[:main] = value[...].astype(f32).T.astype(bf16)
        value_t[main:] = tail.astype(bf16)
        out_gm[...] = small[10]
        out_gq[...] = small[11]
        out_gp[...] = small[12, :feat]

    out_query[...] = dot(late_rows[here, :], key_rows[...], 1, 0) * scaling
    out_out[...] = dot(value_rows[:, here], value_t[...], 0, 0)
    out_key[...] = (dot(late_t[...], w_query[...], 1, 0) * scaling)[:feat]
    out_value[...] = dot(value_t[...], w_out[...], 1, 1)[:feat]
    out_hidden[...] = hidden[...].astype(f32)
    out_back[...] = back[...].astype(f32)
    out_px[...] = jnp.swapaxes(px[...].astype(f32), 0, 1)
    out_up[...] = up[...]
    out_lat[...] = lat[...]


def finished(pixels, latents, w_key, w_value, w_query, w_out, up, lat, px, back, hidden, value, late, small):
    micro, px_rows, feat = pixels.shape
    rows, width = latents.shape[1:]
    main = feat // LANES * LANES
    wide = main + LANES
    steps = 2
    step, px_step = width // steps, -(-feat // (16 * steps)) * 16
    px_last = -(-feat // px_step) - 1
    whole = lambda *shape: pl.BlockSpec(shape, lambda k: (0,) * len(shape))
    by_row = pl.BlockSpec((step, width), lambda k: (k, 0))
    by_column = lambda height: pl.BlockSpec((height, step), lambda k: (0, k))
    lat_block = pl.BlockSpec((micro, rows // steps, width), lambda k: (0, k, 0))
    S = jax.ShapeDtypeStruct
    out = pl.pallas_call(
        functools.partial(finish, (feat, main, wide, width)),
        grid=(steps,),
        in_specs=[
            whole(width, main), whole(width, main), whole(16, width), whole(feat, width), whole(feat, width), by_column(width), by_row,
            by_row, by_row, pl.BlockSpec((micro, px_step, px_rows), lambda k: (0, jnp.minimum(k, px_last), 0)), lat_block, lat_block,
        ],
        out_specs=[
            by_row, by_column(feat), by_column(feat), by_row, by_row, by_row,
            pl.BlockSpec((px_step, micro, px_rows), lambda k: (jnp.minimum(k, px_last), 0, 0)), lat_block, lat_block,
            whole(width), whole(feat), whole(width),
        ],
        out_shape=[
            S((width, width), f32), S((feat, width), f32), S((feat, width), f32), S((width, width), f32),
            S((width, width), f32), S((width, width), f32), S((feat, micro, px_rows), f32),
            S(latents.shape, f32), S(latents.shape, f32), S((width,), f32), S((feat,), f32), S((width,), f32),
        ],
        scratch_shapes=[pltpu.VMEM((wide, width), bf16)] * 4 + [pltpu.VMEM((width, wide), bf16)],
        compiler_params=pltpu.CompilerParams(vmem_limit_bytes=60 * 2**20),
        name="finish",
    )(late, value, small, w_key, w_value, w_query, w_out, hidden, back, px, up, lat)
    g_query, g_key, g_value, g_out, g_hidden, g_back, g_px, g_up, g_lat, g_gq, g_gp, g_gm = out
    g_px = jnp.transpose(g_px, (1, 2, 0))
    return g_up, g_lat, g_px, g_query, g_key, g_value, g_out, g_hidden, g_back, g_gq, g_gp, g_gm


def fused_body(mesh, *args):
    w_query, w_key, w_value, w_out = args[4:8]
    return finished(args[0], args[2], w_key, w_value, w_query, w_out, *fused(mesh, *args))


def layer_norm(values, gain_vec):
    centered = values - jnp.mean(values, axis=-1, keepdims=True)
    variance = jnp.mean(centered * centered, axis=-1, keepdims=True)
    return centered * lax.rsqrt(variance + EPSILON) * gain_vec


def gelu_exact(values):
    return jax.nn.gelu(values, approximate=False)


def low(values):
    return values.astype(jnp.bfloat16)


def product(left_mat, right_mat):
    return jnp.dot(left_mat, right_mat, preferred_element_type=jnp.float32)


def product_tn(left_mat, right_mat):
    return lax.dot_general(
        left_mat, right_mat, (((0,), (0,)), ((), ())), preferred_element_type=jnp.float32
    )


def product_nt(left_mat, right_mat):
    return lax.dot_general(
        left_mat, right_mat, (((1,), (1,)), ((), ())), preferred_element_type=jnp.float32
    )


def each(spec, left, right):
    return jnp.einsum(spec, left, right, preferred_element_type=jnp.float32)


def to_owner(x, peers):
    micro, rows = x.shape[:2]
    blocks = jnp.moveaxis(x.reshape(micro, peers, rows // peers, *x.shape[2:]), 1, 0)
    return lax.all_to_all(blocks, "blk", 0, 0, tiled=True)


def plain_body(pixels, counts, latents, cotangent, w_query, w_key, w_value, w_out, w_hidden, w_back, gain_query, gain_pixel, gain_mlp):
    micro, pixel_rows, features = pixels.shape
    lat_rows, width = latents.shape[1:]
    peers = lax.axis_size("blk")
    scaling = 1.0 / math.sqrt(width)
    rows = micro * lat_rows
    positions = lax.axis_index("blk") * pixel_rows + jnp.arange(pixel_rows, dtype=jnp.int32)
    valid = positions[None, :] < counts[:, None]

    latent_in = latents.reshape(rows, width).astype(jnp.float32)
    normed_qf, query_pull = jax.vjp(layer_norm, latent_in, gain_query)
    normed_q = low(normed_qf)
    queries = low(product(normed_q, w_query))
    query_feats = low(product_nt(queries, w_key) * scaling).reshape(micro, lat_rows, features)
    all_query = lax.all_gather(query_feats, "blk", axis=1, tiled=True)
    normed_pf, pixel_pull = jax.vjp(layer_norm, pixels.astype(jnp.float32), gain_pixel)
    normed_p = low(normed_pf)
    scores = each("mqf,mpf->mqp", all_query, normed_p)
    scores = jnp.where(valid[:, None, :], scores, MASKED)
    highest = jnp.max(scores, axis=2)
    unscaled = jnp.exp(scores - highest[..., None])
    total = jnp.sum(unscaled, axis=2)
    sums = low(each("mqp,mpf->mqf", low(unscaled), normed_p))
    parts = to_owner(sums, peers).astype(jnp.float32)
    stats = to_owner(jnp.stack([highest, total], axis=2), peers)
    top = jnp.max(stats[..., 0], axis=0)
    scale = jnp.exp(stats[..., 0] - top)
    denom = jnp.sum(stats[..., 1] * scale, axis=0)
    lse = top + jnp.log(denom)
    seen = (jnp.sum(parts * scale[..., None], axis=0) / denom[..., None]).reshape(rows, features)
    seen_b = low(seen)
    attended_b = low(product(seen_b, w_value))
    hidden_in = latent_in + product(attended_b, w_out)
    normed_mf, mlp_pull = jax.vjp(layer_norm, hidden_in, gain_mlp)
    normed_m = low(normed_mf)
    pre_act = product(normed_m, w_hidden)
    activated_f, gelu_pull = jax.vjp(gelu_exact, pre_act)
    activated = low(activated_f)
    updated = hidden_in + product(activated, w_back)
    cot = cotangent.reshape(rows, width)
    cot_b = low(cot)
    grad_back = product_tn(activated, cot_b)
    (grad_pre,) = gelu_pull(product_nt(cot_b, w_back))
    grad_pre_b = low(grad_pre)
    grad_hidden = product_tn(normed_m, grad_pre_b)
    grad_h_ln, grad_gm = mlp_pull(product_nt(grad_pre_b, w_hidden))
    grad_h = cot + grad_h_ln
    grad_h_b = low(grad_h)
    grad_att = low(product_nt(grad_h_b, w_out))
    grad_seen = product_nt(grad_att, w_value)
    dots = jnp.sum(grad_seen * seen, axis=1).reshape(micro, lat_rows)
    value_side = product_tn(seen_b, grad_h_b)
    all_grad = lax.all_gather(low(grad_seen).reshape(micro, lat_rows, features), "blk", axis=1, tiled=True)
    all_stat = lax.all_gather(jnp.stack([lse, dots], axis=2), "blk", axis=1, tiled=True)
    probs = unscaled * jnp.exp(highest - all_stat[..., 0])[..., None]
    grad_probs = each("mqf,mpf->mqp", all_grad, normed_p)
    grad_scores = low(probs * (grad_probs - all_stat[..., 1][..., None]))
    back_sums = low(each("mqp,mpf->mqf", grad_scores, normed_p))
    grad_np = each("mqp,mqf->mpf", low(probs), all_grad) + each("mqp,mqf->mpf", grad_scores, all_query)
    grad_pixels, grad_gp = pixel_pull(grad_np)
    back_feats = jnp.sum(to_owner(back_sums, peers).astype(jnp.float32), axis=0).reshape(rows, features)
    back_b = low(back_feats)
    grad_q = low(product(back_b, w_key) * scaling)
    grad_lat_q, grad_gq = query_pull(product_nt(grad_q, w_query))
    grad_latents = grad_h + grad_lat_q
    query_side = product_tn(normed_q, back_b)
    query_side, value_side, grad_hidden, grad_back, grad_gq, grad_gp, grad_gm = lax.psum(
        (query_side, value_side, grad_hidden, grad_back, grad_gq, grad_gp, grad_gm), ("img", "blk")
    )
    query_b, value_b = low(query_side * scaling), low(value_side)
    return (
        updated.reshape(micro, lat_rows, width),
        grad_latents.reshape(micro, lat_rows, width),
        grad_pixels,
        product(query_b, w_key),
        product_tn(query_b, w_query),
        product_nt(value_b, w_out),
        product_tn(w_value, value_b),
        grad_hidden,
        grad_back,
        grad_gq,
        grad_gp,
        grad_gm,
    )


def body(mesh, *args):
    pixels, latents = args[0], args[2]
    rows, width = latents.shape[1:]
    fits = pixels.shape[0] // 2 * rows == LANES and rows % 16 == 0 and width % (16 * mesh.size) == 0
    fits = fits and mesh.shape["img"] == 4 and mesh.shape["blk"] % 2 == 0
    return fused_body(mesh, *args) if fits else plain_body(*args)


def solution(mesh):
    spread, same = P("img", "blk", None), P()
    return jax.shard_map(
        functools.partial(body, mesh),
        mesh=mesh,
        in_specs=(spread, P("img"), spread, spread) + (same,) * 9,
        out_specs=(spread,) * 3 + (same,) * 9,
        check_vma=False,
    )
```

```python
import functools
import math

import jax
import jax.numpy as jnp
from jax import lax
from jax.experimental import pallas as pl
from jax.experimental.pallas import tpu as pltpu
from jax.sharding import PartitionSpec as P

EPSILON = 1e-05
MASKED = -1e30
LANES = 128
MESH = pl.DeviceIdType.MESH
bf16, f32 = jnp.bfloat16, jnp.float32


def dot(left, right, left_dim, right_dim):
    return lax.dot_general(left, right, (((left_dim,), (right_dim,)), ((), ())), preferred_element_type=f32)


def lanes_of(shape):
    return lax.broadcasted_iota(jnp.int32, shape, 1)


def rows_of(shape):
    return lax.broadcasted_iota(jnp.int32, shape, 0)


def normed(values):
    part = 1.0 / values.shape[1]
    centered = values - jnp.sum(values, axis=1, keepdims=True) * part
    spread = lax.rsqrt(jnp.sum(centered * centered, axis=1, keepdims=True) * part + EPSILON)
    return centered * spread, spread


def normed_back(grad, unit, spread):
    part = 1.0 / grad.shape[1]
    first = jnp.sum(grad, axis=1, keepdims=True) * part
    second = jnp.sum(grad * unit, axis=1, keepdims=True) * part
    return spread * (grad - first - unit * second)


def split_low(values):
    high = values.astype(bf16).astype(f32)
    return high, (values - high).astype(bf16).astype(f32)


ORDER = (
    "P0", "p1", "p2", "p3", "p0", "X0", "q0", "E0", "q1", "A0", "q2", "A1", "q3", "M0", "A2", "M1", "Z0", "A3", "M2", "O0", "M3",
    "Z1", "N0", "O1", "B1", "x0", "N1", "U0", "B3", "B0", "e0", "g0", "B2", "g1", "B4", "r01", "x1", "r03", "g2", "a0", "r00",
    "g3", "r02", "a1", "e1", "r04", "r11", "a2", "m0", "a3", "r13", "m1", "r21", "m2", "r10", "m3", "r23", "r12", "r31", "r14",
    "Q0", "r20", "L0", "r22", "r33", "r24", "r05", "b01", "s0", "r30", "r15", "r32", "b03", "b11", "s1", "r25", "r34", "b02",
    "b00", "b13", "r35", "b12", "b04", "b05", "b10", "b21", "s2", "b14", "b23", "b31", "b15", "b20", "b24", "b33", "b22", "b25",
    "b30", "S0", "b34", "b32", "b35",
)


def chunks_of(width, main):
    half = width // 2
    return (
        (0, slice(0, half), ("xyz", "zxy")),
        (0, slice(half, width), ("xzy", "zxy")),
        (1, slice(0, half), ("xyz", "yxz")),
        (1, slice(half, width), ("xyz", "zyx")),
        (2, slice(0, main), ("xyz", "zyx")),
        (3, slice(0, main), ("xyz", "zxy")),
    )


class Links:
    def __init__(self, send_sem, recv_sem):
        self.send_sem, self.recv_sem, self.arrivals, self.groups = send_sem, recv_sem, 0, []

    def group(self, size):
        self.groups.append(size)
        return len(self.groups) - 1

    def arrival(self):
        self.arrivals += 1
        return self.arrivals - 1

    def remote(self, src, dst, device, group, arrival):
        return pltpu.make_async_remote_copy(
            src_ref=src, dst_ref=dst, send_sem=self.send_sem.at[group], recv_sem=self.recv_sem.at[arrival],
            device_id=device, device_id_type=MESH,
        )

    def wait(self, size, arrival):
        pltpu.make_async_copy(size, size, self.recv_sem.at[arrival]).wait()

    def drain(self):
        for group, size in enumerate(self.groups):
            pltpu.make_async_copy(size, size, self.send_sem.at[group]).wait()


class Place:
    def __init__(self, depth):
        img, blk = lax.axis_index("img"), lax.axis_index("blk")
        self.x, self.c = lax.div(img, 2), lax.rem(img, 2)
        self.z, self.y = lax.div(blk, 2), lax.rem(blk, 2)
        self.core_peer = (self.x * 2 + 1 - self.c, blk)
        self.x_peer = ((1 - self.x) * 2 + self.c, blk)
        self.y_peer = (img, self.z * 2 + 1 - self.y)
        self.z_index = [lax.rem(self.z + k, depth) for k in range(1, depth)]
        self.z_peers = [(img, other * 2 + self.y) for other in self.z_index]

    def all(self):
        return [self.core_peer, self.x_peer, self.y_peer] + self.z_peers


class Gather:
    def __init__(self, links, place, ref, group, size):
        own, line = ref.at[place.y, place.z], ref.at[place.y]
        self.links, self.size, self.line = links, size, ref.at[0]
        self.came_z, self.came_y = links.arrival(), links.arrival()
        self.along = [links.remote(own, own, peer, group, self.came_z) for peer in place.z_peers]
        self.across = links.remote(line, line, place.y_peer, group, self.came_y)

    def begin(self):
        for copy in self.along:
            copy.start()

    def forward(self):
        self.links.wait(self.size, self.came_z)
        self.across.start()

    def end(self):
        self.links.wait(self.line, self.came_y)


class Everywhere:
    def __init__(self, links, place, src, recv, slots, group):
        self.links, self.src, self.recv, self.slots, self.z = links, src, recv, slots, place.z
        peers = (place.core_peer, place.x_peer, place.y_peer)
        self.came = [links.arrival() for _ in range(4)]
        self.swaps = [links.remote(src.at[k], recv.at[k], peer, group, self.came[k]) for k, peer in enumerate(peers)]
        mine = slots.at[place.z]
        self.along = [links.remote(mine, mine, peer, group, self.came[3]) for peer in place.z_peers]

    def begin(self, value):
        self.src[0] = value.astype(bf16)
        self.swaps[0].start()

    def stage(self, k):
        self.links.wait(self.recv.at[k], self.came[k])
        total = (self.src[k].astype(f32) + self.recv[k].astype(f32)).astype(bf16)
        if k < 2:
            self.src[k + 1] = total
            self.swaps[k + 1].start()
        else:
            self.slots[self.z] = total
            for copy in self.along:
                copy.start()

    def end(self):
        count = len(self.along)
        self.links.wait(self.slots.at[pl.ds(0, count)], self.came[3])
        return sum(self.slots[k].astype(f32) for k in range(count + 1))


class Total:
    def __init__(self, links, place, orders, src, recv, out, local_sem, lanes):
        self.links, self.src, self.recv = links, src, recv
        there_order, back_order = orders
        depth = len(place.z_peers) + 1
        axes = {
            "c": ([place.core_peer], [1 - place.c], place.c, 2), "x": ([place.x_peer], [1 - place.x], place.x, 2),
            "y": ([place.y_peer], [1 - place.y], place.y, 2), "z": (place.z_peers, place.z_index, place.z, depth),
        }
        last = src.shape[0] // (8 * depth)
        everything = src.at[pl.ds(0, src.shape[0] - last)]
        there, back = links.group(everything), links.group(everything)
        offset, height = 0, src.shape[0]
        self.there, self.spans, heights = [], [], {}
        for k, axis in enumerate("c" + there_order):
            peers, indices, own, count = axes[axis]
            height //= count
            heights[axis] = height
            came = links.arrival()
            copies = []
            for n, (peer, index) in enumerate(zip(peers, indices)):
                start = pl.multiple_of(offset + index * height, height)
                copies.append(links.remote(src.at[pl.ds(start, height)], recv[k].at[n], peer, there, came))
            offset = pl.multiple_of(offset + own * height, height)
            self.there.append((copies, came))
            self.spans.append((offset, height))
        self.kept = pltpu.make_async_copy(src.at[pl.ds(offset, height)], out.at[pl.ds(offset, height), lanes], local_sem)
        self.backs, held, source = [], [(offset, height)], src
        for axis in back_order + "c":
            peers, _, own, count = axes[axis]
            came, step = links.arrival(), heights[axis]
            copies = []
            for peer in peers:
                for start, size in held:
                    region = out.at[pl.ds(start, size), lanes]
                    first = src.at[pl.ds(start, size)] if source is src else region
                    copies.append(links.remote(first, region, peer, back, came))
            size = src.at[pl.ds(0, len(peers) * sum(size for _, size in held))]
            self.backs.append((copies, size, came))
            source = out
            if held[0][1] == step:
                held = [(pl.multiple_of(start - own * step, step), size * count) for start, size in held]
            else:
                align = min(step, held[0][1])
                held = [(pl.multiple_of(start + (v - own) * step, align), size) for start, size in held for v in range(count)]

    def send(self, stage):
        for copy in self.there[stage][0]:
            copy.start()

    def rs(self, stage):
        held = self.recv[stage]
        self.links.wait(held, self.there[stage][1])
        start, size = self.spans[stage]
        step = min(size, 64)

        def some(k):
            here = pl.ds(pl.multiple_of(start + k * step, step), step)
            block = pl.ds(pl.multiple_of(k * step, step), step)
            total = self.src[here, :].astype(f32)
            for n in range(held.shape[0]):
                total = total + held[n, block, :].astype(f32)
            self.src[here, :] = total.astype(bf16)

        pl.loop(0, size // step)(some)
        if stage < 3:
            self.send(stage + 1)
        else:
            self.kept.start()
            for copy in self.backs[0][0]:
                copy.start()

    def back(self, stage):
        _, size, came = self.backs[stage]
        self.links.wait(size, came)
        if stage == 0:
            self.kept.wait()
        if stage < 3:
            for copy in self.backs[stage + 1][0]:
                copy.start()


def kernel(
    dims,
    counts, pixels, latents, cotangent, w_query, w_out, w_hidden, w_back, w_key, w_value, gain_query, gain_pixel, gain_mlp,
    updated, grad_latents, grad_pixels, sum_back, sum_hidden, sum_value, sum_late, sum_small,
    px, px_t, px_stats, np_all, npt_all, scores, probs, grad_s, x_in, cot_in, wq, wo, wh, wb, wk_in, wv_in, wk, wv,
    q_all, qx_all, g_all, gx_all,
    ob, oe, orecv, oerecv, zb, zrecv, bb, be, brecv, berecv, yb, yrecv, zs, zsrecv, y_small, ys, ysrecv,
    tops, seen, lse, g_small, back_low, nq, nm, act, gpre, grad_h, gh_low, up_out, small_src, small_recv, small_slots, small_out, gp_acc,
    sources, recvs, send_sem, recv_sem, load_sem, store_sem, kept_sem,
):
    micro, rows, depth, px_rows, feat, main, wide, width = dims
    pair = micro // 2
    chunks = chunks_of(width, main)
    line = depth * rows
    everyone = 2 * line
    scaling = 1.0 / math.sqrt(width)
    links, place = Links(send_sem, recv_sem), Place(depth)
    loads = {}

    def load(name, src, dst):
        loads[name] = pltpu.make_async_copy(src, dst, load_sem.at[len(loads)])
        return loads[name]

    load("x", latents, x_in).start()
    load("wq", w_query, wq).start()
    load("wk", w_key, wk_in).start()
    barrier = pltpu.get_barrier_semaphore()
    for peer in place.all():
        pl.semaphore_signal(barrier, inc=1, device_id=peer, device_id_type=MESH)
    gp_acc[...] = jnp.zeros_like(gp_acc)

    def pad_rows(raw, dst):
        dst[:main] = raw[:main]
        last = raw[main:].astype(f32)
        dst[main:] = jnp.concatenate([last, jnp.zeros((wide - feat, width), f32)], axis=0).astype(bf16)

    loads["x"].wait()
    unit_q, _ = normed(x_in[...].reshape(micro * rows, width).astype(f32))
    nq[...] = (unit_q * gain_query[...]).astype(bf16)
    loads["wq"].wait()
    loads["wk"].wait()
    load("px", pixels, px).start()
    for name, src, dst in (("wv", w_value, wv_in), ("wo", w_out, wo), ("wh", w_hidden, wh), ("wb", w_back, wb), ("cot", cotangent, cot_in)):
        load(name, src, dst).start()
    pad_rows(wk_in, wk)
    queries = dot(nq[...], wq[...], 1, 0).astype(bf16)
    feats = dot(queries, wk[...], 1, 1) * scaling
    small = jnp.where(lanes_of((rows, LANES)) % 16 == 6, 1.0, 0.0)
    for i in range(micro):
        here = slice(i * rows, (i + 1) * rows)
        q_all[i, place.y, place.z] = feats[here, :main].astype(bf16)
        tail = feats[here, main:]
        small = small + (tail if i == 0 else pltpu.roll(tail, 16 * i, 1))
    qx_all[place.y, place.z] = small.astype(bf16)
    pl.semaphore_wait(barrier, len(place.all()))

    def gathers(main_ref, ext_refs, ext_size):
        blocks = micro * (2 * depth - 1)
        group = links.group(wq.at[pl.ds(0, blocks * rows * main // width)])
        mains = [Gather(links, place, main_ref.at[i], group, zrecv.at[i]) for i in range(micro)]
        group = links.group(lse.at[pl.ds(0, len(ext_refs) * (2 * depth - 1) * ext_size.shape[0] // (depth - 1))])
        return mains, [Gather(links, place, ref, group, ext_size) for ref in ext_refs]

    q_main, (q_ext,) = gathers(q_all, [qx_all], lse.at[pl.ds(0, (depth - 1) * rows // 2)])
    g_main, g_ext = gathers(g_all, [gx_all.at[g] for g in range(2)], lse.at[pl.ds(0, (depth - 1) * 8)])
    q_ext.begin()
    for gather in q_main:
        gather.begin()

    first_pixel = lax.axis_index("blk") * px_rows
    tall = main + 16
    gain_column = jnp.broadcast_to(gain_pixel[...].reshape(1, feat), (LANES, feat))
    gain_column = jnp.concatenate([gain_column, jnp.zeros((LANES, wide - feat), f32)], axis=1).T[:tall, 0:1]

    def pixel_rows():
        loads["px"].wait()
        for first in range(0, feat, 16):
            last = min(first + 16, feat)
            block = px[first:last].astype(f32)
            if last - first < 16:
                block = jnp.concatenate([block, jnp.zeros((16 - last + first,) + block.shape[1:], f32)], axis=0)
            block = jnp.swapaxes(block, 0, 1)
            for i in range(micro):
                px_t[i, first : first + 16] = block[i].astype(bf16)

    def pixel_unit(i, mean):
        centered = px_t[i].astype(f32) - mean
        return jnp.where(rows_of((tall, px_rows)) < feat, centered, 0.0)

    def pixel_norm(i):
        mean = jnp.sum(px_t[i].astype(f32), axis=0, keepdims=True) * (1.0 / feat)
        centered = pixel_unit(i, mean)
        spread = lax.rsqrt(jnp.sum(centered * centered, axis=0, keepdims=True) * (1.0 / feat) + EPSILON)
        px_stats[i, 0:1], px_stats[i, 1:2] = mean, spread
        row = rows_of((tall, px_rows))
        value = centered * spread * gain_column
        value = jnp.where((row == main + 5) | (row == main + 7), 1.0, value)
        npt_all[i] = value.astype(bf16)
        masked = first_pixel + lanes_of((tall, px_rows)) >= counts[i]
        value = jnp.where((row == main + 6) & masked, MASKED, value)
        np_all[i] = jnp.concatenate([value, jnp.zeros((wide - tall, px_rows), f32)], axis=0).T.astype(bf16)

    def query_block(i):
        small = qx_all[...].reshape(everyone, LANES).astype(f32)
        if i:
            small = pltpu.roll(small, LANES - 16 * i, 1)
        small = jnp.where(lanes_of((everyone, LANES)) < 16, small, 0.0)
        return jnp.concatenate([q_all[i].reshape(everyone, main), small.astype(bf16)], axis=1)

    def attend(i):
        q_main[i].end()
        scores[...] = dot(np_all[i], query_block(i), 1, 1)
        top = jnp.max(scores[...], axis=0, keepdims=True)
        tops[i] = jnp.broadcast_to(top, (8, everyone))
        probs[i] = jnp.exp(scores[...] - top).astype(bf16)
        sums = dot(npt_all[i], probs[i], 1, 0)
        small = jnp.where(rows_of((8, everyone)) == 6, top, sums[main : main + 8])
        for y in range(2):
            here = slice(y * line, (y + 1) * line)
            ob[i, y] = sums[:main, here].astype(bf16)
            oe[i, y] = small[:, here]

    def exchanges(sums, small, held, small_held, parts, parts_held):
        main_group = links.group(wq.at[pl.ds(0, micro * line * main // width)])
        small_group = links.group(wq.at[pl.ds(0, micro * 2 * 8 * line // width)])
        owner_group = links.group(wq.at[pl.ds(0, micro * (depth - 1) * rows * main // width)])
        out = []
        for i in range(micro):
            came, small_came, owner_came = links.arrival(), links.arrival(), links.arrival()
            swaps = [
                links.remote(sums.at[i, 1 - place.y], held.at[i], place.y_peer, main_group, came),
                links.remote(small.at[i, 1 - place.y], small_held.at[i], place.y_peer, small_group, small_came),
            ]
            owners = [
                links.remote(parts.at[i, other], parts_held.at[i, k], peer, owner_group, owner_came)
                for k, (peer, other) in enumerate(zip(place.z_peers, place.z_index))
            ]
            out.append((swaps, owners, ((held.at[i], came), (small_held.at[i], small_came), (parts_held.at[i], owner_came))))
        return out

    def begin(copies):
        for copy in copies:
            copy.start()

    q_parts = exchanges(ob, oe, orecv, oerecv, zb, zrecv)
    b_parts = exchanges(bb, be, brecv, berecv, yb, yrecv)

    def own_lanes(part):
        part = pltpu.roll(part, lax.rem((depth - place.z) * rows, line), 1)[:, :LANES]
        return jnp.concatenate([part, jnp.zeros((LANES - part.shape[0], LANES), f32)], axis=0).T[:rows]

    def join(i):
        _, owners, waits = q_parts[i]
        links.wait(*waits[0])
        links.wait(*waits[1])
        mine, theirs = oe[i, place.y], oerecv[i]
        top_m, top_t = mine[6:7], theirs[6:7]
        top = jnp.maximum(top_m, top_t)
        scale_m, scale_t = jnp.exp(top_m - top), jnp.exp(top_t - top)
        total = ob[i, place.y].astype(f32) * scale_m + orecv[i].astype(f32) * scale_t
        zb[i] = total.T.astype(bf16).reshape(depth, rows, main)
        small = mine * scale_m + theirs * scale_t
        zs[i // pair, 8 * (i % pair) : 8 * (i % pair) + 8] = jnp.where(rows_of((8, line)) == 6, top, small)
        begin(owners)

    def attend_out(i):
        attend(i)
        begin(q_parts[i][0])

    def to_peers(src, dst, group):
        came = links.arrival()
        return [links.remote(src, dst.at[k], peer, group, came) for k, peer in enumerate(place.z_peers)], (dst, came)

    z_group = links.group(wq.at[pl.ds(0, 2 * (depth - 1) * 2 * 8 * pair * line // width)])
    z_small = [to_peers(zs.at[g], zsrecv.at[g], z_group) for g in range(2)]
    y_copies, y_came = to_peers(ys, ysrecv, links.group(lse.at[pl.ds(0, (depth - 1) * 4 * micro * line // LANES)]))

    def small_out_of(g):
        begin(z_small[g][0])

    grad_gm, owners = [], {}

    def owner_starts(g):
        owners[g] = owner(g)
        next(owners[g])

    def owner(g):
        images = range(g * pair, (g + 1) * pair)
        links.wait(*z_small[g][1])
        for i in images:
            links.wait(*q_parts[i][2][2])
        smalls = [own_lanes(zs[g])] + [own_lanes(zsrecv[g, k]) for k in range(depth - 1)]
        lane = lanes_of((rows, LANES))
        for i in images:
            mains = [zb[i, place.z]] + [zrecv[i, k] for k in range(depth - 1)]
            base = 8 * (i % pair)
            highs = [small[:, base + 6 : base + 7] for small in smalls]
            top = functools.reduce(jnp.maximum, highs)
            scales = [jnp.exp(high - top) for high in highs]
            total = sum(small * scale for small, scale in zip(smalls, scales))
            denom = total[:, base + 5 : base + 6]
            here = slice(i * rows, (i + 1) * rows)
            seen[here, :main] = sum(value.astype(f32) * scale for value, scale in zip(mains, scales)) / denom
            if base:
                total = pltpu.roll(total, LANES - base, 1)
            seen[here, main:] = jnp.where(lane < feat - main, total / denom, 0.0)
            lse[here, :] = jnp.broadcast_to(top + jnp.log(denom), (rows, LANES))
        if g == 0:
            for name in ("wv", "wo", "wh", "wb", "cot"):
                loads[name].wait()
            pad_rows(wv_in, wv)
        own = pair * rows
        here, images = slice(g * own, (g + 1) * own), slice(g * pair, (g + 1) * pair)
        attended = dot(seen[here, :].astype(bf16), wv[...], 1, 0).astype(bf16)
        hidden_in = x_in[images].reshape(own, width).astype(f32) + dot(attended, wo[...], 1, 0)
        up_out[images] = hidden_in.reshape(pair, rows, width)
        unit_m, spread_m = normed(hidden_in)
        normed_m = (unit_m * gain_mlp[...]).astype(bf16)
        nm[here, :] = normed_m
        pre = dot(normed_m, wh[...], 1, 0)
        cumulative = 0.5 * (1.0 + lax.erf(pre * math.sqrt(0.5)))
        act[here, :] = (pre * cumulative).astype(bf16)
        yield
        slope = cumulative + pre * jnp.exp(-0.5 * pre * pre) * (1.0 / math.sqrt(2.0 * math.pi))
        cot_rows = cot_in[images].reshape(own, width)
        grad_pre = (slope * dot(cot_rows.astype(bf16), wb[...], 1, 1)).astype(bf16)
        gpre[here, :] = grad_pre
        grad_nm = dot(grad_pre, wh[...], 1, 1)
        grad_gm.append(jnp.sum(grad_nm * unit_m, axis=0, keepdims=True))
        grad_hidden = cot_rows + normed_back(grad_nm * gain_mlp[...], unit_m, spread_m)
        grad_h[here, :] = grad_hidden
        grad_low = grad_hidden.astype(bf16)
        gh_low[here, :] = grad_low
        grad_att = dot(grad_low, wo[...], 1, 1).astype(bf16)
        grad_seen = dot(grad_att, wv[...], 1, 1)
        dots_high, dots_low = split_low(-jnp.sum(grad_seen * seen[here, :], axis=1, keepdims=True))
        lse_value = lse[here, 0:1]
        lse_high = lse_value.astype(bf16).astype(f32)
        lse_mid, lse_low = split_low(lse_value - lse_high)
        lane = lanes_of((own, LANES))
        tail = grad_seen[:, main:]
        for k, column in ((5, dots_high), (6, lse_high), (7, lse_mid), (8, lse_low), (9, dots_low)):
            tail = jnp.where(lane == k, column, tail)
        gx_all[g, place.y, place.z] = tail.T[:16].astype(bf16)
        grad_seen = grad_seen[:, :main].astype(bf16)
        for n, i in enumerate(range(g * pair, (g + 1) * pair)):
            g_all[i, place.y, place.z] = grad_seen[n * rows : (n + 1) * rows]
        g_ext[g].begin()
        for i in range(g * pair, (g + 1) * pair):
            g_main[i].begin()

    def small_in(g):
        g_ext[g].end()
        for y in range(2):
            for z in range(depth):
                block = gx_all[g, y, z].astype(f32)
                block = jnp.concatenate([block, jnp.zeros((LANES - 16, LANES), f32)], axis=0).T
                for n in range(pair):
                    g_small[g * pair + n, y, z] = block[n * rows : (n + 1) * rows].astype(bf16)

    stores, totals = [], {}
    owned = micro * rows
    up_store = pltpu.make_async_copy(up_out, updated, store_sem.at[0])

    def summed(k, value):
        sources[k][...] = value.astype(bf16)
        kind, lanes, orders = chunks[k]
        totals[k] = Total(
            links, place, orders, sources[k], recvs[k], (sum_back, sum_hidden, sum_value, sum_late)[kind], kept_sem.at[k], lanes
        )
        totals[k].send(0)

    def term(k):
        kind, lanes, _ = chunks[k]
        if kind == 0:
            right = cot_in[:, :, lanes].reshape(owned, lanes.stop - lanes.start).astype(bf16)
            summed(k, dot(act[...], right, 0, 0))
        elif kind == 1:
            summed(k, dot(nm[...], gpre[:, lanes], 0, 0))
        else:
            summed(k, dot(gh_low[...], seen[:, lanes].astype(bf16), 0, 0))

    def grad_block(i):
        small = g_small[i].reshape(everyone, LANES).astype(f32)
        lane = lanes_of((everyone, LANES))
        whole = small[:, 6:7] + small[:, 7:8] + small[:, 8:9]
        own_top = jnp.broadcast_to(tops[i][0:1], (LANES, everyone)).T
        scale = jnp.exp(own_top[:, 0:1] - whole)
        dots_high, dots_low = split_low((small[:, 5:6] + small[:, 9:10]) * scale)
        tail = jnp.where(lane < 5, small * scale, 0.0)
        tail = jnp.where(lane == 5, dots_high, tail)
        tail = jnp.where(lane == 7, dots_low, tail)
        value = g_all[i].reshape(everyone, main).astype(f32) * scale
        return jnp.concatenate([value.astype(bf16), tail.astype(bf16)], axis=1)

    def attend_back(i):
        g_main[i].end()
        block = grad_block(i)
        scores[...] = dot(np_all[i], block, 1, 1)
        grad_s[...] = (probs[i].astype(f32) * scores[...]).astype(bf16)
        sums = dot(npt_all[i], grad_s[...], 1, 0)
        for y in range(2):
            here = slice(y * line, (y + 1) * line)
            bb[i, y] = sums[:main, here].astype(bf16)
            be[i, y] = sums[main : main + 8, here]
        begin(b_parts[i][0])
        block_t = block.astype(f32).T[:tall].astype(bf16)
        query_t = query_block(i).astype(f32).T[:tall].astype(bf16)
        grad_np = dot(block_t, probs[i], 1, 1) + dot(query_t, grad_s[...], 1, 1)
        grad_np = jnp.where(rows_of((tall, px_rows)) < feat, grad_np, 0.0)
        spread = px_stats[i, 1:2]
        unit = pixel_unit(i, px_stats[i, 0:1]) * spread
        terms = grad_np * unit
        gp_acc[...] += sum(terms[:, k : k + LANES] for k in range(0, px_rows, LANES))
        grad_np = grad_np * gain_column
        first = jnp.sum(grad_np, axis=0, keepdims=True) * (1.0 / feat)
        second = jnp.sum(grad_np * unit, axis=0, keepdims=True) * (1.0 / feat)
        px_t[i] = (spread * (grad_np - first - unit * second)).astype(bf16)
        stores.append(pltpu.make_async_copy(px_t.at[i], grad_pixels.at[i], store_sem.at[1 + i]))
        stores[-1].start()

    def join_back(i):
        _, owners, waits = b_parts[i]
        links.wait(*waits[0])
        links.wait(*waits[1])
        total = bb[i, place.y].astype(f32) + brecv[i].astype(f32)
        yb[i] = total.T.astype(bf16).reshape(depth, rows, main)
        y_small[8 * i : 8 * i + 8] = be[i, place.y] + berecv[i]
        begin(owners)

    def layer_out(k):
        up_out[...] = up_out[...] + dot(act[...], wb[...], 1, 0).reshape(micro, rows, width)
        up_store.start()

    def queries_back(k):
        ys[...] = y_small[...].astype(bf16)
        begin(y_copies)
        for i in range(micro):
            links.wait(*b_parts[i][2][2])
        links.wait(*y_came)
        lane = lanes_of((rows, LANES))
        smalls = own_lanes(y_small[...] + sum(ysrecv[k].astype(f32) for k in range(depth - 1)))
        parts = []
        for i in range(micro):
            value = yb[i, place.z].astype(f32) + sum(yrecv[i, k].astype(f32) for k in range(depth - 1))
            small = smalls if i == 0 else pltpu.roll(smalls, LANES - 8 * i, 1)
            small = jnp.where(lane < feat - main, small, 0.0)
            parts.append(jnp.concatenate([value.astype(bf16), small.astype(bf16)], axis=1))
        back_low[...] = jnp.concatenate(parts, axis=0)
        for j, (kind, lanes, _) in enumerate(chunks):
            if kind == 3:
                summed(j, dot(nq[...], back_low[:, lanes], 0, 0))

    def queries_in(k):
        back_feats = back_low[...]
        grad_q = (dot(back_feats, wk[...], 1, 0) * scaling).astype(bf16)
        grad_nq = dot(grad_q, wq[...], 1, 1)
        unit_q, spread_q = normed(x_in[...].reshape(owned, width).astype(f32))
        value_tail = pltpu.roll(seen[:, main:], 5, 1).astype(bf16)
        row = rows_of((16, width))
        terms = dot(back_feats[:, main:], nq[...], 0, 0)[:16] + dot(value_tail, gh_low[...], 0, 0)[:16]
        terms = jnp.where(row == 10, sum(grad_gm), terms)
        terms = jnp.where(row == 11, jnp.sum(grad_nq * unit_q, axis=0, keepdims=True), terms)
        grad_gp = jnp.concatenate([gp_acc[...], jnp.zeros((wide - tall, LANES), f32)], axis=0).T
        grad_gp = jnp.sum(grad_gp, axis=0, keepdims=True)
        grad_gp = jnp.concatenate([grad_gp, jnp.zeros((1, width - wide), f32)], axis=1)
        small_sum.begin(jnp.where(row == 12, grad_gp, terms))
        up_store.wait()
        up_out[...] = (grad_h[...] + normed_back(grad_nq * gain_query[...], unit_q, spread_q)).reshape(micro, rows, width)
        last = pltpu.make_async_copy(up_out, grad_latents, store_sem.at[1 + micro])
        last.start()
        stores.append(last)


    small_sum = Everywhere(
        links, place, small_src, small_recv, small_slots, links.group(wq.at[pl.ds(0, (3 + depth - 1) * 16)])
    )

    def small_end(k):
        small_out[...] = small_sum.end()
        stores.append(pltpu.make_async_copy(small_out, sum_small, store_sem.at[2 + micro]))
        stores[-1].start()

    steps = {
        "P": lambda k: pixel_rows(), "p": pixel_norm, "X": lambda k: q_ext.forward(), "q": lambda k: q_main[k].forward(),
        "E": lambda k: q_ext.end(), "A": attend_out, "M": join, "Z": small_out_of, "O": owner_starts, "N": lambda k: next(owners[k], None), "B": term, "U": layer_out,
        "x": lambda k: g_ext[k].forward(), "g": lambda k: g_main[k].forward(), "e": small_in, "a": attend_back, "m": join_back,
        "Q": queries_back, "L": queries_in, "s": lambda k: small_sum.stage(k), "S": small_end,
    }
    for step in ORDER:
        if step[0] == "r":
            totals[int(step[2:])].rs(int(step[1]))
        elif step[0] == "b":
            totals[int(step[2:])].back(int(step[1]))
        else:
            steps[step[0]](int(step[1:]))
    for store in stores:
        store.wait()
    links.drain()


def fused(mesh, pixels, counts, latents, cotangent, w_query, w_key, w_value, w_out, w_hidden, w_back, gain_query, gain_pixel, gain_mlp):
    micro, px_rows, feat = pixels.shape
    rows, width = latents.shape[1:]
    depth = mesh.shape["blk"] // 2
    main = feat // LANES * LANES
    wide = main + LANES
    line = depth * rows
    dims = (micro, rows, depth, px_rows, feat, main, wide, width)
    tall = main + 16
    any_spec = pl.BlockSpec(memory_space=pl.ANY)
    vmem = pl.BlockSpec(memory_space=pltpu.VMEM)
    V = pltpu.VMEM
    chunks = chunks_of(width, main)

    def total_recvs(lanes, orders):
        held, height = [], width
        for axis in "c" + orders[0]:
            height //= depth if axis == "z" else 2
            held.append(V((depth - 1 if axis == "z" else 1, height, lanes.stop - lanes.start), bf16))
        return held

    reduce_buffers = [
        V((micro, 2, main, line), bf16), V((micro, 2, 8, line), f32), V((micro, main, line), bf16), V((micro, 8, line), f32),
        V((micro, depth, rows, main), bf16), V((micro, depth - 1, rows, main), bf16),
    ]
    arrivals = 2 * (2 * micro + 3) + 3 * 2 * micro + 3 + 8 * len(chunks) + 4
    groups = 4 + 6 + 2 + 2 * len(chunks) + 1
    scratch = (
        [
            V((feat, micro, px_rows), bf16), V((micro, tall, px_rows), bf16), V((micro, 8, px_rows), f32),
            V((micro, px_rows, wide), bf16), V((micro, tall, px_rows), bf16),
            V((px_rows, 2 * line), f32), V((micro, px_rows, 2 * line), bf16), V((px_rows, 2 * line), bf16),
            V(latents.shape, bf16), V(cotangent.shape, f32),
        ]
        + [V((width, width), bf16)] * 4
        + [V((feat, width), bf16)] * 2
        + [V((wide, width), bf16)] * 2
        + [V((micro, 2, depth, rows, main), bf16), V((2, depth, rows, LANES), bf16)]
        + [V((micro, 2, depth, rows, main), bf16), V((2, 2, depth, 16, LANES), bf16)]
        + reduce_buffers * 2
        + [
            V((2, 4 * micro, line), f32), V((2, depth - 1, 4 * micro, line), f32),
            V((8 * micro, line), f32), V((8 * micro, line), bf16), V((depth - 1, 8 * micro, line), bf16),
            V((micro, 8, 2 * line), f32), V((micro * rows, wide), f32), V((micro * rows, LANES), f32),
            V((micro, 2, depth, rows, LANES), bf16), V((micro * rows, wide), bf16),
        ]
        + [V((micro * rows, width), bf16)] * 4
        + [V((micro * rows, width), f32), V((micro * rows, width), bf16), V(latents.shape, f32)]
        + [
            V((3, 16, width), bf16), V((3, 16, width), bf16), V((depth, 16, width), bf16), V((16, width), f32), V((tall, LANES), f32),
        ]
        + [
            [V((width, lanes.stop - lanes.start), bf16) for _, lanes, _ in chunks],
            [total_recvs(lanes, orders) for _, lanes, orders in chunks],
            pltpu.SemaphoreType.DMA((groups,)), pltpu.SemaphoreType.DMA((arrivals,)),
            pltpu.SemaphoreType.DMA((9,)), pltpu.SemaphoreType.DMA((3 + micro,)), pltpu.SemaphoreType.DMA((len(chunks),)),
        ]
    )
    S = jax.ShapeDtypeStruct
    return pl.pallas_call(
        functools.partial(kernel, dims),
        out_shape=[
            S(latents.shape, f32), S(latents.shape, f32), S((micro, tall, px_rows), bf16),
            S((width, width), bf16), S((width, width), bf16), S((width, main), bf16), S((width, main), bf16), S((16, width), f32),
        ],
        in_specs=[pl.BlockSpec(memory_space=pltpu.SMEM)] + [any_spec] * 9 + [vmem] * 3,
        out_specs=[any_spec] * 8,
        scratch_shapes=scratch,
        compiler_params=pltpu.CompilerParams(collective_id=0, has_side_effects=True, vmem_limit_bytes=63 * 2**20),
        name="layer",
    )(
        counts, jnp.transpose(pixels, (2, 0, 1)), latents, cotangent, w_query, w_out, w_hidden, w_back, w_key, w_value,
        gain_query.reshape(1, -1), gain_pixel, gain_mlp.reshape(1, -1),
    )


def finish(
    dims,
    late, value, small, w_key, w_value, w_query, w_out, hidden, back, px, up, lat,
    out_query, out_key, out_value, out_out, out_hidden, out_back, out_px, out_up, out_lat, out_gq, out_gp, out_gm,
    key_rows, value_rows, late_t, value_t, late_rows,
):
    feat, main, wide, width = dims
    scaling = 1.0 / math.sqrt(width)
    step = out_query.shape[0]
    here = pl.ds(pl.multiple_of(pl.program_id(0) * step, step), step)

    @pl.when(pl.program_id(0) == 0)
    def prepare():
        for raw, dst in ((w_key, key_rows), (w_value, value_rows)):
            dst[:main] = raw[:main]
            last = raw[main:].astype(f32)
            dst[main:] = jnp.concatenate([last, jnp.zeros((wide - feat, width), f32)], axis=0).astype(bf16)
        row = rows_of((16, width))
        rest = jnp.zeros((LANES - 16, width), f32)
        tail = jnp.concatenate([jnp.where(row < 5, small[...], 0.0), rest], axis=0)
        late_rows[:, :main] = late[...]
        late_rows[:, main:] = tail.T.astype(bf16)
        late_t[:main] = late[...].astype(f32).T.astype(bf16)
        late_t[main:] = tail.astype(bf16)
        tail = jnp.concatenate([jnp.where(row < 5, pltpu.roll(small[...], 11, 0), 0.0), rest], axis=0)
        value_t[:main] = value[...].astype(f32).T.astype(bf16)
        value_t[main:] = tail.astype(bf16)
        out_gm[...] = small[10]
        out_gq[...] = small[11]
        out_gp[...] = small[12, :feat]

    out_query[...] = dot(late_rows[here, :], key_rows[...], 1, 0) * scaling
    out_out[...] = dot(value_rows[:, here], value_t[...], 0, 0)
    out_key[...] = (dot(late_t[...], w_query[...], 1, 0) * scaling)[:feat]
    out_value[...] = dot(value_t[...], w_out[...], 1, 1)[:feat]
    out_hidden[...] = hidden[...].astype(f32)
    out_back[...] = back[...].astype(f32)
    out_px[...] = jnp.swapaxes(px[...].astype(f32), 0, 1)
    out_up[...] = up[...]
    out_lat[...] = lat[...]


def finished(pixels, latents, w_key, w_value, w_query, w_out, up, lat, px, back, hidden, value, late, small):
    micro, px_rows, feat = pixels.shape
    rows, width = latents.shape[1:]
    main = feat // LANES * LANES
    wide = main + LANES
    steps = 2
    step, px_step = width // steps, -(-feat // (16 * steps)) * 16
    px_last = -(-feat // px_step) - 1
    whole = lambda *shape: pl.BlockSpec(shape, lambda k: (0,) * len(shape))
    by_row = pl.BlockSpec((step, width), lambda k: (k, 0))
    by_column = lambda height: pl.BlockSpec((height, step), lambda k: (0, k))
    lat_block = pl.BlockSpec((micro, rows // steps, width), lambda k: (0, k, 0))
    S = jax.ShapeDtypeStruct
    out = pl.pallas_call(
        functools.partial(finish, (feat, main, wide, width)),
        grid=(steps,),
        in_specs=[
            whole(width, main), whole(width, main), whole(16, width), whole(feat, width), whole(feat, width), by_column(width), by_row,
            by_row, by_row, pl.BlockSpec((micro, px_step, px_rows), lambda k: (0, jnp.minimum(k, px_last), 0)), lat_block, lat_block,
        ],
        out_specs=[
            by_row, by_column(feat), by_column(feat), by_row, by_row, by_row,
            pl.BlockSpec((px_step, micro, px_rows), lambda k: (jnp.minimum(k, px_last), 0, 0)), lat_block, lat_block,
            whole(width), whole(feat), whole(width),
        ],
        out_shape=[
            S((width, width), f32), S((feat, width), f32), S((feat, width), f32), S((width, width), f32),
            S((width, width), f32), S((width, width), f32), S((feat, micro, px_rows), f32),
            S(latents.shape, f32), S(latents.shape, f32), S((width,), f32), S((feat,), f32), S((width,), f32),
        ],
        scratch_shapes=[pltpu.VMEM((wide, width), bf16)] * 4 + [pltpu.VMEM((width, wide), bf16)],
        compiler_params=pltpu.CompilerParams(vmem_limit_bytes=60 * 2**20),
        name="finish",
    )(late, value, small, w_key, w_value, w_query, w_out, hidden, back, px, up, lat)
    g_query, g_key, g_value, g_out, g_hidden, g_back, g_px, g_up, g_lat, g_gq, g_gp, g_gm = out
    g_px = jnp.transpose(g_px, (1, 2, 0))
    return g_up, g_lat, g_px, g_query, g_key, g_value, g_out, g_hidden, g_back, g_gq, g_gp, g_gm


def fused_body(mesh, *args):
    w_query, w_key, w_value, w_out = args[4:8]
    return finished(args[0], args[2], w_key, w_value, w_query, w_out, *fused(mesh, *args))


def layer_norm(values, gain_vec):
    centered = values - jnp.mean(values, axis=-1, keepdims=True)
    variance = jnp.mean(centered * centered, axis=-1, keepdims=True)
    return centered * lax.rsqrt(variance + EPSILON) * gain_vec


def gelu_exact(values):
    return jax.nn.gelu(values, approximate=False)


def low(values):
    return values.astype(jnp.bfloat16)


def product(left_mat, right_mat):
    return jnp.dot(left_mat, right_mat, preferred_element_type=jnp.float32)


def product_tn(left_mat, right_mat):
    return lax.dot_general(
        left_mat, right_mat, (((0,), (0,)), ((), ())), preferred_element_type=jnp.float32
    )


def product_nt(left_mat, right_mat):
    return lax.dot_general(
        left_mat, right_mat, (((1,), (1,)), ((), ())), preferred_element_type=jnp.float32
    )


def each(spec, left, right):
    return jnp.einsum(spec, left, right, preferred_element_type=jnp.float32)


def to_owner(x, peers):
    micro, rows = x.shape[:2]
    blocks = jnp.moveaxis(x.reshape(micro, peers, rows // peers, *x.shape[2:]), 1, 0)
    return lax.all_to_all(blocks, "blk", 0, 0, tiled=True)


def plain_body(pixels, counts, latents, cotangent, w_query, w_key, w_value, w_out, w_hidden, w_back, gain_query, gain_pixel, gain_mlp):
    micro, pixel_rows, features = pixels.shape
    lat_rows, width = latents.shape[1:]
    peers = lax.axis_size("blk")
    scaling = 1.0 / math.sqrt(width)
    rows = micro * lat_rows
    positions = lax.axis_index("blk") * pixel_rows + jnp.arange(pixel_rows, dtype=jnp.int32)
    valid = positions[None, :] < counts[:, None]

    latent_in = latents.reshape(rows, width).astype(jnp.float32)
    normed_qf, query_pull = jax.vjp(layer_norm, latent_in, gain_query)
    normed_q = low(normed_qf)
    queries = low(product(normed_q, w_query))
    query_feats = low(product_nt(queries, w_key) * scaling).reshape(micro, lat_rows, features)
    all_query = lax.all_gather(query_feats, "blk", axis=1, tiled=True)
    normed_pf, pixel_pull = jax.vjp(layer_norm, pixels.astype(jnp.float32), gain_pixel)
    normed_p = low(normed_pf)
    scores = each("mqf,mpf->mqp", all_query, normed_p)
    scores = jnp.where(valid[:, None, :], scores, MASKED)
    highest = jnp.max(scores, axis=2)
    unscaled = jnp.exp(scores - highest[..., None])
    total = jnp.sum(unscaled, axis=2)
    sums = low(each("mqp,mpf->mqf", low(unscaled), normed_p))
    parts = to_owner(sums, peers).astype(jnp.float32)
    stats = to_owner(jnp.stack([highest, total], axis=2), peers)
    top = jnp.max(stats[..., 0], axis=0)
    scale = jnp.exp(stats[..., 0] - top)
    denom = jnp.sum(stats[..., 1] * scale, axis=0)
    lse = top + jnp.log(denom)
    seen = (jnp.sum(parts * scale[..., None], axis=0) / denom[..., None]).reshape(rows, features)
    seen_b = low(seen)
    attended_b = low(product(seen_b, w_value))
    hidden_in = latent_in + product(attended_b, w_out)
    normed_mf, mlp_pull = jax.vjp(layer_norm, hidden_in, gain_mlp)
    normed_m = low(normed_mf)
    pre_act = product(normed_m, w_hidden)
    activated_f, gelu_pull = jax.vjp(gelu_exact, pre_act)
    activated = low(activated_f)
    updated = hidden_in + product(activated, w_back)
    cot = cotangent.reshape(rows, width)
    cot_b = low(cot)
    grad_back = product_tn(activated, cot_b)
    (grad_pre,) = gelu_pull(product_nt(cot_b, w_back))
    grad_pre_b = low(grad_pre)
    grad_hidden = product_tn(normed_m, grad_pre_b)
    grad_h_ln, grad_gm = mlp_pull(product_nt(grad_pre_b, w_hidden))
    grad_h = cot + grad_h_ln
    grad_h_b = low(grad_h)
    grad_att = low(product_nt(grad_h_b, w_out))
    grad_seen = product_nt(grad_att, w_value)
    dots = jnp.sum(grad_seen * seen, axis=1).reshape(micro, lat_rows)
    value_side = product_tn(seen_b, grad_h_b)
    all_grad = lax.all_gather(low(grad_seen).reshape(micro, lat_rows, features), "blk", axis=1, tiled=True)
    all_stat = lax.all_gather(jnp.stack([lse, dots], axis=2), "blk", axis=1, tiled=True)
    probs = unscaled * jnp.exp(highest - all_stat[..., 0])[..., None]
    grad_probs = each("mqf,mpf->mqp", all_grad, normed_p)
    grad_scores = low(probs * (grad_probs - all_stat[..., 1][..., None]))
    back_sums = low(each("mqp,mpf->mqf", grad_scores, normed_p))
    grad_np = each("mqp,mqf->mpf", low(probs), all_grad) + each("mqp,mqf->mpf", grad_scores, all_query)
    grad_pixels, grad_gp = pixel_pull(grad_np)
    back_feats = jnp.sum(to_owner(back_sums, peers).astype(jnp.float32), axis=0).reshape(rows, features)
    back_b = low(back_feats)
    grad_q = low(product(back_b, w_key) * scaling)
    grad_lat_q, grad_gq = query_pull(product_nt(grad_q, w_query))
    grad_latents = grad_h + grad_lat_q
    query_side = product_tn(normed_q, back_b)
    query_side, value_side, grad_hidden, grad_back, grad_gq, grad_gp, grad_gm = lax.psum(
        (query_side, value_side, grad_hidden, grad_back, grad_gq, grad_gp, grad_gm), ("img", "blk")
    )
    query_b, value_b = low(query_side * scaling), low(value_side)
    return (
        updated.reshape(micro, lat_rows, width),
        grad_latents.reshape(micro, lat_rows, width),
        grad_pixels,
        product(query_b, w_key),
        product_tn(query_b, w_query),
        product_nt(value_b, w_out),
        product_tn(w_value, value_b),
        grad_hidden,
        grad_back,
        grad_gq,
        grad_gp,
        grad_gm,
    )


def body(mesh, *args):
    pixels, latents = args[0], args[2]
    rows, width = latents.shape[1:]
    fits = pixels.shape[0] // 2 * rows == LANES and rows % 16 == 0 and width % (16 * mesh.size) == 0
    fits = fits and mesh.shape["img"] == 4 and mesh.shape["blk"] % 2 == 0
    return fused_body(mesh, *args) if fits else plain_body(*args)


def solution(mesh):
    spread, same = P("img", "blk", None), P()
    return jax.shard_map(
        functools.partial(body, mesh),
        mesh=mesh,
        in_specs=(spread, P("img"), spread, spread) + (same,) * 9,
        out_specs=(spread,) * 3 + (same,) * 9,
        check_vma=False,
    )
```
